128 devices in a mesh: dp: 8 (over y, core), expert: 16 (over z, x).
Axes of the slice: x: 4, y: 4, z: 4, core: 2. Of those that a mesh axis runs over, the one named last changes fastest.
Arguments:
- inputs: bfloat16 [8, 2048, 1024], P('dp', 'expert'), may hold values from -6 to 6
- segments: int32 [8, 2048], P('dp'), may hold values from 0 to 3, as said below
- routes: int32 [8, 2048, 8], P('dp', 'expert'), may hold values from 0 to 31, all different within a row; in each aligned block of 128 rows (0 to 127, 128 to 255, ..., all dimensions but the last counted through in order) at most 40 rows name the same one
- gain_attn: bfloat16 [1024], P('dp'), may hold values from 0.5 to 1.5
- w_query: bfloat16 [1024, 1024], P('dp'), may hold values from -0.25 to 0.25
- w_key: bfloat16 [1024, 512], P('dp'), may hold values from -0.25 to 0.25
- w_value: bfloat16 [1024, 512], P('dp'), may hold values from -0.1875 to 0.1875
- w_out: bfloat16 [1024, 1024], P('dp'), may hold values from -1.5 to 1.5
- gain_ffn: bfloat16 [1024], P('dp'), may hold values from 0.5 to 1.5
- w_router: bfloat16 [1024, 32], P('dp'), may hold values from -0.09375 to 0.09375
- expert_gate: bfloat16 [32, 1024, 512], P('expert', 'dp'), may hold values from -0.1875 to 0.1875
- expert_up: bfloat16 [32, 1024, 512], P('expert', 'dp'), may hold values from -0.1875 to 0.1875
- expert_down: bfloat16 [32, 512, 1024], P('expert', 'dp'), may hold values from -4 to 4
- cotangent: bfloat16 [8, 2048, 1024], P('dp', 'expert'), may hold values from -6 to 6
Outputs:
- output: bfloat16 [8, 2048, 1024], P('dp', 'expert')
- grad_input: float32 [8, 2048, 1024], P('dp', 'expert')
- grad_gain_attn: float32 [1024], P('dp')
- grad_w_query: float32 [1024, 1024], P('dp')
- grad_w_key: float32 [1024, 512], P('dp')
- grad_w_value: float32 [1024, 512], P('dp')
- grad_w_out: float32 [1024, 1024], P('dp')
- grad_gain_ffn: float32 [1024], P('dp')
- grad_w_router: float32 [1024, 32], P('dp')
- grad_expert_gate: float32 [32, 1024, 512], P('expert', 'dp')
- grad_expert_up: float32 [32, 1024, 512], P('expert', 'dp')
- grad_expert_down: float32 [32, 512, 1024], P('expert', 'dp')
The draws below stay inside these ranges and needn't reach their ends.
Inputs may be any that keep to these rules, and one draw needn't show every extreme that they name: Each row of routes names 8 different experts; among the rows of one device no expert is named by more than 40 rows, and some expert reaches 40. `segments`: segment numbers start at 0 in every packed row, never fall, and rise by one at each new document; in every row one document begins among the first 128 positions and ends among the last 128.
All inputs are finite; a program needn't handle non-finite values.
Results may differ from the reference program's by a relative error of at most 0.025.
Values may be sent and summed in bfloat16 or wider, within the bound.
No kernel may reach another device: no remote copies, remote signals or barrier semaphores. Data moves between devices by JAX's collectives and lax.ppermute only.
A program may use at most 128 MiB of HBM per device.

```python
import math
import jax
import jax.numpy as jnp
import numpy as np
from jax import lax

D = 1024
HEADS = 16
KV_HEADS = 8
HD = 64
EF = 512
TOPK = 8
TOK_DEV = 128
EXPERTS = 32
ATT = 1024
KVW = 512
SEQ = 2048
BATCH = 8
CAP = 40


def draw_segments(key, part):
    key = jax.random.fold_in(key, 11)
    first_key, second_key, tail_key, count_key, pick_key = jax.random.split(key, 5)
    first = jax.random.randint(first_key, (BATCH, 1), 1, TOK_DEV // 2 + 1)
    second = first + jax.random.randint(second_key, (BATCH, 1), 1, TOK_DEV // 2)
    tail = SEQ - jax.random.randint(tail_key, (BATCH, 1), 1, TOK_DEV)
    extra = jax.random.randint(count_key, (BATCH, 1), 0, 2)
    chosen = jax.random.randint(pick_key, (), 0, BATCH)
    extra = jnp.maximum(extra, (jnp.arange(BATCH)[:, None] == chosen).astype(jnp.int32))
    index = jnp.arange(SEQ)[None, :]
    return ((index >= first).astype(jnp.int32) + (index >= second).astype(jnp.int32) * extra + (index >= tail).astype(jnp.int32)).astype(jnp.int32)


def shard_levels(stream_key, extent, cuts, least, top_value):
    def one(axis_at, blocks):
        steps = jax.random.uniform(jax.random.fold_in(jax.random.fold_in(stream_key, 6), axis_at), (blocks,), jnp.float32, least / len(cuts), top_value / len(cuts))
        return jnp.repeat(jnp.exp(steps), extent[axis_at] // blocks).reshape((-1,) + (1,) * (len(extent) - axis_at - 1))

    level = one(*cuts[0])
    for cut in cuts[1:]:
        level = level * one(*cut)
    return level


def shared_out(own_key, own, number, rows, number_of, top, reach, skew):
    order = jax.random.permutation(own_key, number_of)
    crowded, common = shares(number_of, rows * top, reach, skew, True), shares(number_of, rows * top, reach, skew, False)
    places = jnp.arange(number_of)

    def named(lengths, offset_by):
        used = int((lengths > 0).sum())
        fixed = max(1, used // 4)
        passed = fixed + (places - fixed + offset_by * (used - fixed)) % max(1, number_of - fixed)
        return jnp.zeros((number_of,), jnp.int32).at[order[jnp.where(places < fixed, places, passed)]].set(jnp.asarray(lengths, jnp.int32))

    lengths = jnp.where(number % 4 == 0, named(crowded, number // 4), named(common, number - number // 4 - 1))
    mixed = jax.random.permutation(jax.random.fold_in(own, 3), number_of)
    source_of, taker = mixed[0:number_of // 2 * 2:2], mixed[1:number_of // 2 * 2:2]
    room = jnp.minimum(lengths[source_of] - 1, reach - lengths[taker]) // 2
    room = jnp.where((source_of == order[0]) | (taker == order[0]) | (lengths[taker] == 0), 0, jnp.maximum(room, 0))
    passed = jax.random.randint(jax.random.fold_in(own, 4), (number_of // 2,), 0, 1 << 20) % (room + 1)
    lengths = lengths.at[source_of].add(-passed).at[taker].add(passed)
    items = jnp.searchsorted(jnp.cumsum(lengths), jnp.arange(rows * top), side="right").astype(jnp.int32)
    table = items.reshape(top, rows).T
    table = table[jax.random.permutation(jax.random.fold_in(own, 1), rows)]
    offset_by = jax.random.randint(jax.random.fold_in(own, 2), (rows, 1), 0, top)
    return jnp.take_along_axis(table, (jnp.arange(top)[None, :] + offset_by) % top, axis=1)


def shares(number_of, total, bound, skew, full):
    portions = [(1 << 20) // math.isqrt(rank ** skew) + 1 for rank in range(1, number_of + 1)]
    largest = bound if full else min(bound, max(-(-total // number_of), total * portions[0] // sum(portions)))
    least = 1 if total - largest >= number_of - 1 else 0
    holding, rest = [largest] + [least] * (number_of - 1), total - largest - least * (number_of - 1)
    while rest > 0:
        candidates = [i for i in range(1, number_of) if holding[i] < largest] or [i for i in range(1, number_of) if holding[i] < bound]
        whole, remaining = sum([portions[i] for i in candidates]), rest
        for i in candidates:
            addition = min(bound - holding[i], max(1, remaining * portions[i] // whole), rest)
            holding[i] = holding[i] + addition
            rest = rest - addition
    return np.array(holding)


def noise(rng, dims, width, reach, cuts=(), held_as=jnp.bfloat16):
    level = shard_levels(rng, dims, cuts, -0.22, 0.18) if cuts else 1.0
    values = jax.random.normal(rng, dims, jnp.float32) * width * level
    return jnp.minimum(jnp.maximum(values, -reach), reach).astype(held_as)


def setup_inputs(seed: int = 0) -> dict:
    arg_keys = jax.random.split(jax.random.key(seed), 15)
    inputs = noise(arg_keys[0], (BATCH, SEQ, D), 1.0, 6.0, ((0, 8), (1, 16)))
    segments = draw_segments(jax.random.fold_in(arg_keys[14], 71), 0)
    routes_keys = jax.random.split(jax.random.fold_in(arg_keys[2], 1), BATCH * SEQ // TOK_DEV)
    routes_turns = jax.random.permutation(jax.random.fold_in(arg_keys[2], 3), BATCH * SEQ // TOK_DEV)
    routes = jax.vmap(lambda own, number: shared_out(jax.random.fold_in(arg_keys[2], 2), own, number, TOK_DEV, EXPERTS, TOPK, CAP, 1))(routes_keys, routes_turns).reshape((BATCH, SEQ, TOPK))
    gain_attn = jnp.clip(1.0 + 0.1 * jax.random.normal(arg_keys[3], (D,), jnp.float32), 0.5, 1.5).astype(jnp.bfloat16)
    w_query = noise(arg_keys[4], (D, ATT), (D // 2) ** -0.5, 0.25, ((0, 8),))
    w_key = noise(arg_keys[5], (D, KVW), (D // 2) ** -0.5, 0.25, ((0, 8),))
    w_value = noise(arg_keys[6], (D, KVW), D ** -0.5, 0.1875, ((0, 8),))
    w_out = noise(arg_keys[7], (ATT, D), (ATT // 64) ** -0.5, 1.5, ((0, 8),))
    gain_ffn = jnp.clip(1.0 + 0.1 * jax.random.normal(arg_keys[8], (D,), jnp.float32), 0.5, 1.5).astype(jnp.bfloat16)
    w_router = noise(arg_keys[9], (D, EXPERTS), (4 * D) ** -0.5, 0.09375, ((0, 8),))
    expert_gate = noise(arg_keys[10], (EXPERTS, D, EF), D ** -0.5, 0.1875, ((0, 16), (1, 8)))
    expert_up = noise(arg_keys[11], (EXPERTS, D, EF), D ** -0.5, 0.1875, ((0, 16), (1, 8)))
    expert_down = noise(arg_keys[12], (EXPERTS, EF, D), (max(EF * 4 // (EXPERTS * EXPERTS), 1)) ** -0.5, 4.0, ((0, 16), (1, 8)))
    cotangent = noise(arg_keys[13], (BATCH, SEQ, D), 1.0, 6.0, ((0, 8), (1, 16)))
    return dict(inputs=inputs, segments=segments, routes=routes, gain_attn=gain_attn, w_query=w_query, w_key=w_key, w_value=w_value, w_out=w_out, gain_ffn=gain_ffn, w_router=w_router, expert_gate=expert_gate, expert_up=expert_up, expert_down=expert_down, cotangent=cotangent)


@jax.custom_vjp
def low(v):
    return lax.optimization_barrier(v.astype(jnp.bfloat16)).astype(jnp.float32)

@jax.custom_vjp
def low_back(v):
    return v

def low_keep(v):
    return (low(v), None)

def low_pass(kept, grad):
    return (grad,)

def back_keep(v):
    return (v, None)

def back_low(kept, grad):
    return (low(grad),)
low.defvjp(low_keep, low_pass)
low_back.defvjp(back_keep, back_low)
eps = 1e-06
theta = 10000.0
highest = lax.Precision.HIGHEST

def product(left, right):
    return jnp.dot(left, right, precision=highest, preferred_element_type=jnp.float32)

def rms_norm(values, gain):
    return values * lax.rsqrt(lax.optimization_barrier(jnp.mean(values * values, axis=-1, keepdims=True)) + eps) * gain

def doc_positions(segment_row):
    index = jnp.arange(segment_row.shape[0], dtype=jnp.int32)
    fresh = jnp.concatenate([jnp.ones((1,), dtype=jnp.bool_), segment_row[1:] != segment_row[:-1]])
    return index - lax.cummax(jnp.where(fresh, index, 0), axis=0)

def rope_tables(positions):
    freqs = theta ** (-jnp.arange(0, HD, 2, dtype=jnp.float32) / HD)
    angles = positions.astype(jnp.float32)[:, None] * freqs[None, :]
    angles = jnp.concatenate([angles, angles], axis=-1)
    return (jnp.cos(angles), jnp.sin(angles))

def rotate(values, cosine, sine):
    half = HD // 2
    turned = jnp.concatenate([-values[..., half:], values[..., :half]], axis=-1)
    return values * cosine[:, None, :] + turned * sine[:, None, :]

def attend(query_rot, key_rot, values, segment_row):
    length = query_rot.shape[0]
    block = min(512, length)
    group = HEADS // KV_HEADS
    grouped = query_rot.reshape(length, KV_HEADS, group, HD)
    index = jnp.arange(length, dtype=jnp.int32)
    scale = HD ** (-0.5)

    @jax.checkpoint
    def one_block(start):
        query_rows = lax.dynamic_slice_in_dim(grouped, start, block, 0)
        row_segment = lax.dynamic_slice_in_dim(segment_row, start, block, 0)
        row_index = start + jnp.arange(block, dtype=jnp.int32)
        scores = low_back(jnp.einsum('qkgd,tkd->kgqt', query_rows, key_rot, precision=highest) * scale)
        allowed = (row_segment[:, None] == segment_row[None, :]) & (row_index[:, None] >= index[None, :])
        scores = jnp.where(allowed[None, None], scores, -1000000000.0)
        weights = low(jnp.exp(scores - jax.nn.logsumexp(scores, axis=-1, keepdims=True)))
        return jnp.einsum('kgqt,tkd->qkgd', weights, values, precision=highest)
    starts = jnp.arange(length // block, dtype=jnp.int32) * block
    return lax.map(one_block, starts).reshape(length, HEADS, HD)

def routing_places(route_row):
    blocks = route_row.shape[0] // TOK_DEV
    flat = route_row.reshape(blocks, TOK_DEV * TOPK)
    choose = (flat[..., None] == jnp.arange(EXPERTS, dtype=jnp.int32)).astype(jnp.int32)
    rank = jnp.cumsum(choose, axis=1) - choose
    slot = lax.optimization_barrier(jnp.sum(rank * choose, axis=-1))
    block_ids = jnp.arange(blocks, dtype=jnp.int32)[:, None]
    places = (flat * blocks + block_ids) * CAP + slot
    return places.reshape(-1).astype(jnp.int32)

def layer_row(inputs, params, segment_row, route_row):
    gain_attn, w_query, w_key, w_value, w_out, gain_ffn, w_router, expert_gate, expert_up, expert_down = params
    length = inputs.shape[0]
    cosine, sine = rope_tables(doc_positions(segment_row))
    normed = low(rms_norm(inputs, gain_attn))
    query = low_back(product(normed, w_query)).reshape(length, HEADS, HD)
    keys = low_back(product(normed, w_key)).reshape(length, KV_HEADS, HD)
    values = low(low_back(product(normed, w_value))).reshape(length, KV_HEADS, HD)
    mixed = attend(low(rotate(query, cosine, sine)), low(rotate(keys, cosine, sine)), values, segment_row)
    mixed = low(low_back(mixed.reshape(length, HEADS * HD)))
    hidden = inputs + low_back(product(mixed, w_out))
    ffn_in = low(rms_norm(hidden, gain_ffn))
    chances = jax.nn.softmax(low_back(product(ffn_in, w_router)), axis=-1)
    gates = jnp.take_along_axis(chances, route_row, axis=1)
    places = routing_places(route_row)
    blocks = length // TOK_DEV
    owners = jnp.full((EXPERTS * blocks * CAP,), length, dtype=jnp.int32)
    owners = owners.at[places].set(jnp.repeat(jnp.arange(length, dtype=jnp.int32), TOPK))
    padded = jnp.concatenate([ffn_in, jnp.zeros((1, D), ffn_in.dtype)], axis=0)
    buffers = low_back(jnp.take(padded, owners, axis=0)).reshape(EXPERTS, blocks * CAP, D)
    gate_pre = low_back(jnp.einsum('erd,edf->erf', buffers, expert_gate, precision=highest))
    up_pre = low_back(jnp.einsum('erd,edf->erf', buffers, expert_up, precision=highest))
    acted = low(jax.nn.silu(gate_pre) * up_pre)
    returned = low(low_back(jnp.einsum('erf,efd->erd', acted, expert_down, precision=highest)))
    picked = jnp.take(returned.reshape(-1, D), places, axis=0).reshape(length, TOPK, D)
    routed = lax.optimization_barrier(jnp.sum(gates[..., None] * picked, axis=1))
    return hidden + routed

def reference(inputs, segments, routes, gain_attn, w_query, w_key, w_value, w_out, gain_ffn, w_router, expert_gate, expert_up, expert_down, cotangent):
    params = tuple((weight.astype(jnp.float32) for weight in (gain_attn, w_query, w_key, w_value, w_out, gain_ffn, w_router, expert_gate, expert_up, expert_down)))

    def row_step(totals, row):
        row_inputs, row_segments, row_routes, row_cotangent = row

        def forward(values, weights):
            return layer_row(values, weights, row_segments, row_routes)
        result, pullback = jax.vjp(forward, row_inputs.astype(jnp.float32), params)
        grad_inputs, grad_params = pullback(row_cotangent.astype(jnp.float32))
        return (jax.tree.map(jnp.add, totals, grad_params), (result.astype(jnp.bfloat16), grad_inputs))
    zeros = jax.tree.map(jnp.zeros_like, params)
    totals, (outputs, grad_inputs) = lax.scan(row_step, zeros, (inputs, segments, routes, cotangent))
    return (outputs, grad_inputs, totals[0], totals[1], totals[2], totals[3], totals[4], totals[5], totals[6], totals[7], totals[8], totals[9])
```

```python
import jax
import jax.numpy as jnp
from jax import lax
from jax.experimental import pallas as pl
from jax.experimental.pallas import tpu as pltpu
from jax.sharding import PartitionSpec as P

D = 1024
HEADS = 16
HD = 64
EF = 512
EXPERTS = 32
CAP = 40
TOK = 128
SEQ = 2048
SIDE = 4
PEERS = 16
DP = 8
QB = 512
ROWS = PEERS * CAP
EXTRA = 16
PACK = 1152
WIDE = 3072

eps = 1e-06
theta = 10000.0
masked = -1000000000.0
bf16 = jnp.bfloat16
f32 = jnp.float32
MIB = 1 << 20

VM = pl.BlockSpec(memory_space=pltpu.VMEM)
SM = pl.BlockSpec(memory_space=pltpu.SMEM)
HB = pl.BlockSpec(memory_space=pl.ANY)
NN = (((1,), (0,)), ((), ()))
NT = (((1,), (1,)), ((), ()))
TN = (((0,), (0,)), ((), ()))


def mm(left, right, dims=NN):
    return lax.dot_general(left, right, dims, preferred_element_type=f32)


def shape(dims, dtype):
    return jax.ShapeDtypeStruct(dims, dtype)


def run(kernel, name, outs, ins, specs, scratch=(), limit=24, flops=0, moved=0):
    return pl.pallas_call(
        kernel,
        name=name,
        out_shape=outs,
        in_specs=specs,
        out_specs=jax.tree.map(lambda _: VM, outs),
        scratch_shapes=scratch,
        compiler_params=pltpu.CompilerParams(vmem_limit_bytes=limit * MIB),
        cost_estimate=pl.CostEstimate(flops=flops, bytes_accessed=moved, transcendentals=0),
    )(*ins)


def expert_from(values, dz, dx):
    pairs = [
        (z * SIDE + x, ((z - dz) % SIDE) * SIDE + (x - dx) % SIDE)
        for z in range(SIDE)
        for x in range(SIDE)
    ]
    return lax.ppermute(values, "expert", pairs)


def dp_from(values, dy):
    pairs = [(y * 2 + c, ((y - dy) % SIDE) * 2 + c) for y in range(SIDE) for c in range(2)]
    return lax.ppermute(values, "dp", pairs)


def core_swap(values):
    return lax.ppermute(values, "dp", [(d, d ^ 1) for d in range(DP)])


def gather_z(values):
    far = {m: expert_from(values, m, 0) for m in (1, 3, 2)}
    return [values, far[1], far[2], far[3]]


def gather_x(values):
    far = {m: expert_from(values, 0, m) for m in (1, 3, 2)}
    return [values, far[1], far[2], far[3]]


def gather_dp(values):
    far = {m: dp_from(values, m) for m in (1, 3, 2)}
    mine = [values, far[1], far[2], far[3]]
    return mine + [core_swap(part) for part in mine]


def reduce_dp(mine, other):
    swapped = core_swap(other)
    pairs = [(mine[m].astype(f32) + swapped[m].astype(f32)).astype(bf16) for m in range(SIDE)]
    total = pairs[0].astype(f32)
    for m in (1, 3, 2):
        total = total + dp_from(pairs[m], SIDE - m).astype(f32)
    return total


def swap_all(values):
    return lax.all_to_all(values, "expert", split_axis=0, concat_axis=0, tiled=True)


def part_place(info, r):
    return ((info[2] + r % SIDE) % SIDE) * 2 + (info[3] ^ (r // SIDE))


def rotated(values, c, s):
    w1, w2 = values[: HD // 2], values[HD // 2 :]
    return jnp.concatenate([w1 * c - w2 * s, w2 * c + w1 * s], axis=0)


def rotated_back(values, c, s):
    w1, w2 = values[: HD // 2], values[HD // 2 :]
    return jnp.concatenate([w1 * c + w2 * s, w2 * c - w1 * s], axis=0)


def allowed(ki, qi, start):
    key = ki * QB + lax.broadcasted_iota(jnp.int32, (QB, QB), 0)
    keep = key >= start
    if ki == qi:
        keep = keep & (key <= qi * QB + lax.broadcasted_iota(jnp.int32, (QB, QB), 1))
    return keep


def attend_kernel(info, *refs):
    a, b, parts = refs[0:4], refs[4:8], refs[8:16]
    cos, sin, start, normed, small, qz, kvt, out_t, lse, send = refs[16:26]
    w_block, w_turned, kvn, sems = refs[26:30]
    z, x = info[0], info[1]
    e = z * SIDE + x
    columns = (e // 2, 8 + e // 4, 12 + e // 4)
    copies = []
    for r in range(8):
        place = pl.multiple_of(part_place(info, r) * TOK, TOK)
        for j in range(3):
            copies.append(
                pltpu.make_async_copy(
                    parts[r].at[pl.ds(0, TOK), pl.ds(pl.multiple_of(columns[j] * 128, 128), 128)],
                    w_block.at[j, pl.ds(place, TOK), :],
                    sems.at[r * 6 + j],
                )
            )
            copies.append(
                pltpu.make_async_copy(
                    parts[r].at[pl.ds(TOK, EXTRA), pl.ds(j * 128, 128)],
                    small.at[pl.ds(j * EXTRA, EXTRA), pl.ds(place, 128)],
                    sems.at[r * 6 + 3 + j],
                )
            )
    for copy in copies:
        copy.start()
    for copy in copies:
        copy.wait()
    gain = small[2 * EXTRA : 3 * EXTRA, :].astype(f32)[0:1, :]
    for mz in range(SIDE):
        for mx in range(SIDE):
            block = ((z + mz) % SIDE) * SIDE + (x + mx) % SIDE
            rows = pl.ds(pl.multiple_of(block * TOK, TOK), TOK)
            left = a[mz][mx * TOK : (mx + 1) * TOK, :].astype(f32)
            right = b[mx][mz * TOK : (mz + 1) * TOK, :].astype(f32)
            square = jnp.sum(left * left + right * right, axis=-1, keepdims=True)
            r = lax.rsqrt(square * (1.0 / D) + eps)
            normed[rows, 0:512] = (left * r * gain[:, 0:512]).astype(bf16)
            normed[rows, 512:1024] = (right * r * gain[:, 512:1024]).astype(bf16)
    halves = (e % 2, (e // 2) % 2, (e // 2) % 2)
    for j in range(3):
        w_turned[j] = w_block[j].astype(f32).T.astype(bf16)
    w_head = jnp.concatenate(
        [w_turned[j, pl.ds(pl.multiple_of(halves[j] * HD, HD), HD), :] for j in range(3)], axis=0
    )
    for i in range(SEQ // QB):
        span = slice(i * QB, (i + 1) * QB)
        turned = mm(w_head, normed[span, :], NT)
        c, s = cos[:, span], sin[:, span]
        query = rotated(turned[0:HD], c, s).astype(bf16).astype(f32) * (HD**-0.5)
        key = rotated(turned[HD : 2 * HD], c, s)
        both = jnp.concatenate([key, turned[2 * HD : 3 * HD]], axis=0).astype(bf16)
        qz[0:HD, span] = query.astype(bf16)
        qz[HD:128, span] = jnp.zeros((HD, QB), bf16)
        kvt[:, span] = both
        kvn[span, :] = both.astype(f32).T.astype(bf16)
    for qi in range(SEQ // QB):
        span = slice(qi * QB, (qi + 1) * QB)
        query = qz[:, span]
        top = jnp.full((1, QB), -jnp.inf, f32)
        total = jnp.zeros((1, QB), f32)
        mixed = jnp.zeros((HD, QB), f32)
        for ki in range(qi, -1, -1):
            keys = slice(ki * QB, (ki + 1) * QB)
            scores = jnp.where(allowed(ki, qi, start[:, span]), mm(kvn[keys, :], query), masked)
            higher = jnp.maximum(top, jnp.max(scores, axis=0, keepdims=True))
            weights = jnp.exp(scores - higher)
            shrink = jnp.exp(top - higher)
            total = total * shrink + jnp.sum(weights, axis=0, keepdims=True)
            mixed = mixed * shrink + mm(kvt[HD:128, keys], weights.astype(bf16))
            top = higher
        mixed = mixed / total
        lse[:, span] = top + jnp.log(total)
        out_t[:, span] = mixed
        for j in range(QB // TOK):
            send[qi * (QB // TOK) + j] = mixed[:, j * TOK : (j + 1) * TOK].astype(bf16)


def load_rows(info, parts, column, width, target, sems):
    copies = []
    for r in range(8):
        place = pl.multiple_of(part_place(info, r) * TOK, TOK)
        copies.append(
            pltpu.make_async_copy(
                parts[r].at[pl.ds(0, TOK), pl.ds(column, width)],
                target.at[pl.ds(place, TOK), :],
                sems.at[r],
            )
        )
    return copies


def project_kernel(info, *refs):
    mixed_t, states, small, table = refs[0:4]
    parts = refs[4:12]
    hidden, send, w_out, sems = refs[12:16]
    copies = load_rows(info, parts, 2048, D, w_out, sems)
    for copy in copies:
        copy.start()
    mixed = mixed_t[...].astype(f32).T.astype(bf16)
    for copy in copies:
        copy.wait()
    gain = small[2 * EXTRA : 3 * EXTRA, :].astype(f32)[1:2, :]
    value = states[...].astype(f32) + mm(mixed, w_out[...])
    hidden[...] = value
    r = lax.rsqrt(jnp.mean(value * value, axis=-1, keepdims=True) + eps)
    ffn = (value * r * gain).astype(bf16)
    send[...] = mm(table[...], ffn).astype(bf16)


def unweave(source, spread, target):
    for s in range(PEERS):
        rows = source[s * 2 * CAP : (s + 1) * 2 * CAP, :].astype(f32)
        spread[0, s * CAP : (s + 1) * CAP, :] = rows[0:CAP]
        spread[1, s * CAP : (s + 1) * CAP, :] = rows[CAP : 2 * CAP]
    for i in range(2):
        target[i] = spread[i].astype(bf16)


def weave(spread, target):
    for s in range(PEERS):
        rows = slice(s * CAP, (s + 1) * CAP)
        target[s * 2 * CAP : (s + 1) * 2 * CAP, :] = jnp.concatenate(
            [spread[0, rows, :], spread[1, rows, :]], axis=0
        ).astype(bf16)


def expert_kernel(info, *refs):
    arrived, arrived_grad, small = refs[0:3]
    parts = refs[3:11]
    sent, xs, gs, acted, dgate, dup, gates, lgs = refs[11:19]
    spread, wg, wu, wd, sems = refs[19:24]
    copies = []
    for r in range(8):
        d = part_place(info, r)
        rows = pl.ds(pl.multiple_of(d * TOK, TOK), TOK)
        half = pl.ds(pl.multiple_of(d * HD, HD), HD)
        part = parts[r]
        for k, (first, count, target) in enumerate(
            (
                (0, 128, wg.at[:, rows, :]),
                (128, 128, wu.at[:, rows, :]),
                (256, 64, wd.at[:, half, 0:512]),
                (320, 64, wd.at[:, half, 512:1024]),
            )
        ):
            copies.append(
                pltpu.make_async_copy(
                    part.at[:, pl.ds(first, count), :], target, sems.at[r * 4 + k]
                )
            )
    for copy in copies:
        copy.start()
    unweave(arrived, spread, xs)
    unweave(arrived_grad, spread, gs)
    for copy in copies:
        copy.wait()
    router = small[0 : 2 * EXTRA, :]
    first = (info[0] * SIDE + info[1]) * 2
    chunk = ROWS // 2

    def step(n, carry):
        i = n // 2
        rows = pl.ds(pl.multiple_of((n % 2) * chunk, chunk), chunk)
        x = xs[i, rows, :]
        logits = mm(x, router, NT)
        peak = jnp.max(logits, axis=-1, keepdims=True)
        chances = jnp.exp(logits - peak)
        chances = chances / jnp.sum(chances, axis=-1, keepdims=True)
        mine = (lax.broadcasted_iota(jnp.int32, (chunk, EXPERTS), 1) == first + i).astype(f32)
        gate = jnp.sum(chances * mine, axis=-1, keepdims=True)
        gate_pre = mm(x, wg[i])
        up_pre = mm(x, wu[i])
        sigmoid = 1.0 / (1.0 + jnp.exp(-gate_pre))
        silu = gate_pre * sigmoid
        act = (silu * up_pre).astype(bf16)
        acted[i, rows, :] = act
        back = mm(gs[i, rows, :], wd[i], NT)
        dot = jnp.sum(act.astype(f32) * back, axis=-1, keepdims=True)
        back = back * gate
        gate_grad = (back * up_pre * (sigmoid * (1.0 + gate_pre * (1.0 - sigmoid)))).astype(bf16)
        up_grad = (back * silu).astype(bf16)
        dgate[i, rows, :] = gate_grad
        dup[i, rows, :] = up_grad
        lg = (dot * gate * (mine - chances)).astype(bf16)
        lgs[i, rows, :] = lg
        gates[i, rows, :] = jnp.broadcast_to(gate, (chunk, 128))
        spread[i, rows, :] = (
            mm(gate_grad, wg[i], NT) + mm(up_grad, wu[i], NT) + mm(lg, router)
        )
        return carry

    lax.fori_loop(0, 4, step, 0)
    weave(spread, sent)


def weights_kernel(info, *refs):
    xs, gs, acted, dgate, dup, gates, lgs = refs[0:7]
    parts = refs[7:15]
    returned, mine, other, router_grad = refs[15:19]
    spread, wd, sums, down_sums, sems = refs[19:24]
    copies = []
    for r in range(8):
        half = pl.ds(pl.multiple_of(part_place(info, r) * HD, HD), HD)
        for k in range(2):
            copies.append(
                pltpu.make_async_copy(
                    parts[r].at[:, pl.ds(256 + 64 * k, 64), :],
                    wd.at[:, half, k * 512 : (k + 1) * 512],
                    sems.at[r * 2 + k],
                )
            )
    for copy in copies:
        copy.start()
    for copy in copies:
        copy.wait()
    router_grad[...] = jnp.zeros_like(router_grad)

    def step(i, carry):
        x = xs[i]
        gate = gates[i][:, 0:1]
        spread[i] = mm(acted[i], wd[i]) * gate
        slot_grad = (gs[i].astype(f32) * gate).astype(bf16)
        router_grad[...] += mm(lgs[i], x, TN)
        sums[0] = mm(x, dgate[i], TN).astype(bf16)
        sums[1] = mm(x, dup[i], TN).astype(bf16)
        down_sums[...] = mm(acted[i], slot_grad, TN).astype(bf16)
        for r in range(8):
            d = part_place(info, r)
            rows = pl.ds(pl.multiple_of(d * TOK, TOK), TOK)
            half = pl.ds(pl.multiple_of(d * HD, HD), HD)
            target = mine if r < SIDE else other
            m = r % SIDE
            target[m, i, 0:128, :] = sums[0, rows, :]
            target[m, i, 128:256, :] = sums[1, rows, :]
            target[m, i, 256:320, :] = down_sums[half, 0:512]
            target[m, i, 320:384, :] = down_sums[half, 512:1024]
        return carry

    lax.fori_loop(0, 2, step, 0)
    weave(spread, returned)


def hidden_kernel(info, *refs):
    arrived, table_t, hidden_ref, cot, small = refs[0:5]
    parts = refs[5:13]
    hidden_grad, low, send, gain_grad, w_out, sems = refs[13:19]
    copies = load_rows(info, parts, 2048, D, w_out, sems)
    for copy in copies:
        copy.start()
    grad = mm(table_t[...], arrived[...])
    hidden = hidden_ref[...]
    gain = small[2 * EXTRA : 3 * EXTRA, :].astype(f32)[1:2, :]
    r = lax.rsqrt(jnp.mean(hidden * hidden, axis=-1, keepdims=True) + eps)
    scaled = grad * gain
    dot = jnp.mean(scaled * hidden, axis=-1, keepdims=True)
    total = cot[...].astype(f32) + r * scaled - hidden * (r * r * r * dot)
    gain_grad[...] = jnp.sum(grad * hidden * r, axis=0, keepdims=True)
    hidden_grad[...] = total
    low[...] = total.astype(bf16)
    for copy in copies:
        copy.wait()
    turned = mm(w_out[...], low[...], NT).astype(bf16)
    send[...] = turned.reshape(HEADS, HD, TOK)


def out_weights_kernel(info, *refs):
    mixed_t, low, router_grad, gain_grad = refs[0:4]
    mine, other, extra = refs[4:7]
    block = jnp.concatenate(
        [router_grad[...], jnp.broadcast_to(gain_grad[...], (8, D)), jnp.zeros((88, D), f32)],
        axis=0,
    )
    extra[...] = block.T
    for r in range(8):
        rows = pl.ds(pl.multiple_of(part_place(info, r) * TOK, TOK), TOK)
        target = mine if r < SIDE else other
        target[r % SIDE, :, 0:D] = mm(mixed_t[rows, :], low[...]).astype(bf16)
        target[r % SIDE, :, D:PACK] = extra[rows, :].astype(bf16)


def attend_back_kernel(info, *refs):
    qz, kvt, out_t, lse, arrived, cos, sin, start, normed = refs[0:9]
    send, mine, other = refs[9:12]
    kvn, oz, qon, dq, low, delta, sums = refs[12:19]
    steps = SEQ // QB
    for i in range(steps):
        span = slice(i * QB, (i + 1) * QB)
        kvn[span, :] = kvt[:, span].astype(f32).T.astype(bf16)
        got = jnp.concatenate([arrived[i * 4 + j] for j in range(4)], axis=1)
        oz[0:HD, span] = jnp.zeros((HD, QB), bf16)
        oz[HD:128, span] = got
        wide = got.astype(f32)
        delta[:, span] = jnp.sum(wide * out_t[:, span], axis=0, keepdims=True)
        qon[span, :] = jnp.concatenate([qz[0:HD, span].astype(f32), wide], axis=0).T.astype(bf16)
        dq[:, span] = jnp.zeros((HD, QB), f32)
    for ki in range(steps):
        keys = slice(ki * QB, (ki + 1) * QB)
        value_sum = jnp.zeros((QB, 128), f32)
        key_sum = jnp.zeros((QB, 128), f32)
        for qi in range(ki, steps):
            span = slice(qi * QB, (qi + 1) * QB)
            scores = mm(kvn[keys, :], qz[:, span])
            expo = jnp.where(
                allowed(ki, qi, start[:, span]), jnp.exp(scores - lse[:, span]), 0.0
            )
            back = mm(kvn[keys, :], oz[:, span])
            score_grad = (expo * (back - delta[:, span])).astype(bf16)
            value_sum = value_sum + mm(expo.astype(bf16), qon[span, :])
            key_sum = key_sum + mm(score_grad, qon[span, :])
            dq[:, span] += mm(kvt[0:HD, keys], score_grad)
        lane = lax.broadcasted_iota(jnp.int32, (QB, 128), 1)
        turned = jnp.where(lane < HD, key_sum, value_sum).T
        low[HD : 2 * HD, keys] = rotated_back(turned[0:HD], cos[:, keys], sin[:, keys]).astype(bf16)
        low[2 * HD : 3 * HD, keys] = turned[HD:128].astype(bf16)
    for i in range(steps):
        span = slice(i * QB, (i + 1) * QB)
        low[0:HD, span] = rotated_back(
            dq[:, span] * (HD**-0.5), cos[:, span], sin[:, span]
        ).astype(bf16)
    for j in range(PEERS):
        send[j] = low[:, j * TOK : (j + 1) * TOK]
    total = mm(low[...], normed[...]).astype(bf16)
    for d in range(DP):
        sums[d] = total[:, d * TOK : (d + 1) * TOK]
    for r in range(8):
        target = mine if r < SIDE else other
        target[r % SIDE] = sums[part_place(info, r)]


def input_kernel(info, *refs):
    arrived, hidden_grad, states, small = refs[0:4]
    parts = refs[4:12]
    grad, wide, sems = refs[12:15]
    copies = load_rows(info, parts, 0, 2048, wide, sems)
    for copy in copies:
        copy.start()
    turned = arrived[...].astype(f32)
    dq = turned[:, 0:HD].reshape(HEADS * HD, TOK).T.astype(bf16)
    pairs = turned[:, HD : 3 * HD].reshape(HEADS // 2, 2, 2 * HD, TOK)
    pairs = pairs[:, 0] + pairs[:, 1]
    dk = pairs[:, 0:HD].reshape(512, TOK).T.astype(bf16)
    dv = pairs[:, HD : 2 * HD].reshape(512, TOK).T.astype(bf16)
    for copy in copies:
        copy.wait()
    back = (
        mm(dq, wide[:, 0:1024], NT)
        + mm(dk, wide[:, 1024:1536], NT)
        + mm(dv, wide[:, 1536:2048], NT)
    )
    x = states[...].astype(f32)
    gain = small[2 * EXTRA : 3 * EXTRA, :].astype(f32)[0:1, :]
    r = lax.rsqrt(jnp.mean(x * x, axis=-1, keepdims=True) + eps)
    scaled = back * gain
    dot = jnp.mean(scaled * x, axis=-1, keepdims=True)
    grad[...] = hidden_grad[...] + r * scaled - x * (r * r * r * dot)


def unpack_kernel(*refs):
    arrived, query, key, value, out = refs
    turned = arrived[:, 0:192, :].astype(f32)
    query[...] = turned[:, 0:HD].reshape(HEADS * HD, TOK).T
    pairs = turned[:, HD : 3 * HD].reshape(HEADS // 2, 2, 2 * HD, TOK)
    pairs = pairs[:, 0] + pairs[:, 1]
    key[...] = pairs[:, 0:HD].reshape(512, TOK).T
    value[...] = pairs[:, HD : 2 * HD].reshape(512, TOK).T
    for j in range(PEERS):
        rows = arrived[j, 192:264, :].astype(f32)
        for g in range(9):
            out[j * 8 : (j + 1) * 8, g * 128 : (g + 1) * 128] = rows[g * 8 : (g + 1) * 8, :]


def per_device(
    inputs,
    segments,
    routes,
    gain_attn,
    w_query,
    w_key,
    w_value,
    w_out,
    gain_ffn,
    w_router,
    expert_gate,
    expert_up,
    expert_down,
    cotangent,
):
    place = lax.axis_index("expert")
    row = lax.axis_index("dp")
    info = jnp.stack([place // SIDE, place % SIDE, row // 2, row % 2]).astype(jnp.int32)
    states = inputs[0]
    cot = cotangent[0]

    first_a = jnp.concatenate(gather_x(states[:, 0:512]), axis=0)
    first_b = jnp.concatenate(gather_z(states[:, 512:1024]), axis=0)
    row_a = gather_z(first_a)
    row_b = gather_x(first_b)

    extra = jnp.concatenate(
        [
            w_router.T.reshape(2, EXTRA, TOK).transpose(1, 0, 2).reshape(EXTRA, 256),
            jnp.concatenate(
                [gain_attn[None, :], gain_ffn[None, :], jnp.zeros((EXTRA - 2, TOK), bf16)], axis=0
            ),
            jnp.zeros((EXTRA, WIDE - 384), bf16),
        ],
        axis=1,
    )
    dense = jnp.concatenate(
        [jnp.concatenate([w_query, w_key, w_value, w_out], axis=1), extra], axis=0
    )
    dense = gather_dp(dense)
    packed = jnp.concatenate(
        [expert_gate, expert_up, expert_down[:, :, 0:512], expert_down[:, :, 512:1024]], axis=1
    )
    packed = gather_dp(packed)

    segment_row = segments[0][None, :]
    index = jnp.arange(SEQ, dtype=jnp.int32)[None, :]
    start = jnp.zeros((1, SEQ), jnp.int32)
    for s in range(3):
        count = jnp.sum((segment_row == s).astype(jnp.int32))
        start = start + jnp.where(segment_row > s, count, 0)
    freqs = theta ** (-jnp.arange(0, HD, 2, dtype=f32) / HD)
    angles = freqs[:, None] * (index - start).astype(f32)
    cosine, sine = jnp.cos(angles), jnp.sin(angles)

    my_routes = routes[0]
    names = jnp.arange(EXPERTS, dtype=jnp.int32)
    choose = jnp.any(my_routes.T[None, :, :] == names[:, None, None], axis=1).astype(f32)
    order = jnp.arange(TOK, dtype=jnp.int32)
    before = (order[:, None] < order[None, :]).astype(f32)
    rank = jnp.dot(choose, before, preferred_element_type=f32).astype(jnp.int32)
    slots = jnp.arange(CAP, dtype=jnp.int32)
    table = ((rank[:, None, :] == slots[None, :, None]) & (choose[:, None, :] > 0)).astype(bf16)
    table = table.reshape(EXPERTS * CAP, TOK)
    table_t = table.T
    cot_send = jnp.dot(table, cot, preferred_element_type=f32).astype(bf16)
    cot_arrived = swap_all(cot_send)

    normed, small, qz, kvt, out_t, lse, mixed_send = run(
        attend_kernel,
        "attend",
        (
            shape((SEQ, D), bf16),
            shape((3 * EXTRA, D), bf16),
            shape((128, SEQ), bf16),
            shape((128, SEQ), bf16),
            shape((HD, SEQ), f32),
            shape((1, SEQ), f32),
            shape((HEADS, HD, TOK), bf16),
        ),
        (info, *row_a, *row_b, *dense, cosine, sine, start),
        [SM] + [VM] * 8 + [HB] * 8 + [VM] * 3,
        (
            pltpu.VMEM((3, D, 128), bf16),
            pltpu.VMEM((3, 128, D), bf16),
            pltpu.VMEM((SEQ, 128), bf16),
            pltpu.SemaphoreType.DMA((48,)),
        ),
        limit=32,
        flops=6 * 10**9,
        moved=10 * MIB,
    )
    mixed_t = swap_all(mixed_send).reshape(HEADS * HD, TOK)

    hidden, send = run(
        project_kernel,
        "project",
        (shape((TOK, D), f32), shape((2 * ROWS, D), bf16)),
        (info, mixed_t, states, small, table, *dense),
        [SM] + [VM] * 4 + [HB] * 8,
        (pltpu.VMEM((D, D), bf16), pltpu.SemaphoreType.DMA((8,))),
        flops=10**9,
        moved=6 * MIB,
    )
    arrived = swap_all(send)

    sent_grad, xs, gs, acted, dgate, dup, gates, lgs = run(
        expert_kernel,
        "experts",
        (
            shape((2 * ROWS, D), bf16),
            shape((2, ROWS, D), bf16),
            shape((2, ROWS, D), bf16),
            shape((2, ROWS, EF), bf16),
            shape((2, ROWS, EF), bf16),
            shape((2, ROWS, EF), bf16),
            shape((2, ROWS, 128), f32),
            shape((2, ROWS, EXPERTS), bf16),
        ),
        (info, arrived, cot_arrived, small, *packed),
        [SM] + [VM] * 3 + [HB] * 8,
        (
            pltpu.VMEM((2, ROWS, D), f32),
            pltpu.VMEM((2, D, EF), bf16),
            pltpu.VMEM((2, D, EF), bf16),
            pltpu.VMEM((2, EF, D), bf16),
            pltpu.SemaphoreType.DMA((32,)),
        ),
        limit=48,
        flops=7 * 10**9,
        moved=20 * MIB,
    )
    back = swap_all(sent_grad)

    returned, grads_mine, grads_other, router_grad = run(
        weights_kernel,
        "weights",
        (
            shape((2 * ROWS, D), bf16),
            shape((SIDE, 2, 384, 512), bf16),
            shape((SIDE, 2, 384, 512), bf16),
            shape((EXPERTS, D), f32),
        ),
        (info, xs, gs, acted, dgate, dup, gates, lgs, *packed),
        [SM] + [VM] * 7 + [HB] * 8,
        (
            pltpu.VMEM((2, ROWS, D), f32),
            pltpu.VMEM((2, EF, D), bf16),
            pltpu.VMEM((2, D, EF), bf16),
            pltpu.VMEM((EF, D), bf16),
            pltpu.SemaphoreType.DMA((16,)),
        ),
        limit=48,
        flops=6 * 10**9,
        moved=20 * MIB,
    )
    expert_sums = reduce_dp(grads_mine, grads_other)

    hidden_grad, low, grad_send, gain_grad = run(
        hidden_kernel,
        "hidden_grad",
        (
            shape((TOK, D), f32),
            shape((TOK, D), bf16),
            shape((HEADS, HD, TOK), bf16),
            shape((1, D), f32),
        ),
        (info, back, table_t, hidden, cot, small, *dense),
        [SM] + [VM] * 5 + [HB] * 8,
        (pltpu.VMEM((D, D), bf16), pltpu.SemaphoreType.DMA((8,))),
        flops=10**9,
        moved=6 * MIB,
    )
    mixed_grad = swap_all(grad_send)

    out_mine, out_other = run(
        out_weights_kernel,
        "out_weights",
        (shape((SIDE, TOK, PACK), bf16), shape((SIDE, TOK, PACK), bf16)),
        (info, mixed_t, low, router_grad, gain_grad),
        [SM] + [VM] * 4,
        (pltpu.VMEM((D, 128), f32),),
        flops=10**9,
        moved=4 * MIB,
    )
    out_sums = reduce_dp(out_mine, out_other).astype(bf16)
    out_sums = swap_all(out_sums).reshape(PEERS, 8, PACK)
    out_sums = jnp.sum(out_sums.astype(f32), axis=0).astype(bf16)
    out_sums = jnp.concatenate([out_sums[:, g * 128 : (g + 1) * 128] for g in range(9)], axis=0)

    grads_send, w_mine, w_other = run(
        attend_back_kernel,
        "attend_back",
        (
            shape((PEERS, 192, TOK), bf16),
            shape((SIDE, 192, TOK), bf16),
            shape((SIDE, 192, TOK), bf16),
        ),
        (info, qz, kvt, out_t, lse, mixed_grad, cosine, sine, start, normed),
        [SM] + [VM] * 9,
        (
            pltpu.VMEM((SEQ, 128), bf16),
            pltpu.VMEM((128, SEQ), bf16),
            pltpu.VMEM((SEQ, 128), bf16),
            pltpu.VMEM((HD, SEQ), f32),
            pltpu.VMEM((192, SEQ), bf16),
            pltpu.VMEM((1, SEQ), f32),
            pltpu.VMEM((DP, 192, TOK), bf16),
        ),
        limit=32,
        flops=8 * 10**9,
        moved=10 * MIB,
    )
    w_sums = reduce_dp(w_mine, w_other).astype(bf16)

    last = jnp.concatenate([w_sums, out_sums], axis=0)
    last = jnp.concatenate(
        [grads_send, jnp.broadcast_to(last[None], (PEERS, 264, TOK))], axis=1
    )
    last = swap_all(last)
    grads_arrived, sums_arrived = last[:, 0:192], last[:, 192:456]

    grad_input = run(
        input_kernel,
        "grad_input",
        shape((TOK, D), f32),
        (info, grads_arrived, hidden_grad, states, small, *dense),
        [SM] + [VM] * 4 + [HB] * 8,
        (pltpu.VMEM((D, 2048), bf16), pltpu.SemaphoreType.DMA((8,))),
        flops=10**9,
        moved=6 * MIB,
    )
    sum_query, sum_key, sum_value, sum_rest = run(
        unpack_kernel,
        "unpack",
        (
            shape((TOK, 1024), f32),
            shape((TOK, 512), f32),
            shape((TOK, 512), f32),
            shape((TOK, PACK), f32),
        ),
        (sums_arrived,),
        [VM],
        moved=4 * MIB,
    )
    weighted = (
        jnp.sum(sum_query * w_query.astype(f32), axis=-1)
        + jnp.sum(sum_key * w_key.astype(f32), axis=-1)
        + jnp.sum(sum_value * w_value.astype(f32), axis=-1)
    )
    sum_gain_attn = weighted / gain_attn.astype(f32)

    picked = swap_all(returned)
    output = hidden + jnp.dot(table_t, picked, preferred_element_type=f32)

    return (
        output.astype(bf16)[None],
        grad_input[None],
        sum_gain_attn,
        sum_query,
        sum_key,
        sum_value,
        sum_rest[:, 0:1024],
        sum_rest[:, 1056],
        sum_rest[:, 1024:1056],
        expert_sums[:, 0:128],
        expert_sums[:, 128:256],
        jnp.concatenate([expert_sums[:, 256:320], expert_sums[:, 320:384]], axis=2),
    )


def solution(mesh):
    placed = (
        P("dp", "expert", None),
        P("dp", None),
        P("dp", "expert", None),
        P("dp"),
        P("dp", None),
        P("dp", None),
        P("dp", None),
        P("dp", None),
        P("dp"),
        P("dp", None),
        P("expert", "dp", None),
        P("expert", "dp", None),
        P("expert", "dp", None),
        P("dp", "expert", None),
    )
    return jax.shard_map(
        per_device,
        mesh=mesh,
        in_specs=placed,
        out_specs=(
            P("dp", "expert", None),
            P("dp", "expert", None),
            P("dp"),
            P("dp", None),
            P("dp", None),
            P("dp", None),
            P("dp", None),
            P("dp"),
            P("dp", None),
            P("expert", "dp", None),
            P("expert", "dp", None),
            P("expert", "dp", None),
        ),
        check_vma=False,
    )
```

```python
import jax
import jax.numpy as jnp
from jax import lax
from jax.experimental import pallas as pl
from jax.experimental.pallas import tpu as pltpu
from jax.sharding import PartitionSpec as P

D = 1024
HEADS = 16
HD = 64
EF = 512
EXPERTS = 32
CAP = 40
TOK = 128
SEQ = 2048
SIDE = 4
PEERS = 16
DP = 8
QB = 512
HALF = 512
ROWS = PEERS * CAP
EXTRA = 16
PACK = 1152
ROW_STEP = 2 * TOK + EXTRA

eps = 1e-06
theta = 10000.0
masked = -1000000000.0
bf16 = jnp.bfloat16
f32 = jnp.float32
MIB = 1 << 20

NN = (((1,), (0,)), ((), ()))
NT = (((1,), (1,)), ((), ()))
TN = (((0,), (0,)), ((), ()))


def mm(left, right, dims=NN):
    return lax.dot_general(left, right, dims, preferred_element_type=f32)


def shape(dims, dtype):
    return jax.ShapeDtypeStruct(dims, dtype)


def cuts(dims, dtype):
    size = jnp.dtype(dtype).itemsize
    for dim in dims:
        size *= dim
    step = 16 if len(dims) == 2 else 1
    for count in (8, 4, 2):
        if dims[0] % (count * step) == 0 and size // count >= MIB // 4:
            return count
    return 1


class Moved:
    def __init__(self, source, target, sems, first, dims, dtype):
        count = cuts(dims, dtype)
        rows = dims[0] // count
        self.copies = [
            pltpu.make_async_copy(
                source.at[pl.ds(k * rows, rows)], target.at[pl.ds(k * rows, rows)], sems.at[first + k]
            )
            for k in range(count)
        ]
        self.started = False
        self.waited = False

    def start(self):
        self.started = True
        for copy in self.copies:
            copy.start()

    def wait(self):
        if not self.waited:
            self.waited = True
            for copy in self.copies:
                copy.wait()


class In(Moved):
    def __init__(self, source, target, *rest):
        super().__init__(source, target, *rest)
        self.target = target

    def get(self):
        self.wait()
        return self.target


class Out(Moved):
    def __init__(self, source, target, *rest):
        super().__init__(source, target, *rest)
        self.ref = source

    def start_part(self, k):
        self.started = True
        self.copies[k].start()


class Near:
    def __init__(self, array):
        self.array = array


class Held:
    def __init__(self, ref):
        self.ref = ref

    def get(self):
        return self.ref

    def start(self):
        pass


def tied(value, *others):
    return lax.optimization_barrier((value, *others))[0]


def run(body, name, ins, raws, outs, scratch=(), limit=24, after=(), cost=0):
    info, arrays = ins[0], ins[1:]
    in_near = [isinstance(v, Near) for v in arrays]
    out_near = [isinstance(v, Near) for v in outs]
    arrays = [v.array if isinstance(v, Near) else v for v in arrays]
    outs = [v.array if isinstance(v, Near) else v for v in outs]
    both = list(zip((*arrays, *outs), (*in_near, *out_near)))
    count = sum(cuts(v.shape, v.dtype) for v, near in both if not near)
    held = [pltpu.VMEM(v.shape, v.dtype) for v, near in both if not near]

    def kernel(*refs):
        info_ref, refs = refs[0], refs[1:]
        in_refs, refs = refs[: len(arrays)], refs[len(arrays) :]
        raw_refs, refs = refs[: len(raws)], refs[len(raws) :]
        out_refs, refs = refs[: len(outs)], refs[len(outs) :]
        spaces, refs = list(refs[: len(held)]), refs[len(held) :]
        sems, rest = refs[0], refs[1:]
        first = 0
        fetched, sent = [], []
        for v, near, ref in zip(arrays, in_near, in_refs):
            if near:
                fetched.append(Held(ref))
                continue
            fetched.append(In(ref, spaces.pop(0), sems, first, v.shape, v.dtype))
            first += cuts(v.shape, v.dtype)
        for v, near, ref in zip(outs, out_near, out_refs):
            if near:
                sent.append(Held(ref))
                continue
            sent.append(Out(spaces.pop(0), ref, sems, first, v.shape, v.dtype))
            first += cuts(v.shape, v.dtype)
        for one in fetched:
            one.start()
        body(info_ref, fetched, raw_refs, sent, rest)
        for one in fetched:
            one.get()
        moves = [one for one in sent if isinstance(one, Out)]
        for one in moves:
            if not one.started:
                one.start()
        for one in moves:
            one.wait()

    if after:
        info = tied(info, *after)

    def pinned(v, near=False):
        return v if near else pltpu.with_memory_space_constraint(v, pltpu.HBM)

    def spec(near=False):
        return pl.BlockSpec(memory_space=pltpu.VMEM if near else pltpu.HBM)

    return pl.pallas_call(
        kernel,
        name=name,
        out_shape=tuple(
            shape(v.shape, v.dtype) if near else pltpu.HBM(v.shape, v.dtype)
            for v, near in zip(outs, out_near)
        ),
        in_specs=[pl.BlockSpec(memory_space=pltpu.SMEM)]
        + [spec(near) for near in in_near]
        + [spec()] * len(raws),
        out_specs=tuple(spec(near) for near in out_near),
        scratch_shapes=[*held, pltpu.SemaphoreType.DMA((max(count, 1),)), *scratch],
        compiler_params=pltpu.CompilerParams(vmem_limit_bytes=limit * MIB),
        cost_estimate=pl.CostEstimate(
            flops=1000 + cost * 10**9, bytes_accessed=1000, transcendentals=0
        ),
    )(info, *[pinned(v, near) for v, near in zip(arrays, in_near)], *[pinned(v) for v in raws])


def expert_from(values, dz, dx):
    pairs = [
        (z * SIDE + x, ((z - dz) % SIDE) * SIDE + (x - dx) % SIDE)
        for z in range(SIDE)
        for x in range(SIDE)
    ]
    return lax.ppermute(values, "expert", pairs)


def dp_from(values, dy):
    pairs = [(y * 2 + c, ((y - dy) % SIDE) * 2 + c) for y in range(SIDE) for c in range(2)]
    return lax.ppermute(values, "dp", pairs)


def core_swap(values):
    return lax.ppermute(values, "dp", [(d, d ^ 1) for d in range(DP)])


def gather_ring(values, step, *others):
    near = {m: step(values, m) for m in (1, 3)}
    far = step(tied(values, *others) if others else values, 2)
    return [values, near[1], far, near[3]]


def along_z(values, m):
    return expert_from(values, m, 0)


def along_x(values, m):
    return expert_from(values, 0, m)


def gather_dp(values, *others):
    far = {m: dp_from(values, m) for m in (1, 3, 2)}
    if others:
        far[2] = tied(far[2], *others)
    mine = [values, far[1], far[2], far[3]]
    return mine + [core_swap(part) for part in mine]


def send_pairs(pairs):
    return [dp_from(pairs[m], SIDE - m) for m in (1, 3, 2)]


def add_parts(first, others):
    total = first.astype(f32)
    for other in others:
        total = total + other.astype(f32)
    return total


def pair_kernel(info, ins, parts, outs, scratch):
    for m in range(SIDE):
        mine, other = ins[m].get()[...], ins[SIDE + m].get()[...]
        outs[m].ref[...] = (mine.astype(f32) + other.astype(f32)).astype(bf16)
        outs[m].start()


def pair_up(info, mine, other, name):
    swapped = [core_swap(part) for part in other]
    part = shape(mine[0].shape, bf16)
    return run(pair_kernel, name, (info, *mine, *swapped), (), (part,) * SIDE)


def swap_all(values):
    return lax.all_to_all(values, "expert", split_axis=0, concat_axis=0, tiled=True)


def part_place(info, r):
    return ((info[2] + r % SIDE) % SIDE) * 2 + (info[3] ^ (r // SIDE))


def aligned(index, step):
    return pl.ds(pl.multiple_of(index * step, step), step)


def rotated(values, c, s):
    w1, w2 = values[: HD // 2], values[HD // 2 :]
    return jnp.concatenate([w1 * c - w2 * s, w2 * c + w1 * s], axis=0)


def rotated_back(values, c, s):
    w1, w2 = values[: HD // 2], values[HD // 2 :]
    return jnp.concatenate([w1 * c + w2 * s, w2 * c - w1 * s], axis=0)


def allowed(ki, qi, start):
    key = ki * QB + lax.broadcasted_iota(jnp.int32, (QB, QB), 0)
    keep = key >= start
    if ki == qi:
        keep = keep & (key <= qi * QB + lax.broadcasted_iota(jnp.int32, (QB, QB), 1))
    return keep


def place_parts(info, parts, pieces, sems, place=part_place):
    copies = []
    for r in range(8):
        for k, piece in enumerate(pieces):
            source, target = piece(parts[r], place(info, r))
            copies.append(pltpu.make_async_copy(source, target, sems.at[r * len(pieces) + k]))
    for copy in copies:
        copy.start()
    return copies


def wait_all(copies):
    for copy in copies:
        copy.wait()


def dense_kernel(info, ins, parts, outs, scratch):
    router, gain_attn, gain_ffn, routes = ins
    query, key, value, cot, states = parts
    dense, cots = [out.ref for out in outs]
    sems = scratch[0]
    copies = [
        pltpu.make_async_copy(source, target, sems.at[k])
        for k, (source, target) in enumerate(
            (
                (query, dense.at[pl.ds(0, TOK), pl.ds(0, 1024)]),
                (key, dense.at[pl.ds(0, TOK), pl.ds(1024, 512)]),
                (value, dense.at[pl.ds(0, TOK), pl.ds(1536, 512)]),
                (cot, cots.at[pl.ds(0, TOK), :]),
                (states, cots.at[pl.ds(TOK + EXTRA, TOK), :]),
            )
        )
    ]
    for copy in copies:
        copy.start()
    rows = slice(TOK, TOK + EXTRA)
    dense[rows, 384:2048] = jnp.zeros((EXTRA, 2048 - 384), bf16)
    dense[rows, 0:128] = router.get()[0:EXTRA, :]
    dense[rows, 128:256] = router.get()[EXTRA : 2 * EXTRA, :]
    gains = [gain_attn.get()[...].astype(f32), gain_ffn.get()[...].astype(f32)]
    gains = jnp.concatenate([*gains, jnp.zeros((EXTRA - 2, TOK), f32)], axis=0)
    dense[rows, 256:384] = gains.astype(bf16)
    cots[rows, TOK:D] = jnp.zeros((EXTRA, D - TOK), bf16)
    names = jnp.concatenate([routes.get()[...].astype(f32), jnp.zeros((8, TOK), f32)], axis=0)
    cots[rows, 0:TOK] = names.astype(bf16)
    wait_all(copies)


def pack_kernel(info, ins, parts, outs, scratch):
    gate, up, down = parts
    packed = outs[0].ref
    sems = scratch[0]
    pairs = []
    for i in range(2):
        for k, source in enumerate(
            (
                gate.at[i],
                up.at[i],
                down.at[i, :, pl.ds(0, HALF)],
                down.at[i, :, pl.ds(HALF, HALF)],
            )
        ):
            row, count = i * 384 + (0, 128, 256, 320)[k], (128, 128, 64, 64)[k]
            pairs.append((source, packed.at[pl.ds(row, count), :]))
    copies = [
        pltpu.make_async_copy(source, target, sems.at[k])
        for k, (source, target) in enumerate(pairs)
    ]
    for copy in copies:
        copy.start()
    wait_all(copies)


def qkv_kernel(info, ins, parts, outs, scratch):
    states, cos, sin = ins
    small, send = outs
    wide, sems = scratch
    copies = place_parts(
        info,
        parts,
        [
            lambda part, d: (part.at[pl.ds(0, TOK), :], wide.at[aligned(d, TOK), :]),
            *(
                lambda part, d, k=k: (
                    part.at[pl.ds(TOK, EXTRA), pl.ds(128 * k, 128)],
                    small.ref.at[pl.ds(EXTRA * k, EXTRA), aligned(d, TOK)],
                )
                for k in range(3)
            ),
        ],
        sems,
    )
    x = states.get()[...].astype(f32)
    r = lax.rsqrt(jnp.mean(x * x, axis=-1, keepdims=True) + eps)
    cos, sin = cos.get()[...], sin.get()[...]
    wait_all(copies)
    small.start()
    gain = small.ref[2 * EXTRA : 3 * EXTRA, :].astype(f32)[0:1, :]
    low = (x * r * gain).astype(bf16)
    turned = mm(low, wide[:, 1024:2048]).T
    for g in range(HEADS // 2):
        key = rotated(turned[g * HD : (g + 1) * HD], cos, sin)
        value = turned[512 + g * HD : 512 + (g + 1) * HD]
        both = jnp.concatenate([key, value], axis=0).astype(bf16)
        send.ref[2 * g, HD : 3 * HD, :] = both
        send.ref[2 * g + 1, HD : 3 * HD, :] = both
    turned = mm(low, wide[:, 0:1024]).T
    for h in range(HEADS):
        query = rotated(turned[h * HD : (h + 1) * HD], cos, sin).astype(bf16).astype(f32)
        send.ref[h, 0:HD, :] = (query * (HD**-0.5)).astype(bf16)


def spread_heads(arrived, qz, kvt, kvn):
    for i in range(SEQ // QB):
        span = slice(i * QB, (i + 1) * QB)
        got = jnp.concatenate([arrived[i * 4 + j] for j in range(4)], axis=1)
        qz[0:HD, span] = got[0:HD]
        qz[HD:128, span] = jnp.zeros((HD, QB), bf16)
        kvt[:, span] = got[HD : 3 * HD]
        kvn[span, :] = got[HD : 3 * HD].astype(f32).T.astype(bf16)


def attend_kernel(info, ins, parts, outs, scratch):
    start = ins[1].get()
    out_t, lse, send = outs
    qz, kvt, kvn = scratch
    spread_heads(ins[0].get(), qz, kvt, kvn)
    for qi in range(SEQ // QB):
        span = slice(qi * QB, (qi + 1) * QB)
        query = qz[:, span]
        top = jnp.full((1, QB), -jnp.inf, f32)
        total = jnp.zeros((1, QB), f32)
        mixed = jnp.zeros((HD, QB), f32)
        for ki in range(qi, -1, -1):
            keys = slice(ki * QB, (ki + 1) * QB)
            scores = jnp.where(allowed(ki, qi, start[:, span]), mm(kvn[keys, :], query), masked)
            higher = jnp.maximum(top, jnp.max(scores, axis=0, keepdims=True))
            weights = jnp.exp(scores - higher)
            shrink = jnp.exp(top - higher)
            total = total * shrink + jnp.sum(weights, axis=0, keepdims=True)
            mixed = mixed * shrink + mm(kvt[HD:128, keys], weights.astype(bf16))
            top = higher
        mixed = mixed / total
        lse.ref[:, span] = top + jnp.log(total)
        out_t.ref[:, span] = mixed
        for j in range(QB // TOK):
            send.ref[qi * (QB // TOK) + j] = mixed[:, j * TOK : (j + 1) * TOK].astype(bf16)


def shards(gathered):
    return [gathered.at[d] for d in range(DP)]


def shard_place(info, r):
    return r


def w_out_pieces(target):
    return [lambda part, d: (part.at[:, :], target.at[aligned(d, TOK), :])]


def ranks(choose):
    order = lax.broadcasted_iota(jnp.int32, (TOK, TOK), 0)
    before = (order < lax.broadcasted_iota(jnp.int32, (TOK, TOK), 1)).astype(bf16)
    return mm(choose.astype(bf16), before).astype(jnp.int32)


def project_kernel(info, ins, parts, outs, scratch):
    mixed_t, states, small, routes = ins
    hidden, send, table = outs
    w_out, sems = scratch
    copies = place_parts(info, parts, w_out_pieces(w_out), sems)
    names = lax.broadcasted_iota(jnp.int32, (EXPERTS, TOK), 0)
    choose = jnp.zeros((EXPERTS, TOK), f32)
    routes = routes.get()
    for j in range(8):
        choose = choose + (names == routes[j : j + 1, :]).astype(f32)
    rank = jnp.where(choose > 0.0, ranks(choose), -1)
    slots = lax.broadcasted_iota(jnp.int32, (CAP, TOK), 0)
    for e in range(0, EXPERTS, 2):
        table.ref[e * CAP : (e + 2) * CAP, :] = jnp.concatenate(
            [(rank[e : e + 1] == slots).astype(f32), (rank[e + 1 : e + 2] == slots).astype(f32)],
            axis=0,
        ).astype(bf16)
    mixed = mixed_t.get()[...].astype(f32).T.astype(bf16)
    gain = small.get()[2 * EXTRA : 3 * EXTRA, :].astype(f32)[1:2, :]
    wait_all(copies)
    value = states.get()[...].astype(f32) + mm(mixed, w_out[...])
    hidden.ref[...] = value
    r = lax.rsqrt(jnp.mean(value * value, axis=-1, keepdims=True) + eps)
    ffn = (value * r * gain).astype(bf16)
    step = 2 * ROWS // len(send.copies)
    for k in range(len(send.copies)):
        rows = slice(k * step, (k + 1) * step)
        send.ref[rows, :] = mm(table.ref[rows, :], ffn).astype(bf16)
        send.start_part(k)


def rows_kernel(info, ins, parts, outs, scratch):
    grads, slots = outs
    cots, choose, spread, sems = scratch
    first = (info[0] * SIDE + info[1]) * 2
    copies = [
        pltpu.make_async_copy(
            parts[0].at[pl.ds(t * ROW_STEP, TOK + EXTRA), :], cots.at[t], sems.at[t]
        )
        for t in range(PEERS)
    ]
    for copy in copies:
        copy.start()
    wait_all(copies)
    for t in range(PEERS):
        routes = cots[t, TOK : TOK + EXTRA, 0:TOK].astype(f32)[0:8, :].astype(jnp.int32)
        for i in range(2):
            named = (routes == first + i).astype(f32)
            choose[2 * t + i : 2 * t + i + 1, :] = jnp.sum(named, axis=0, keepdims=True)
    rank = jnp.where(choose[...] > 0.0, ranks(choose[...]), -1)
    order = lax.broadcasted_iota(jnp.int32, (CAP, TOK), 0)
    for t in range(PEERS):
        hot = jnp.concatenate(
            [(rank[2 * t + i : 2 * t + i + 1] == order).astype(f32) for i in range(2)], axis=0
        )
        slots.ref[t] = hot.astype(bf16)
        rows = mm(hot.astype(bf16), cots[t, 0:TOK, :])
        for i in range(2):
            spread[i, t * CAP : (t + 1) * CAP, :] = rows[i * CAP : (i + 1) * CAP]
    for i in range(2):
        grads.ref[i] = spread[i].astype(bf16)


def norm_kernel(info, ins, parts, outs, scratch):
    gain = ins[0].get()[2 * EXTRA : 3 * EXTRA, :].astype(f32)[0:1, :]
    normed = outs[0]
    rows, sems = scratch
    copies = [
        pltpu.make_async_copy(
            parts[0].at[pl.ds(t * ROW_STEP + TOK + EXTRA, TOK), :], rows.at[t], sems.at[t]
        )
        for t in range(PEERS)
    ]
    for copy in copies:
        copy.start()
    step = PEERS // len(normed.copies)
    for t in range(PEERS):
        copies[t].wait()
        x = rows[t].astype(f32)
        r = lax.rsqrt(jnp.mean(x * x, axis=-1, keepdims=True) + eps)
        normed.ref[t * TOK : (t + 1) * TOK, :] = (x * r * gain).astype(bf16)
        if t % step == step - 1:
            normed.start_part(t // step)


def unweave(source, spread, target):
    for s in range(PEERS):
        rows = source[s * 2 * CAP : (s + 1) * 2 * CAP, :].astype(f32)
        spread[0, s * CAP : (s + 1) * CAP, :] = rows[0:CAP]
        spread[1, s * CAP : (s + 1) * CAP, :] = rows[CAP : 2 * CAP]
    for i in range(2):
        target[i] = spread[i].astype(bf16)


def weave(spread, sent):
    for s in range(PEERS):
        rows = slice(s * CAP, (s + 1) * CAP)
        sent.ref[s * 2 * CAP : (s + 1) * 2 * CAP, :] = jnp.concatenate(
            [spread[0, rows, :], spread[1, rows, :]], axis=0
        ).astype(bf16)
        if s % 2 == 1:
            sent.start_part(s // 2)


def expert_kernel(info, ins, parts, outs, scratch):
    arrived, grads, small = ins
    sent, xs, acted, dgate, dup, gates, lgs = [out.ref for out in outs]
    spread, wg, wu, wd, sems = scratch

    def piece(i, k):
        first, count, target, column = (
            (0, TOK, wg, 0),
            (128, TOK, wu, 0),
            (256, HD, wd, 0),
            (320, HD, wd, HALF),
        )[k]
        return lambda part, d: (
            part.at[pl.ds(i * 384 + first, count), :],
            target.at[i, aligned(d, count), pl.ds(column, HALF)],
        )

    copies = place_parts(
        info,
        shards(parts[0]),
        [piece(i, k) for i in range(2) for k in range(4)],
        sems,
        shard_place,
    )
    unweave(arrived.get(), spread, xs)
    outs[1].start()
    grads = grads.get()
    small = small.get()
    wait_all(copies)
    first = (info[0] * SIDE + info[1]) * 2
    chunk = ROWS // 2

    def step(n, carry):
        i = n // 2
        rows = aligned(n % 2, chunk)
        x = xs[i, rows, :]
        router = small[0 : 2 * EXTRA, :]
        logits = mm(x, router, NT)
        peak = jnp.max(logits, axis=-1, keepdims=True)
        chances = jnp.exp(logits - peak)
        chances = chances / jnp.sum(chances, axis=-1, keepdims=True)
        mine = (lax.broadcasted_iota(jnp.int32, (chunk, EXPERTS), 1) == first + i).astype(f32)
        gate = jnp.sum(chances * mine, axis=-1, keepdims=True)
        gate_pre = mm(x, wg[i])
        up_pre = mm(x, wu[i])
        sigmoid = 1.0 / (1.0 + jnp.exp(-gate_pre))
        silu = gate_pre * sigmoid
        act = (silu * up_pre).astype(bf16)
        acted[i, rows, :] = act
        back = mm(grads[i, rows, :], wd[i], NT)
        dot = jnp.sum(act.astype(f32) * back, axis=-1, keepdims=True)
        back = back * gate
        gate_grad = (back * up_pre * (sigmoid * (1.0 + gate_pre * (1.0 - sigmoid)))).astype(bf16)
        up_grad = (back * silu).astype(bf16)
        dgate[i, rows, :] = gate_grad
        dup[i, rows, :] = up_grad
        lg = (dot * gate * (mine - chances)).astype(bf16)
        lgs[i, rows, :] = jnp.concatenate([lg, jnp.zeros((chunk, 128 - EXPERTS), bf16)], axis=1)
        gates[i, rows, :] = jnp.broadcast_to(gate, (chunk, 128))
        spread[i, rows, :] = (
            mm(gate_grad, wg[i], NT) + mm(up_grad, wu[i], NT) + mm(lg, router)
        )
        return carry

    lax.fori_loop(0, 4, step, 0)
    for one in outs[2:]:
        one.start()
    weave(spread, outs[0])


def weights_kernel(info, ins, parts, outs, scratch):
    xs, gs, acted, dgate, dup, gates, lgs, slots = ins
    routed, router_grad = outs[0].ref, outs[9].ref
    mine, other = [out.ref for out in outs[1:5]], [out.ref for out in outs[5:9]]
    spread, wd, sums, down_sums, sems = scratch
    def piece(i, k):
        return lambda part, d: (
            part.at[pl.ds(i * 384 + 256 + HD * k, HD), :],
            wd.at[i, aligned(d, HD), pl.ds(k * HALF, HALF)],
        )

    copies = place_parts(
        info,
        shards(parts[0]),
        [piece(i, k) for i in range(2) for k in range(2)],
        sems,
        shard_place,
    )
    xs, gs, acted, dgate, dup, gates, lgs, slots = [one.get() for one in ins]
    wait_all(copies)
    router_grad[...] = jnp.zeros_like(router_grad)

    def step(i, carry):
        source = xs[i]
        gate = gates[i][:, 0:1]
        spread[i] = mm(acted[i], wd[i]) * gate
        slot_grad = (gs[i].astype(f32) * gate).astype(bf16)
        router_grad[...] += mm(lgs[i], source, TN)
        sums[0] = mm(source, dgate[i], TN).astype(bf16)
        sums[1] = mm(source, dup[i], TN).astype(bf16)
        down_sums[...] = mm(acted[i], slot_grad, TN).astype(bf16)
        for r in range(8):
            d = part_place(info, r)
            target = (*mine, *other)[r]
            target[i, 0:128, :] = sums[0, aligned(d, TOK), :]
            target[i, 128:256, :] = sums[1, aligned(d, TOK), :]
            target[i, 256:320, :] = down_sums[aligned(d, HD), 0:HALF]
            target[i, 320:384, :] = down_sums[aligned(d, HD), HALF:D]
        return carry

    lax.fori_loop(0, 2, step, 0)
    for one in (*outs[5:9], *outs[1:5]):
        one.start()
    for t in range(PEERS):
        span = slice(t * CAP, (t + 1) * CAP)
        rows = jnp.concatenate([spread[i, span, :] for i in range(2)], axis=0).astype(bf16)
        routed[t * TOK : (t + 1) * TOK, :] = mm(slots[t], rows, TN).astype(bf16)


def hidden_kernel(info, ins, parts, outs, scratch):
    arrived, table, hidden, cot, small = ins
    hidden_grad, low, send, gain_grad = outs
    w_out, sems = scratch
    copies = place_parts(info, parts, w_out_pieces(w_out), sems)
    grad = mm(table.get()[...], arrived.get()[...], TN)
    hidden = hidden.get()[...]
    gain = small.get()[2 * EXTRA : 3 * EXTRA, :].astype(f32)[1:2, :]
    r = lax.rsqrt(jnp.mean(hidden * hidden, axis=-1, keepdims=True) + eps)
    scaled = grad * gain
    dot = jnp.mean(scaled * hidden, axis=-1, keepdims=True)
    total = cot.get()[...].astype(f32) + r * scaled - hidden * (r * r * r * dot)
    gain_grad.ref[...] = jnp.sum(grad * hidden * r, axis=0, keepdims=True)
    hidden_grad.ref[...] = total
    low.ref[...] = total.astype(bf16)
    wait_all(copies)
    turned = mm(w_out[...], low.ref[...], NT).astype(bf16)
    send.ref[...] = turned.reshape(HEADS, HD, TOK)


def out_weights_kernel(info, ins, parts, outs, scratch):
    mixed_t, low, router_grad, gain_grad = [one.get() for one in ins]
    extra = scratch[0]
    block = jnp.concatenate(
        [
            router_grad[0:EXPERTS, :],
            jnp.broadcast_to(gain_grad[...], (8, D)),
            jnp.zeros((128 - EXPERTS - 8, D), f32),
        ],
        axis=0,
    )
    extra[...] = block.T
    for r in (4, 5, 6, 7, 0, 1, 2, 3):
        rows = aligned(part_place(info, r), TOK)
        target = outs[r].ref
        target[:, 0:D] = mm(mixed_t[rows, :], low[...]).astype(bf16)
        target[:, D:PACK] = extra[rows, :].astype(bf16)
        outs[r].start()


def attend_back_kernel(info, ins, parts, outs, scratch):
    heads, out_t, lse, arrived, cos, sin, start = [one.get() for one in ins[0:7]]
    send = outs[0].ref
    qz, kvt, kvn, oz, qon, dq, low, delta, sums = scratch
    steps = SEQ // QB
    spread_heads(heads, qz, kvt, kvn)
    for i in range(steps):
        span = slice(i * QB, (i + 1) * QB)
        got = jnp.concatenate([arrived[i * 4 + j] for j in range(4)], axis=1)
        oz[0:HD, span] = jnp.zeros((HD, QB), bf16)
        oz[HD:128, span] = got
        wide = got.astype(f32)
        delta[:, span] = jnp.sum(wide * out_t[:, span], axis=0, keepdims=True)
        qon[span, :] = jnp.concatenate([qz[0:HD, span].astype(f32), wide], axis=0).T.astype(bf16)
        dq[:, span] = jnp.zeros((HD, QB), f32)
    for ki in range(steps):
        keys = slice(ki * QB, (ki + 1) * QB)
        value_sum = jnp.zeros((QB, 128), f32)
        key_sum = jnp.zeros((QB, 128), f32)
        for qi in range(ki, steps):
            span = slice(qi * QB, (qi + 1) * QB)
            scores = mm(kvn[keys, :], qz[:, span])
            expo = jnp.where(
                allowed(ki, qi, start[:, span]), jnp.exp(scores - lse[:, span]), 0.0
            )
            back = mm(kvn[keys, :], oz[:, span])
            score_grad = (expo * (back - delta[:, span])).astype(bf16)
            value_sum = value_sum + mm(expo.astype(bf16), qon[span, :])
            key_sum = key_sum + mm(score_grad, qon[span, :])
            dq[:, span] += mm(kvt[0:HD, keys], score_grad)
        lane = lax.broadcasted_iota(jnp.int32, (QB, 128), 1)
        turned = jnp.where(lane < HD, key_sum, value_sum).T
        low[HD : 2 * HD, keys] = rotated_back(turned[0:HD], cos[:, keys], sin[:, keys]).astype(bf16)
        low[2 * HD : 3 * HD, keys] = turned[HD:128].astype(bf16)
    for i in range(steps):
        span = slice(i * QB, (i + 1) * QB)
        low[0:HD, span] = rotated_back(
            dq[:, span] * (HD**-0.5), cos[:, span], sin[:, span]
        ).astype(bf16)
    for j in range(PEERS):
        send[j] = low[:, j * TOK : (j + 1) * TOK]
    outs[0].start()
    total = mm(low[...], ins[7].get()[...]).astype(bf16)
    for d in range(DP):
        sums[d] = total[:, d * TOK : (d + 1) * TOK]
    for r in (4, 5, 6, 7, 0, 1, 2, 3):
        outs[1 + r].ref[...] = sums[part_place(info, r)]
        outs[1 + r].start()


def input_kernel(info, ins, parts, outs, scratch):
    arrived, hidden_grad, states, small = ins[0:4]
    grad, query, key, value, out, router, rest = [one.ref for one in outs]
    wide, sums, sems = scratch
    copies = place_parts(
        info,
        parts,
        [lambda part, d: (part.at[pl.ds(0, TOK), :], wide.at[aligned(d, TOK), :])],
        sems,
    )
    arrived = arrived.get()

    def pair_sum(first, count):
        pairs = arrived[:, first : first + count, :].astype(f32).reshape(HEADS // 2, 2, count, TOK)
        return (pairs[:, 0] + pairs[:, 1]).reshape(HEADS // 2 * count, TOK)

    dq = arrived[:, 0:HD, :].astype(f32).reshape(HEADS * HD, TOK).T.astype(bf16)
    dk = pair_sum(HD, HD).T.astype(bf16)
    dv = pair_sum(2 * HD, HD).T.astype(bf16)
    query[...] = arrived[:, 192 : 192 + HD, :].astype(f32).reshape(HEADS * HD, TOK).T
    key[...] = pair_sum(192 + HD, HD).T
    value[...] = pair_sum(192 + 2 * HD, HD).T
    for j in range(PEERS):
        rows = arrived[j, 384:456, :].astype(f32)
        for g in range(9):
            target = out.at[:, g * 128 : (g + 1) * 128] if g < 8 else sums
            target[j * 8 : (j + 1) * 8, :] = rows[g * 8 : (g + 1) * 8, :]
    for one in outs[1:5]:
        one.start()
    turned = sums[...].T
    router[...] = turned[0:EXPERTS, :]
    rest[1:2, :] = turned[EXPERTS : EXPERTS + 1, :]
    weighted = sum(
        jnp.sum(total[...] * own.get()[...].astype(f32), axis=-1, keepdims=True)
        for total, own in zip((query, key, value), ins[4:7])
    )
    weighted = jnp.concatenate([weighted, jnp.zeros((TOK, 127), f32)], axis=1).T
    rest[0:1, :] = weighted[0:1, :] / ins[7].get()[...].astype(f32)
    wait_all(copies)
    back = (
        mm(dq, wide[:, 0:1024], NT)
        + mm(dk, wide[:, 1024:1536], NT)
        + mm(dv, wide[:, 1536:2048], NT)
    )
    x = states.get()[...].astype(f32)
    gain = small.get()[2 * EXTRA : 3 * EXTRA, :].astype(f32)[0:1, :]
    r = lax.rsqrt(jnp.mean(x * x, axis=-1, keepdims=True) + eps)
    scaled = back * gain
    dot = jnp.mean(scaled * x, axis=-1, keepdims=True)
    grad[...] = hidden_grad.get()[...] + r * scaled - x * (r * r * r * dot)


def per_device(
    inputs,
    segments,
    routes,
    gain_attn,
    w_query,
    w_key,
    w_value,
    w_out,
    gain_ffn,
    w_router,
    expert_gate,
    expert_up,
    expert_down,
    cotangent,
):
    place = lax.axis_index("expert")
    row = lax.axis_index("dp")
    info = jnp.stack([place // SIDE, place % SIDE, row // 2, row % 2]).astype(jnp.int32)
    states = inputs[0]
    cot = cotangent[0]
    my_routes = routes[0].T

    segment_row = segments[0][None, :]
    index = jnp.arange(SEQ, dtype=jnp.int32)[None, :]
    start = jnp.zeros((1, SEQ), jnp.int32)
    for s in range(3):
        count = jnp.sum((segment_row == s).astype(jnp.int32))
        start = start + jnp.where(segment_row > s, count, 0)
    freqs = theta ** (-jnp.arange(0, HD, 2, dtype=f32) / HD)
    angles = freqs[:, None] * (index - start).astype(f32)
    cosine, sine = jnp.cos(angles), jnp.sin(angles)
    my_angles = lax.dynamic_slice_in_dim(angles, place * TOK, TOK, 1)
    my_cosine, my_sine = jnp.cos(my_angles), jnp.sin(my_angles)

    packed = run(
        pack_kernel,
        "pack",
        (info,),
        (expert_gate, expert_up, expert_down),
        (shape((768, HALF), bf16),),
        (pltpu.SemaphoreType.DMA((8,)),),
    )[0]
    dense, cots = run(
        dense_kernel,
        "dense",
        (info, w_router.T, Near(gain_attn[None, :]), Near(gain_ffn[None, :]), Near(my_routes)),
        (w_query, w_key, w_value, cot, states),
        (shape((TOK + EXTRA, 2048), bf16), shape((ROW_STEP, D), bf16)),
        (pltpu.SemaphoreType.DMA((5,)),),
    )
    cots = lax.all_gather(cots, "expert", axis=0, tiled=True)
    dense = gather_dp(dense, packed, cosine, sine, my_cosine, my_sine)

    small, heads = run(
        qkv_kernel,
        "qkv",
        (info, states, Near(my_cosine), Near(my_sine)),
        dense,
        (
            shape((3 * EXTRA, D), bf16),
            shape((HEADS, 3 * HD, TOK), bf16),
        ),
        (pltpu.VMEM((D, 2048), bf16), pltpu.SemaphoreType.DMA((32,))),
        cost=25,
    )
    heads = swap_all(heads)

    packed = lax.all_gather(tied(packed, small), "dp", axis=0)
    outward = gather_dp(tied(w_out, small))

    out_t, lse, mixed_send = run(
        attend_kernel,
        "attend",
        (info, Near(heads), Near(start)),
        (),
        (
            shape((HD, SEQ), f32),
            shape((1, SEQ), f32),
            shape((HEADS, HD, TOK), bf16),
        ),
        (
            pltpu.VMEM((128, SEQ), bf16),
            pltpu.VMEM((128, SEQ), bf16),
            pltpu.VMEM((SEQ, 128), bf16),
        ),
        cost=30,
    )
    mixed_t = swap_all(mixed_send).reshape(HEADS * HD, TOK)

    hidden, send, table = run(
        project_kernel,
        "project",
        (info, Near(mixed_t), states, small, my_routes),
        outward,
        (shape((TOK, D), f32), shape((2 * ROWS, D), bf16), shape((2 * ROWS, TOK), bf16)),
        (pltpu.VMEM((D, D), bf16), pltpu.SemaphoreType.DMA((8,))),
        cost=25,
    )
    arrived = swap_all(send)

    grad_rows, slots = run(
        rows_kernel,
        "grad_rows",
        (info,),
        (cots,),
        (shape((2, ROWS, D), bf16), shape((PEERS, 2 * CAP, TOK), bf16)),
        (
            pltpu.VMEM((PEERS, TOK + EXTRA, D), bf16),
            pltpu.VMEM((2 * PEERS, TOK), f32),
            pltpu.VMEM((2, ROWS, D), f32),
            pltpu.SemaphoreType.DMA((PEERS,)),
        ),
        limit=32,
    )
    sent_grad, xs, acted, dgate, dup, gates, lgs = run(
        expert_kernel,
        "experts",
        (info, Near(arrived), grad_rows, small),
        (packed,),
        (
            shape((2 * ROWS, D), bf16),
            shape((2, ROWS, D), bf16),
            shape((2, ROWS, EF), bf16),
            shape((2, ROWS, EF), bf16),
            shape((2, ROWS, EF), bf16),
            shape((2, ROWS, 128), f32),
            shape((2, ROWS, 128), bf16),
        ),
        (
            pltpu.VMEM((2, ROWS, D), f32),
            pltpu.VMEM((2, D, EF), bf16),
            pltpu.VMEM((2, D, EF), bf16),
            pltpu.VMEM((2, EF, D), bf16),
            pltpu.SemaphoreType.DMA((64,)),
        ),
        limit=40,
        cost=60,
    )
    back = swap_all(sent_grad)

    routed, *expert_grads, router_grad = run(
        weights_kernel,
        "weights",
        (info, xs, grad_rows, acted, dgate, dup, gates, lgs, slots),
        (packed,),
        (
            shape((SEQ, D), bf16),
            *(shape((2, 384, 512), bf16),) * 8,
            shape((128, D), f32),
        ),
        (
            pltpu.VMEM((2, ROWS, D), f32),
            pltpu.VMEM((2, EF, D), bf16),
            pltpu.VMEM((2, D, EF), bf16),
            pltpu.VMEM((EF, D), bf16),
            pltpu.SemaphoreType.DMA((32,)),
        ),
        limit=40,
    )
    expert_pairs = pair_up(info, expert_grads[0:4], expert_grads[4:8], "expert_pairs")
    expert_far = send_pairs(expert_pairs)

    normed = run(
        norm_kernel,
        "normed",
        (info, small),
        (cots,),
        (shape((SEQ, D), bf16),),
        (pltpu.VMEM((PEERS, TOK, D), bf16), pltpu.SemaphoreType.DMA((PEERS,))),
        after=(sent_grad,),
    )[0]

    hidden_grad, low, grad_send, gain_grad = run(
        hidden_kernel,
        "hidden_grad",
        (info, Near(back), table, hidden, cot, small),
        outward,
        (
            shape((TOK, D), f32),
            shape((TOK, D), bf16),
            shape((HEADS, HD, TOK), bf16),
            shape((1, D), f32),
        ),
        (pltpu.VMEM((D, D), bf16), pltpu.SemaphoreType.DMA((8,))),
        after=(router_grad, normed, *expert_pairs),
        cost=20,
    )
    mixed_grad = swap_all(grad_send)

    out_grads = run(
        out_weights_kernel,
        "out_weights",
        (info, Near(mixed_t), low, router_grad, gain_grad),
        (),
        (shape((TOK, PACK), bf16),) * 8,
        (pltpu.VMEM((D, 128), f32),),
    )
    out_pairs = pair_up(info, out_grads[0:4], out_grads[4:8], "out_pairs")

    routed = lax.psum_scatter(tied(routed, low), "expert", scatter_dimension=0, tiled=True)
    output = (hidden + routed.astype(f32)).astype(bf16)

    grads_send, *w_grads = run(
        attend_back_kernel,
        "attend_back",
        (info, heads, out_t, lse, Near(mixed_grad), cosine, sine, start, normed),
        (),
        (
            shape((PEERS, 192, TOK), bf16),
            *(shape((192, TOK), bf16),) * 8,
        ),
        (
            pltpu.VMEM((128, SEQ), bf16),
            pltpu.VMEM((128, SEQ), bf16),
            pltpu.VMEM((SEQ, 128), bf16),
            pltpu.VMEM((128, SEQ), bf16),
            pltpu.VMEM((SEQ, 128), bf16),
            pltpu.VMEM((HD, SEQ), f32),
            pltpu.VMEM((192, SEQ), bf16),
            pltpu.VMEM((1, SEQ), f32),
            pltpu.VMEM((DP, 192, TOK), bf16),
        ),
        limit=32,
        after=out_pairs,
        cost=60,
    )
    w_pairs = [
        (mine.astype(f32) + core_swap(other).astype(f32)).astype(bf16)
        for mine, other in zip(w_grads[0:4], w_grads[4:8])
    ]
    w_sums = add_parts(w_pairs[0], send_pairs(w_pairs)).astype(bf16)
    expert_sums = add_parts(expert_pairs[0], expert_far)
    out_sums = add_parts(out_pairs[0], send_pairs(out_pairs)).astype(bf16)
    out_sums = swap_all(out_sums).reshape(PEERS, 8, PACK)
    out_sums = jnp.sum(out_sums.astype(f32), axis=0).astype(bf16)
    out_sums = jnp.concatenate([out_sums[:, g * 128 : (g + 1) * 128] for g in range(9)], axis=0)

    ends = jnp.concatenate([w_sums, out_sums], axis=0)
    last = jnp.concatenate(
        [grads_send, jnp.broadcast_to(ends[None], (PEERS, 264, TOK))], axis=1
    )
    last = swap_all(last)

    grad_input, sum_query, sum_key, sum_value, sum_out, sum_router, sum_gains = run(
        input_kernel,
        "grad_input",
        (info, Near(last), hidden_grad, states, small, w_query, w_key, w_value, gain_attn[None, :]),
        dense,
        (
            shape((TOK, D), f32),
            shape((TOK, 1024), f32),
            shape((TOK, 512), f32),
            shape((TOK, 512), f32),
            shape((TOK, D), f32),
            Near(shape((EXPERTS, TOK), f32)),
            Near(shape((2, TOK), f32)),
        ),
        (
            pltpu.VMEM((D, 2048), bf16),
            pltpu.VMEM((TOK, 128), f32),
            pltpu.SemaphoreType.DMA((8,)),
        ),
        limit=32,
        after=(output,),
        cost=35,
    )
    return (
        output[None],
        grad_input[None],
        sum_gains[0],
        sum_query,
        sum_key,
        sum_value,
        sum_out,
        sum_gains[1],
        sum_router.T,
        expert_sums[:, 0:128],
        expert_sums[:, 128:256],
        jnp.concatenate([expert_sums[:, 256:320], expert_sums[:, 320:384]], axis=2),
    )


def solution(mesh):
    placed = (
        P("dp", "expert", None),
        P("dp", None),
        P("dp", "expert", None),
        P("dp"),
        P("dp", None),
        P("dp", None),
        P("dp", None),
        P("dp", None),
        P("dp"),
        P("dp", None),
        P("expert", "dp", None),
        P("expert", "dp", None),
        P("expert", "dp", None),
        P("dp", "expert", None),
    )
    return jax.shard_map(
        per_device,
        mesh=mesh,
        in_specs=placed,
        out_specs=(
            P("dp", "expert", None),
            P("dp", "expert", None),
            P("dp"),
            P("dp", None),
            P("dp", None),
            P("dp", None),
            P("dp", None),
            P("dp"),
            P("dp", None),
            P("expert", "dp", None),
            P("expert", "dp", None),
            P("expert", "dp", None),
        ),
        check_vma=False,
    )
```

```python
import jax
import jax.numpy as jnp
from jax import lax
from jax.experimental import pallas as pl
from jax.experimental.pallas import tpu as pltpu
from jax.sharding import PartitionSpec as P

D = 1024
HEADS = 16
HD = 64
EF = 512
EXPERTS = 32
CAP = 40
TOK = 128
SEQ = 2048
SIDE = 4
PEERS = 16
DP = 8
QB = 512
HALF = 512
ROWS = PEERS * CAP
EXTRA = 16
PACK = 1152
ROW_STEP = 2 * TOK + EXTRA

eps = 1e-06
theta = 10000.0
masked = -1000000000.0
bf16 = jnp.bfloat16
f32 = jnp.float32
MIB = 1 << 20

NN = (((1,), (0,)), ((), ()))
NT = (((1,), (1,)), ((), ()))
TN = (((0,), (0,)), ((), ()))


def mm(left, right, dims=NN):
    return lax.dot_general(left, right, dims, preferred_element_type=f32)


def shape(dims, dtype):
    return jax.ShapeDtypeStruct(dims, dtype)


def cuts(dims, dtype):
    if dims[0] == 2 and len(dims) == 3:
        return 2
    size = jnp.dtype(dtype).itemsize
    for dim in dims:
        size *= dim
    step = 16 if len(dims) == 2 else 1
    for count in (8, 4, 2):
        if dims[0] % (count * step) == 0 and size // count >= MIB // 4:
            return count
    return 1


class Moved:
    def __init__(self, source, target, sems, first, dims, dtype):
        count = cuts(dims, dtype)
        rows = dims[0] // count
        self.copies = [
            pltpu.make_async_copy(
                source.at[pl.ds(k * rows, rows)], target.at[pl.ds(k * rows, rows)], sems.at[first + k]
            )
            for k in range(count)
        ]
        self.started = False
        self.waited = False

    def start(self):
        self.started = True
        for copy in self.copies:
            copy.start()

    def wait(self):
        if not self.waited:
            self.waited = True
            for copy in self.copies:
                copy.wait()


class In(Moved):
    def __init__(self, source, target, *rest):
        super().__init__(source, target, *rest)
        self.target = target

    def get(self):
        self.wait()
        return self.target

    def get_part(self, k):
        self.copies[k].wait()
        self.waited = k == len(self.copies) - 1
        return self.target


class Out(Moved):
    def __init__(self, source, target, *rest):
        super().__init__(source, target, *rest)
        self.ref = source

    def start_part(self, k):
        self.started = True
        self.copies[k].start()


class Near:
    def __init__(self, array):
        self.array = array


class Held:
    def __init__(self, ref):
        self.ref = ref

    def get(self):
        return self.ref

    def start(self):
        pass


def tied(value, *others):
    return lax.optimization_barrier((value, *others))[0]


def run(body, name, ins, raws, outs, scratch=(), limit=24, after=(), cost=0):
    info, arrays = ins[0], ins[1:]
    in_near = [isinstance(v, Near) for v in arrays]
    out_near = [isinstance(v, Near) for v in outs]
    arrays = [v.array if isinstance(v, Near) else v for v in arrays]
    outs = [v.array if isinstance(v, Near) else v for v in outs]
    both = list(zip((*arrays, *outs), (*in_near, *out_near)))
    count = sum(cuts(v.shape, v.dtype) for v, near in both if not near)
    held = [pltpu.VMEM(v.shape, v.dtype) for v, near in both if not near]

    def kernel(*refs):
        info_ref, refs = refs[0], refs[1:]
        in_refs, refs = refs[: len(arrays)], refs[len(arrays) :]
        raw_refs, refs = refs[: len(raws)], refs[len(raws) :]
        out_refs, refs = refs[: len(outs)], refs[len(outs) :]
        spaces, refs = list(refs[: len(held)]), refs[len(held) :]
        sems, rest = refs[0], refs[1:]
        first = 0
        fetched, sent = [], []
        for v, near, ref in zip(arrays, in_near, in_refs):
            if near:
                fetched.append(Held(ref))
                continue
            fetched.append(In(ref, spaces.pop(0), sems, first, v.shape, v.dtype))
            first += cuts(v.shape, v.dtype)
        for v, near, ref in zip(outs, out_near, out_refs):
            if near:
                sent.append(Held(ref))
                continue
            sent.append(Out(spaces.pop(0), ref, sems, first, v.shape, v.dtype))
            first += cuts(v.shape, v.dtype)
        for one in fetched:
            one.start()
        body(info_ref, fetched, raw_refs, sent, rest)
        for one in fetched:
            one.get()
        moves = [one for one in sent if isinstance(one, Out)]
        for one in moves:
            if not one.started:
                one.start()
        for one in moves:
            one.wait()

    if after:
        info = tied(info, *after)

    def pinned(v, near=False):
        return v if near else pltpu.with_memory_space_constraint(v, pltpu.HBM)

    def spec(near=False):
        return pl.BlockSpec(memory_space=pltpu.VMEM if near else pltpu.HBM)

    return pl.pallas_call(
        kernel,
        name=name,
        out_shape=tuple(
            shape(v.shape, v.dtype) if near else pltpu.HBM(v.shape, v.dtype)
            for v, near in zip(outs, out_near)
        ),
        in_specs=[pl.BlockSpec(memory_space=pltpu.SMEM)]
        + [spec(near) for near in in_near]
        + [spec()] * len(raws),
        out_specs=tuple(spec(near) for near in out_near),
        scratch_shapes=[*held, pltpu.SemaphoreType.DMA((max(count, 1),)), *scratch],
        compiler_params=pltpu.CompilerParams(vmem_limit_bytes=limit * MIB),
        cost_estimate=pl.CostEstimate(
            flops=1000 + cost * 10**9, bytes_accessed=1000, transcendentals=0
        ),
    )(info, *[pinned(v, near) for v, near in zip(arrays, in_near)], *[pinned(v) for v in raws])


def expert_from(values, dz, dx):
    pairs = [
        (z * SIDE + x, ((z - dz) % SIDE) * SIDE + (x - dx) % SIDE)
        for z in range(SIDE)
        for x in range(SIDE)
    ]
    return lax.ppermute(values, "expert", pairs)


def dp_from(values, dy):
    pairs = [(y * 2 + c, ((y - dy) % SIDE) * 2 + c) for y in range(SIDE) for c in range(2)]
    return lax.ppermute(values, "dp", pairs)


def core_swap(values):
    return lax.ppermute(values, "dp", [(d, d ^ 1) for d in range(DP)])


def gather_ring(values, step, *others):
    near = {m: step(values, m) for m in (1, 3)}
    far = step(tied(values, *others) if others else values, 2)
    return [values, near[1], far, near[3]]


def along_z(values, m):
    return expert_from(values, m, 0)


def along_x(values, m):
    return expert_from(values, 0, m)


def gather_dp(values, *others):
    far = {m: dp_from(values, m) for m in (1, 3, 2)}
    if others:
        far[2] = tied(far[2], *others)
    mine = [values, far[1], far[2], far[3]]
    return mine + [core_swap(part) for part in mine]


def send_pairs(pairs):
    return [dp_from(pairs[m], SIDE - m) for m in (1, 3, 2)]


def add_parts(first, others):
    total = first.astype(f32)
    for other in others:
        total = total + other.astype(f32)
    return total


def pair_kernel(info, ins, parts, outs, scratch):
    for m in range(SIDE):
        mine, other = ins[m].get()[...], ins[SIDE + m].get()[...]
        outs[m].ref[...] = (mine.astype(f32) + other.astype(f32)).astype(bf16)
        outs[m].start()


def pair_up(info, mine, other, name):
    swapped = [core_swap(part) for part in other]
    part = shape(mine[0].shape, bf16)
    return run(pair_kernel, name, (info, *mine, *swapped), (), (part,) * SIDE)


def swap_all(values):
    return lax.all_to_all(values, "expert", split_axis=0, concat_axis=0, tiled=True)


def part_place(info, r):
    return ((info[2] + r % SIDE) % SIDE) * 2 + (info[3] ^ (r // SIDE))


def aligned(index, step):
    return pl.ds(pl.multiple_of(index * step, step), step)


def rotated(values, c, s):
    w1, w2 = values[: HD // 2], values[HD // 2 :]
    return jnp.concatenate([w1 * c - w2 * s, w2 * c + w1 * s], axis=0)


def rotated_back(values, c, s):
    w1, w2 = values[: HD // 2], values[HD // 2 :]
    return jnp.concatenate([w1 * c + w2 * s, w2 * c - w1 * s], axis=0)


def allowed(ki, qi, start):
    key = ki * QB + lax.broadcasted_iota(jnp.int32, (QB, QB), 0)
    keep = key >= start
    if ki == qi:
        keep = keep & (key <= qi * QB + lax.broadcasted_iota(jnp.int32, (QB, QB), 1))
    return keep


def place_parts(info, parts, pieces, sems, place=part_place):
    copies = []
    for r in range(8):
        for k, piece in enumerate(pieces):
            source, target = piece(parts[r], place(info, r))
            copies.append(pltpu.make_async_copy(source, target, sems.at[r * len(pieces) + k]))
    for copy in copies:
        copy.start()
    return copies


def wait_all(copies):
    for copy in copies:
        copy.wait()


def dense_kernel(info, ins, parts, outs, scratch):
    router, names = ins
    query, key, value, cot, states = parts
    dense, cots = [out.ref for out in outs]
    sems = scratch[0]
    copies = [
        pltpu.make_async_copy(source, target, sems.at[k])
        for k, (source, target) in enumerate(
            (
                (query, dense.at[pl.ds(0, TOK), pl.ds(0, 1024)]),
                (key, dense.at[pl.ds(0, TOK), pl.ds(1024, 512)]),
                (value, dense.at[pl.ds(0, TOK), pl.ds(1536, 512)]),
                (cot, cots.at[pl.ds(0, TOK), :]),
                (states, cots.at[pl.ds(TOK + EXTRA, TOK), :]),
            )
        )
    ]
    for copy in copies:
        copy.start()
    rows = slice(TOK, TOK + EXTRA)
    dense[rows, 384:2048] = jnp.zeros((EXTRA, 2048 - 384), bf16)
    dense[rows, 0:128] = router.get()[0:EXTRA, :]
    dense[rows, 128:256] = router.get()[EXTRA : 2 * EXTRA, :]
    dense[rows, 256:384] = names.get()[EXTRA : 2 * EXTRA, :].astype(bf16)
    cots[rows, TOK:D] = jnp.zeros((EXTRA, D - TOK), bf16)
    cots[rows, 0:TOK] = names.get()[0:EXTRA, :].astype(bf16)
    wait_all(copies)


def pack_kernel(info, ins, parts, outs, scratch):
    gate, up, down = parts
    packed = outs[0].ref
    sems = scratch[0]
    pairs = []
    for i in range(2):
        for k, source in enumerate(
            (
                gate.at[i],
                up.at[i],
                down.at[i, :, pl.ds(0, HALF)],
                down.at[i, :, pl.ds(HALF, HALF)],
            )
        ):
            row, count = i * 384 + (0, 128, 256, 320)[k], (128, 128, 64, 64)[k]
            pairs.append((source, packed.at[pl.ds(row, count), :]))
    copies = [
        pltpu.make_async_copy(source, target, sems.at[k])
        for k, (source, target) in enumerate(pairs)
    ]
    for copy in copies:
        copy.start()
    wait_all(copies)


def qkv_kernel(info, ins, parts, outs, scratch):
    states, cos, sin = ins
    small, send = outs
    wide, sems = scratch
    copies = place_parts(
        info,
        parts,
        [
            lambda part, d: (part.at[pl.ds(0, TOK), :], wide.at[aligned(d, TOK), :]),
            *(
                lambda part, d, k=k: (
                    part.at[pl.ds(TOK, EXTRA), pl.ds(128 * k, 128)],
                    small.ref.at[pl.ds(EXTRA * k, EXTRA), aligned(d, TOK)],
                )
                for k in range(3)
            ),
        ],
        sems,
    )
    x = states.get()[...].astype(f32)
    r = lax.rsqrt(jnp.mean(x * x, axis=-1, keepdims=True) + eps)
    cos, sin = cos.get()[...], sin.get()[...]
    wait_all(copies)
    small.start()
    gain = small.ref[2 * EXTRA : 3 * EXTRA, :].astype(f32)[0:1, :]
    low = (x * r * gain).astype(bf16)
    turned = mm(low, wide[:, 1024:2048]).T
    for g in range(HEADS // 2):
        key = rotated(turned[g * HD : (g + 1) * HD], cos, sin)
        value = turned[512 + g * HD : 512 + (g + 1) * HD]
        both = jnp.concatenate([key, value], axis=0).astype(bf16)
        send.ref[2 * g, HD : 3 * HD, :] = both
        send.ref[2 * g + 1, HD : 3 * HD, :] = both
    turned = mm(low, wide[:, 0:1024]).T
    for h in range(HEADS):
        query = rotated(turned[h * HD : (h + 1) * HD], cos, sin).astype(bf16).astype(f32)
        send.ref[h, 0:HD, :] = (query * (HD**-0.5)).astype(bf16)


def spread_heads(arrived, qz, kvt, kvn):
    for i in range(SEQ // QB):
        span = slice(i * QB, (i + 1) * QB)
        got = jnp.concatenate([arrived[i * 4 + j] for j in range(4)], axis=1)
        qz[0:HD, span] = got[0:HD]
        qz[HD:128, span] = jnp.zeros((HD, QB), bf16)
        kvt[:, span] = got[HD : 3 * HD]
        kvn[span, :] = got[HD : 3 * HD].astype(f32).T.astype(bf16)


def attend_kernel(info, ins, parts, outs, scratch):
    start = ins[1].get()
    out_t, lse, send = outs
    qz, kvt, kvn = scratch
    spread_heads(ins[0].get(), qz, kvt, kvn)
    for qi in range(SEQ // QB):
        span = slice(qi * QB, (qi + 1) * QB)
        query = qz[:, span]
        top = jnp.full((1, QB), -jnp.inf, f32)
        total = jnp.zeros((1, QB), f32)
        mixed = jnp.zeros((HD, QB), f32)
        for ki in range(qi, -1, -1):
            keys = slice(ki * QB, (ki + 1) * QB)
            scores = jnp.where(allowed(ki, qi, start[:, span]), mm(kvn[keys, :], query), masked)
            higher = jnp.maximum(top, jnp.max(scores, axis=0, keepdims=True))
            weights = jnp.exp(scores - higher)
            shrink = jnp.exp(top - higher)
            total = total * shrink + jnp.sum(weights, axis=0, keepdims=True)
            mixed = mixed * shrink + mm(kvt[HD:128, keys], weights.astype(bf16))
            top = higher
        mixed = mixed / total
        lse.ref[:, span] = top + jnp.log(total)
        out_t.ref[:, span] = mixed
        for j in range(QB // TOK):
            send.ref[qi * (QB // TOK) + j] = mixed[:, j * TOK : (j + 1) * TOK].astype(bf16)


def shards(gathered):
    return [gathered.at[d] for d in range(DP)]


def shard_place(info, r):
    return r


def w_out_pieces(target):
    return [lambda part, d: (part.at[:, :], target.at[aligned(d, TOK), :])]


def ranks(choose):
    order = lax.broadcasted_iota(jnp.int32, (TOK, TOK), 0)
    before = (order < lax.broadcasted_iota(jnp.int32, (TOK, TOK), 1)).astype(bf16)
    return mm(choose.astype(bf16), before).astype(jnp.int32)


def project_kernel(info, ins, parts, outs, scratch):
    mixed_t, states, small, routes = ins
    hidden, send, table = outs
    w_out, sems = scratch
    copies = place_parts(info, parts, w_out_pieces(w_out), sems)
    names = lax.broadcasted_iota(jnp.int32, (EXPERTS, TOK), 0)
    choose = jnp.zeros((EXPERTS, TOK), f32)
    routes = routes.get()
    for j in range(8):
        choose = choose + (names == routes[j : j + 1, :]).astype(f32)
    rank = jnp.where(choose > 0.0, ranks(choose), -1)
    slots = lax.broadcasted_iota(jnp.int32, (CAP, TOK), 0)
    for e in range(0, EXPERTS, 2):
        table.ref[e * CAP : (e + 2) * CAP, :] = jnp.concatenate(
            [(rank[e : e + 1] == slots).astype(f32), (rank[e + 1 : e + 2] == slots).astype(f32)],
            axis=0,
        ).astype(bf16)
    mixed = mixed_t.get()[...].astype(f32).T.astype(bf16)
    gain = small.get()[2 * EXTRA : 3 * EXTRA, :].astype(f32)[1:2, :]
    wait_all(copies)
    value = states.get()[...].astype(f32) + mm(mixed, w_out[...])
    hidden.ref[...] = value
    r = lax.rsqrt(jnp.mean(value * value, axis=-1, keepdims=True) + eps)
    ffn = (value * r * gain).astype(bf16)
    step = 2 * ROWS // len(send.copies)
    for k in range(len(send.copies)):
        rows = slice(k * step, (k + 1) * step)
        send.ref[rows, :] = mm(table.ref[rows, :], ffn).astype(bf16)
        send.start_part(k)


def rows_kernel(info, ins, parts, outs, scratch):
    grads, slots = outs
    cots, choose, sems = scratch
    first = (info[0] * SIDE + info[1]) * 2
    copies = [
        pltpu.make_async_copy(
            parts[0].at[pl.ds(t * ROW_STEP, TOK + EXTRA), :], cots.at[t], sems.at[t]
        )
        for t in range(PEERS)
    ]
    for copy in copies:
        copy.start()
    wait_all(copies)
    for t in range(PEERS):
        routes = cots[t, TOK : TOK + EXTRA, 0:TOK].astype(f32)[0:8, :].astype(jnp.int32)
        for i in range(2):
            named = (routes == first + i).astype(f32)
            choose[2 * t + i : 2 * t + i + 1, :] = jnp.sum(named, axis=0, keepdims=True)
    rank = jnp.where(choose[...] > 0.0, ranks(choose[...]), -1)
    order = lax.broadcasted_iota(jnp.int32, (CAP, TOK), 0)
    for t in range(0, PEERS, 2):
        rows = []
        for k in (t, t + 1):
            hot = jnp.concatenate(
                [(rank[2 * k + i : 2 * k + i + 1] == order).astype(f32) for i in range(2)], axis=0
            )
            slots.ref[k] = hot.astype(bf16)
            rows.append(mm(hot.astype(bf16), cots[k, 0:TOK, :]))
        for i in range(2):
            mine = jnp.concatenate([row[i * CAP : (i + 1) * CAP] for row in rows], axis=0)
            grads.ref[i, t * CAP : (t + 2) * CAP, :] = mine.astype(bf16)


def norm_kernel(info, ins, parts, outs, scratch):
    gain = ins[0].get()[2 * EXTRA : 3 * EXTRA, :].astype(f32)[0:1, :]
    normed = outs[0]
    rows, sems = scratch
    copies = [
        pltpu.make_async_copy(
            parts[0].at[pl.ds(t * ROW_STEP + TOK + EXTRA, TOK), :], rows.at[t], sems.at[t]
        )
        for t in range(PEERS)
    ]
    for copy in copies:
        copy.start()
    step = PEERS // len(normed.copies)
    for t in range(PEERS):
        copies[t].wait()
        x = rows[t].astype(f32)
        r = lax.rsqrt(jnp.mean(x * x, axis=-1, keepdims=True) + eps)
        normed.ref[t * TOK : (t + 1) * TOK, :] = (x * r * gain).astype(bf16)
        if t % step == step - 1:
            normed.start_part(t // step)


def unweave(source, target):
    for s in range(0, PEERS, 2):
        held = source.get_part(s // 2)
        rows = [held[(s + k) * 2 * CAP : (s + k + 1) * 2 * CAP, :].astype(f32) for k in range(2)]
        for i in range(2):
            mine = jnp.concatenate([row[i * CAP : (i + 1) * CAP] for row in rows], axis=0)
            target[i, s * CAP : (s + 2) * CAP, :] = mine.astype(bf16)


def weave(spread, sent):
    for s in range(PEERS):
        rows = slice(s * CAP, (s + 1) * CAP)
        sent.ref[s * 2 * CAP : (s + 1) * 2 * CAP, :] = jnp.concatenate(
            [spread[0, rows, :], spread[1, rows, :]], axis=0
        ).astype(bf16)
        if s % 2 == 1:
            sent.start_part(s // 2)


def expert_kernel(info, ins, parts, outs, scratch):
    arrived, grads, small = ins
    sent, xs, acted, dgate, dup, gates, lgs = [out.ref for out in outs]
    spread, wg, wu, wd, sems = scratch

    def piece(i, k):
        first, count, target, column = (
            (0, TOK, wg, 0),
            (128, TOK, wu, 0),
            (256, HD, wd, 0),
            (320, HD, wd, HALF),
        )[k]
        return lambda part, d: (
            part.at[pl.ds(i * 384 + first, count), :],
            target.at[i, aligned(d, count), pl.ds(column, HALF)],
        )

    copies = place_parts(
        info,
        shards(parts[0]),
        [piece(i, k) for i in range(2) for k in range(4)],
        sems,
        shard_place,
    )
    unweave(arrived, xs)
    outs[1].start()
    grads = grads.get()
    small = small.get()
    wait_all(copies)
    first = (info[0] * SIDE + info[1]) * 2
    chunk = ROWS // 2

    for n in range(4):
        i = n // 2
        rows = slice(n % 2 * chunk, (n % 2 + 1) * chunk)
        x = xs[i, rows, :]
        router = small[0 : 2 * EXTRA, :]
        logits = mm(x, router, NT)
        peak = jnp.max(logits, axis=-1, keepdims=True)
        chances = jnp.exp(logits - peak)
        chances = chances / jnp.sum(chances, axis=-1, keepdims=True)
        mine = (lax.broadcasted_iota(jnp.int32, (chunk, EXPERTS), 1) == first + i).astype(f32)
        gate = jnp.sum(chances * mine, axis=-1, keepdims=True)
        gate_pre = mm(x, wg[i])
        up_pre = mm(x, wu[i])
        sigmoid = 1.0 / (1.0 + jnp.exp(-gate_pre))
        silu = gate_pre * sigmoid
        act = (silu * up_pre).astype(bf16)
        acted[i, rows, :] = act
        back = mm(grads[i, rows, :], wd[i], NT)
        dot = jnp.sum(act.astype(f32) * back, axis=-1, keepdims=True)
        back = back * gate
        gate_grad = (back * up_pre * (sigmoid * (1.0 + gate_pre * (1.0 - sigmoid)))).astype(bf16)
        up_grad = (back * silu).astype(bf16)
        dgate[i, rows, :] = gate_grad
        dup[i, rows, :] = up_grad
        lg = (dot * gate * (mine - chances)).astype(bf16)
        lgs[i, rows, :] = jnp.concatenate([lg, jnp.zeros((chunk, 128 - EXPERTS), bf16)], axis=1)
        gates[i, rows, :] = jnp.broadcast_to(gate, (chunk, 128))
        spread[i, rows, :] = (
            mm(gate_grad, wg[i], NT) + mm(up_grad, wu[i], NT) + mm(lg, router)
        )
        if n % 2 == 1:
            for one in outs[2:]:
                one.start_part(i)
    weave(spread, outs[0])


def weights_kernel(info, ins, parts, outs, scratch):
    xs, gs, acted, dgate, dup, gates, lgs, slots = ins
    routed, router_grad = outs[0].ref, outs[9].ref
    mine, other = [out.ref for out in outs[1:5]], [out.ref for out in outs[5:9]]
    spread, wd, sums, down_sums, sems = scratch
    def piece(i, k):
        return lambda part, d: (
            part.at[pl.ds(i * 384 + 256 + HD * k, HD), :],
            wd.at[i, aligned(d, HD), pl.ds(k * HALF, HALF)],
        )

    copies = place_parts(
        info,
        shards(parts[0]),
        [piece(i, k) for i in range(2) for k in range(2)],
        sems,
        shard_place,
    )
    xs, gs, acted, dgate, dup, gates, lgs, slots = [one.get() for one in ins]
    wait_all(copies)
    router_grad[...] = jnp.zeros_like(router_grad)

    def step(i, carry):
        source = xs[i]
        gate = gates[i][:, 0:1]
        spread[i] = mm(acted[i], wd[i]) * gate
        slot_grad = (gs[i].astype(f32) * gate).astype(bf16)
        router_grad[...] += mm(lgs[i], source, TN)
        sums[0] = mm(source, dgate[i], TN).astype(bf16)
        sums[1] = mm(source, dup[i], TN).astype(bf16)
        down_sums[...] = mm(acted[i], slot_grad, TN).astype(bf16)
        for r in range(8):
            d = part_place(info, r)
            target = (*mine, *other)[r]
            target[i, 0:128, :] = sums[0, aligned(d, TOK), :]
            target[i, 128:256, :] = sums[1, aligned(d, TOK), :]
            target[i, 256:320, :] = down_sums[aligned(d, HD), 0:HALF]
            target[i, 320:384, :] = down_sums[aligned(d, HD), HALF:D]
        return carry

    lax.fori_loop(0, 2, step, 0)
    for one in (*outs[5:9], *outs[1:5]):
        one.start()
    for t in range(PEERS):
        span = slice(t * CAP, (t + 1) * CAP)
        rows = jnp.concatenate([spread[i, span, :] for i in range(2)], axis=0).astype(bf16)
        routed[t * TOK : (t + 1) * TOK, :] = mm(slots[t], rows, TN).astype(bf16)


def hidden_kernel(info, ins, parts, outs, scratch):
    arrived, table, hidden, cot, small = ins
    hidden_grad, low, send, gain_grad = outs
    w_out, sems = scratch
    copies = place_parts(info, parts, w_out_pieces(w_out), sems)
    step = 2 * ROWS // 8
    table = table.get()
    grad = jnp.zeros((TOK, D), f32)
    for k in range(8):
        rows = slice(k * step, (k + 1) * step)
        grad = grad + mm(table[rows, :], arrived.get_part(k)[rows, :], TN)
    hidden = hidden.get()[...]
    gain = small.get()[2 * EXTRA : 3 * EXTRA, :].astype(f32)[1:2, :]
    r = lax.rsqrt(jnp.mean(hidden * hidden, axis=-1, keepdims=True) + eps)
    scaled = grad * gain
    dot = jnp.mean(scaled * hidden, axis=-1, keepdims=True)
    total = cot.get()[...].astype(f32) + r * scaled - hidden * (r * r * r * dot)
    gain_grad.ref[...] = jnp.sum(grad * hidden * r, axis=0, keepdims=True)
    hidden_grad.ref[...] = total
    low.ref[...] = total.astype(bf16)
    wait_all(copies)
    turned = mm(w_out[...], low.ref[...], NT).astype(bf16)
    send.ref[...] = turned.reshape(HEADS, HD, TOK)


def out_weights_kernel(info, ins, parts, outs, scratch):
    mixed_t, low, router_grad, gain_grad = [one.get() for one in ins]
    extra = scratch[0]
    block = jnp.concatenate(
        [
            router_grad[0:EXPERTS, :],
            jnp.broadcast_to(gain_grad[...], (8, D)),
            jnp.zeros((128 - EXPERTS - 8, D), f32),
        ],
        axis=0,
    )
    extra[...] = block.T
    for r in (4, 5, 6, 7, 0, 1, 2, 3):
        rows = aligned(part_place(info, r), TOK)
        target = outs[r].ref
        target[:, 0:D] = mm(mixed_t[rows, :], low[...]).astype(bf16)
        target[:, D:PACK] = extra[rows, :].astype(bf16)
        outs[r].start()


def attend_back_kernel(info, ins, parts, outs, scratch):
    heads, out_t, lse, arrived, cos, sin, start = [one.get() for one in ins[0:7]]
    send = outs[0].ref
    qz, kvt, kvn, oz, qon, dq, low, delta, sums = scratch
    steps = SEQ // QB
    spread_heads(heads, qz, kvt, kvn)
    for i in range(steps):
        span = slice(i * QB, (i + 1) * QB)
        got = jnp.concatenate([arrived[i * 4 + j] for j in range(4)], axis=1)
        oz[0:HD, span] = jnp.zeros((HD, QB), bf16)
        oz[HD:128, span] = got
        wide = got.astype(f32)
        delta[:, span] = jnp.sum(wide * out_t[:, span], axis=0, keepdims=True)
        qon[span, :] = jnp.concatenate([qz[0:HD, span].astype(f32), wide], axis=0).T.astype(bf16)
        dq[:, span] = jnp.zeros((HD, QB), f32)
    for ki in range(steps):
        keys = slice(ki * QB, (ki + 1) * QB)
        value_sum = jnp.zeros((QB, 128), f32)
        key_sum = jnp.zeros((QB, 128), f32)
        for qi in range(ki, steps):
            span = slice(qi * QB, (qi + 1) * QB)
            scores = mm(kvn[keys, :], qz[:, span])
            expo = jnp.where(
                allowed(ki, qi, start[:, span]), jnp.exp(scores - lse[:, span]), 0.0
            )
            back = mm(kvn[keys, :], oz[:, span])
            score_grad = (expo * (back - delta[:, span])).astype(bf16)
            value_sum = value_sum + mm(expo.astype(bf16), qon[span, :])
            key_sum = key_sum + mm(score_grad, qon[span, :])
            dq[:, span] += mm(kvt[0:HD, keys], score_grad)
        lane = lax.broadcasted_iota(jnp.int32, (QB, 128), 1)
        turned = jnp.where(lane < HD, key_sum, value_sum).T
        low[HD : 2 * HD, keys] = rotated_back(turned[0:HD], cos[:, keys], sin[:, keys]).astype(bf16)
        low[2 * HD : 3 * HD, keys] = turned[HD:128].astype(bf16)
    for i in range(steps):
        span = slice(i * QB, (i + 1) * QB)
        low[0:HD, span] = rotated_back(
            dq[:, span] * (HD**-0.5), cos[:, span], sin[:, span]
        ).astype(bf16)
    for j in range(PEERS):
        send[j] = low[:, j * TOK : (j + 1) * TOK]
    outs[0].start()
    total = mm(low[...], ins[7].get()[...]).astype(bf16)
    for d in range(DP):
        sums[d] = total[:, d * TOK : (d + 1) * TOK]
    for r in (4, 5, 6, 7, 0, 1, 2, 3):
        outs[1 + r].ref[...] = sums[part_place(info, r)]
        outs[1 + r].start()


def input_kernel(info, ins, parts, outs, scratch):
    arrived, hidden_grad, states, small = ins[0:4]
    grad, query, key, value, out, router, rest = [one.ref for one in outs]
    wide, sums, sems = scratch
    copies = place_parts(
        info,
        parts,
        [lambda part, d: (part.at[pl.ds(0, TOK), :], wide.at[aligned(d, TOK), :])],
        sems,
    )
    arrived = arrived.get()

    def pair_sum(first, count):
        pairs = arrived[:, first : first + count, :].astype(f32).reshape(HEADS // 2, 2, count, TOK)
        return (pairs[:, 0] + pairs[:, 1]).reshape(HEADS // 2 * count, TOK)

    dq = arrived[:, 0:HD, :].astype(f32).reshape(HEADS * HD, TOK).T.astype(bf16)
    dk = pair_sum(HD, HD).T.astype(bf16)
    dv = pair_sum(2 * HD, HD).T.astype(bf16)
    query[...] = arrived[:, 192 : 192 + HD, :].astype(f32).reshape(HEADS * HD, TOK).T
    key[...] = pair_sum(192 + HD, HD).T
    value[...] = pair_sum(192 + 2 * HD, HD).T
    for j in range(PEERS):
        rows = arrived[j, 384:456, :].astype(f32)
        for g in range(9):
            target = out.at[:, g * 128 : (g + 1) * 128] if g < 8 else sums
            target[j * 8 : (j + 1) * 8, :] = rows[g * 8 : (g + 1) * 8, :]
    for one in outs[1:5]:
        one.start()
    turned = sums[...].T
    router[...] = turned[0:EXPERTS, :]
    rest[1:2, :] = turned[EXPERTS : EXPERTS + 1, :]
    weighted = sum(
        jnp.sum(total[...] * own.get()[...].astype(f32), axis=-1, keepdims=True)
        for total, own in zip((query, key, value), ins[4:7])
    )
    weighted = jnp.concatenate([weighted, jnp.zeros((TOK, 127), f32)], axis=1).T
    rest[0:1, :] = weighted[0:1, :] / ins[7].get()[...].astype(f32)
    wait_all(copies)
    back = (
        mm(dq, wide[:, 0:1024], NT)
        + mm(dk, wide[:, 1024:1536], NT)
        + mm(dv, wide[:, 1536:2048], NT)
    )
    x = states.get()[...].astype(f32)
    gain = small.get()[2 * EXTRA : 3 * EXTRA, :].astype(f32)[0:1, :]
    r = lax.rsqrt(jnp.mean(x * x, axis=-1, keepdims=True) + eps)
    scaled = back * gain
    dot = jnp.mean(scaled * x, axis=-1, keepdims=True)
    grad[...] = hidden_grad.get()[...] + r * scaled - x * (r * r * r * dot)


def per_device(
    inputs,
    segments,
    routes,
    gain_attn,
    w_query,
    w_key,
    w_value,
    w_out,
    gain_ffn,
    w_router,
    expert_gate,
    expert_up,
    expert_down,
    cotangent,
):
    place = lax.axis_index("expert")
    row = lax.axis_index("dp")
    info = jnp.stack([place // SIDE, place % SIDE, row // 2, row % 2]).astype(jnp.int32)
    states = inputs[0]
    cot = cotangent[0]
    my_routes = routes[0].T

    segment_row = segments[0][None, :]
    index = jnp.arange(SEQ, dtype=jnp.int32)[None, :]
    start = jnp.zeros((1, SEQ), jnp.int32)
    for s in range(3):
        count = jnp.sum((segment_row == s).astype(jnp.int32))
        start = start + jnp.where(segment_row > s, count, 0)
    freqs = theta ** (-jnp.arange(0, HD, 2, dtype=f32) / HD)
    angles = freqs[:, None] * (index - start).astype(f32)
    cosine, sine = jnp.cos(angles), jnp.sin(angles)
    my_angles = lax.dynamic_slice_in_dim(angles, place * TOK, TOK, 1)
    my_cosine, my_sine = jnp.cos(my_angles), jnp.sin(my_angles)

    packed = run(
        pack_kernel,
        "pack",
        (info,),
        (expert_gate, expert_up, expert_down),
        (shape((768, HALF), bf16),),
        (pltpu.SemaphoreType.DMA((8,)),),
    )[0]
    names = jnp.concatenate(
        [
            my_routes.astype(f32),
            jnp.zeros((EXTRA - 8, TOK), f32),
            gain_attn.astype(f32)[None, :],
            gain_ffn.astype(f32)[None, :],
            jnp.zeros((EXTRA - 2, TOK), f32),
        ],
        axis=0,
    )
    dense, cots = run(
        dense_kernel,
        "dense",
        (info, w_router.T, Near(names)),
        (w_query, w_key, w_value, cot, states),
        (shape((TOK + EXTRA, 2048), bf16), shape((ROW_STEP, D), bf16)),
        (pltpu.SemaphoreType.DMA((5,)),),
    )
    cots = lax.all_gather(cots, "expert", axis=0, tiled=True)
    dense = gather_dp(dense, packed, cosine, sine, my_cosine, my_sine)

    small, heads = run(
        qkv_kernel,
        "qkv",
        (info, states, Near(my_cosine), Near(my_sine)),
        dense,
        (
            shape((3 * EXTRA, D), bf16),
            shape((HEADS, 3 * HD, TOK), bf16),
        ),
        (pltpu.VMEM((D, 2048), bf16), pltpu.SemaphoreType.DMA((32,))),
        cost=5,
    )
    heads = swap_all(heads)

    packed = lax.all_gather(tied(packed, small), "dp", axis=0)
    outward = gather_dp(tied(w_out, small))

    out_t, lse, mixed_send = run(
        attend_kernel,
        "attend",
        (info, Near(heads), Near(start)),
        (),
        (
            shape((HD, SEQ), f32),
            shape((1, SEQ), f32),
            shape((HEADS, HD, TOK), bf16),
        ),
        (
            pltpu.VMEM((128, SEQ), bf16),
            pltpu.VMEM((128, SEQ), bf16),
            pltpu.VMEM((SEQ, 128), bf16),
        ),
        cost=6,
    )
    mixed_t = swap_all(mixed_send).reshape(HEADS * HD, TOK)

    hidden, send, table = run(
        project_kernel,
        "project",
        (info, Near(mixed_t), states, small, my_routes),
        outward,
        (shape((TOK, D), f32), shape((2 * ROWS, D), bf16), shape((2 * ROWS, TOK), bf16)),
        (pltpu.VMEM((D, D), bf16), pltpu.SemaphoreType.DMA((8,))),
        cost=5,
    )
    arrived = swap_all(send)

    grad_rows, slots = run(
        rows_kernel,
        "grad_rows",
        (info,),
        (cots,),
        (Near(shape((2, ROWS, D), bf16)), shape((PEERS, 2 * CAP, TOK), bf16)),
        (
            pltpu.VMEM((PEERS, TOK + EXTRA, D), bf16),
            pltpu.VMEM((2 * PEERS, TOK), f32),
            pltpu.SemaphoreType.DMA((PEERS,)),
        ),
        limit=32,
    )
    normed = run(
        norm_kernel,
        "normed",
        (info, small),
        (cots,),
        (shape((SEQ, D), bf16),),
        (pltpu.VMEM((PEERS, TOK, D), bf16), pltpu.SemaphoreType.DMA((PEERS,))),
        after=(table,),
    )[0]

    sent_grad, xs, acted, dgate, dup, gates, lgs = run(
        expert_kernel,
        "experts",
        (info, arrived, Near(grad_rows), small),
        (packed,),
        (
            shape((2 * ROWS, D), bf16),
            shape((2, ROWS, D), bf16),
            shape((2, ROWS, EF), bf16),
            shape((2, ROWS, EF), bf16),
            shape((2, ROWS, EF), bf16),
            shape((2, ROWS, 128), f32),
            shape((2, ROWS, 128), bf16),
        ),
        (
            pltpu.VMEM((2, ROWS, D), f32),
            pltpu.VMEM((2, D, EF), bf16),
            pltpu.VMEM((2, D, EF), bf16),
            pltpu.VMEM((2, EF, D), bf16),
            pltpu.SemaphoreType.DMA((64,)),
        ),
        limit=28,
        after=(normed,),
        cost=12,
    )
    back = swap_all(sent_grad)

    routed, *expert_grads, router_grad = run(
        weights_kernel,
        "weights",
        (info, xs, Near(grad_rows), acted, dgate, dup, gates, lgs, slots),
        (packed,),
        (
            shape((SEQ, D), bf16),
            *(shape((2, 384, 512), bf16),) * 8,
            shape((128, D), f32),
        ),
        (
            pltpu.VMEM((2, ROWS, D), f32),
            pltpu.VMEM((2, EF, D), bf16),
            pltpu.VMEM((2, D, EF), bf16),
            pltpu.VMEM((EF, D), bf16),
            pltpu.SemaphoreType.DMA((32,)),
        ),
        limit=40,
    )
    expert_pairs = pair_up(info, expert_grads[0:4], expert_grads[4:8], "expert_pairs")
    expert_near = [dp_from(expert_pairs[m], SIDE - m) for m in (1, 3)]

    hidden_grad, low, grad_send, gain_grad = run(
        hidden_kernel,
        "hidden_grad",
        (info, back, table, hidden, cot, small),
        outward,
        (
            shape((TOK, D), f32),
            shape((TOK, D), bf16),
            shape((HEADS, HD, TOK), bf16),
            shape((1, D), f32),
        ),
        (pltpu.VMEM((D, D), bf16), pltpu.SemaphoreType.DMA((8,))),
        after=(router_grad, *expert_pairs),
        cost=4,
    )
    mixed_grad = swap_all(grad_send)

    out_grads = run(
        out_weights_kernel,
        "out_weights",
        (info, Near(mixed_t), low, router_grad, gain_grad),
        (),
        (shape((TOK, PACK), bf16),) * 8,
        (pltpu.VMEM((D, 128), f32),),
    )
    out_pairs = pair_up(info, out_grads[0:4], out_grads[4:8], "out_pairs")

    routed = lax.psum_scatter(tied(routed, expert_pairs[0]), "expert", scatter_dimension=0, tiled=True)
    output = (hidden + routed.astype(f32)).astype(bf16)

    grads_send, *w_grads = run(
        attend_back_kernel,
        "attend_back",
        (info, heads, out_t, lse, Near(mixed_grad), cosine, sine, start, normed),
        (),
        (
            shape((PEERS, 192, TOK), bf16),
            *(shape((192, TOK), bf16),) * 8,
        ),
        (
            pltpu.VMEM((128, SEQ), bf16),
            pltpu.VMEM((128, SEQ), bf16),
            pltpu.VMEM((SEQ, 128), bf16),
            pltpu.VMEM((128, SEQ), bf16),
            pltpu.VMEM((SEQ, 128), bf16),
            pltpu.VMEM((HD, SEQ), f32),
            pltpu.VMEM((192, SEQ), bf16),
            pltpu.VMEM((1, SEQ), f32),
            pltpu.VMEM((DP, 192, TOK), bf16),
        ),
        limit=32,
        after=(*out_pairs, *expert_near),
        cost=12,
    )
    out_far = send_pairs(out_pairs)
    *w_grads, _, _, _ = lax.optimization_barrier((*w_grads, *out_far))
    w_pairs = [
        (mine.astype(f32) + core_swap(other).astype(f32)).astype(bf16)
        for mine, other in zip(w_grads[0:4], w_grads[4:8])
    ]
    w_sums = add_parts(w_pairs[0], send_pairs(w_pairs)).astype(bf16)
    expert_far = dp_from(tied(expert_pairs[2], w_sums), 2)
    expert_sums = add_parts(expert_pairs[0], (*expert_near, expert_far))
    out_sums = add_parts(out_pairs[0], out_far).astype(bf16)
    out_sums = swap_all(out_sums).reshape(PEERS, 8, PACK)
    out_sums = jnp.sum(out_sums.astype(f32), axis=0).astype(bf16)
    out_sums = jnp.concatenate([out_sums[:, g * 128 : (g + 1) * 128] for g in range(9)], axis=0)

    ends = jnp.concatenate([w_sums, out_sums], axis=0)
    last = jnp.concatenate(
        [grads_send, jnp.broadcast_to(ends[None], (PEERS, 264, TOK))], axis=1
    )
    last = swap_all(last)

    grad_input, sum_query, sum_key, sum_value, sum_out, sum_router, sum_gains = run(
        input_kernel,
        "grad_input",
        (info, Near(last), hidden_grad, states, small, w_query, w_key, w_value, gain_attn[None, :]),
        dense,
        (
            shape((TOK, D), f32),
            shape((TOK, 1024), f32),
            shape((TOK, 512), f32),
            shape((TOK, 512), f32),
            shape((TOK, D), f32),
            Near(shape((EXPERTS, TOK), f32)),
            Near(shape((2, TOK), f32)),
        ),
        (
            pltpu.VMEM((D, 2048), bf16),
            pltpu.VMEM((TOK, 128), f32),
            pltpu.SemaphoreType.DMA((8,)),
        ),
        limit=32,
        after=(output,),
        cost=7,
    )
    return (
        output[None],
        grad_input[None],
        sum_gains[0],
        sum_query,
        sum_key,
        sum_value,
        sum_out,
        sum_gains[1],
        sum_router.T,
        expert_sums[:, 0:128],
        expert_sums[:, 128:256],
        jnp.concatenate([expert_sums[:, 256:320], expert_sums[:, 320:384]], axis=2),
    )


def solution(mesh):
    placed = (
        P("dp", "expert", None),
        P("dp", None),
        P("dp", "expert", None),
        P("dp"),
        P("dp", None),
        P("dp", None),
        P("dp", None),
        P("dp", None),
        P("dp"),
        P("dp", None),
        P("expert", "dp", None),
        P("expert", "dp", None),
        P("expert", "dp", None),
        P("dp", "expert", None),
    )
    return jax.shard_map(
        per_device,
        mesh=mesh,
        in_specs=placed,
        out_specs=(
            P("dp", "expert", None),
            P("dp", "expert", None),
            P("dp"),
            P("dp", None),
            P("dp", None),
            P("dp", None),
            P("dp", None),
            P("dp"),
            P("dp", None),
            P("expert", "dp", None),
            P("expert", "dp", None),
            P("expert", "dp", None),
        ),
        check_vma=False,
    )
```

```python
import jax
import jax.numpy as jnp
from jax import lax
from jax.experimental import pallas as pl
from jax.experimental.pallas import tpu as pltpu
from jax.sharding import PartitionSpec as P

D = 1024
HEADS = 16
HD = 64
EF = 512
EXPERTS = 32
CAP = 40
TOK = 128
SEQ = 2048
SIDE = 4
PEERS = 16
DP = 8
QB = 512
HALF = 512
ROWS = PEERS * CAP
EXTRA = 16
PACK = 1152
ROW_STEP = 2 * TOK + EXTRA

HEAD_OF = [(e // 4 % 2) * 8 + e // 8 * 4 + e % 4 for e in range(PEERS)]
DEV_OF = [HEAD_OF.index(h) for h in range(HEADS)]
SAME_SIDE = [[e for e in range(PEERS) if e // 4 % 2 == p] for p in range(2)]

eps = 1e-06
theta = 10000.0
masked = -1000000000.0
bf16 = jnp.bfloat16
f32 = jnp.float32
MIB = 1 << 20

NN = (((1,), (0,)), ((), ()))
NT = (((1,), (1,)), ((), ()))
TN = (((0,), (0,)), ((), ()))


def mm(left, right, dims=NN):
    return lax.dot_general(left, right, dims, preferred_element_type=f32)


def shape(dims, dtype):
    return jax.ShapeDtypeStruct(dims, dtype)


def cuts(dims, dtype):
    if dims[0] == 2 and len(dims) == 3:
        return 2
    size = jnp.dtype(dtype).itemsize
    for dim in dims:
        size *= dim
    step = 16 if len(dims) == 2 else 1
    for count in (8, 4, 2):
        if dims[0] % (count * step) == 0 and size // count >= MIB // 4:
            return count
    return 1


class Moved:
    def __init__(self, source, target, sems, first, dims, dtype):
        count = cuts(dims, dtype)
        rows = dims[0] // count
        self.copies = [
            pltpu.make_async_copy(
                source.at[pl.ds(k * rows, rows)], target.at[pl.ds(k * rows, rows)], sems.at[first + k]
            )
            for k in range(count)
        ]
        self.started = False
        self.waited = False

    def start(self):
        self.started = True
        for copy in self.copies:
            copy.start()

    def wait(self):
        if not self.waited:
            self.waited = True
            for copy in self.copies:
                copy.wait()


class In(Moved):
    def __init__(self, source, target, *rest):
        super().__init__(source, target, *rest)
        self.target = target

    def get(self):
        self.wait()
        return self.target

    def get_part(self, k):
        self.copies[k].wait()
        self.waited = k == len(self.copies) - 1
        return self.target


class Out(Moved):
    def __init__(self, source, target, *rest):
        super().__init__(source, target, *rest)
        self.ref = source

    def start_part(self, k):
        self.started = True
        self.copies[k].start()


class Near:
    def __init__(self, array):
        self.array = array


class Held:
    def __init__(self, ref):
        self.ref = ref

    def get(self):
        return self.ref

    def start(self):
        pass


def tied(value, *others):
    return lax.optimization_barrier((value, *others))[0]


def run(body, name, ins, raws, outs, scratch=(), limit=24, after=(), cost=0):
    info, arrays = ins[0], ins[1:]
    in_near = [isinstance(v, Near) for v in arrays]
    out_near = [isinstance(v, Near) for v in outs]
    arrays = [v.array if isinstance(v, Near) else v for v in arrays]
    outs = [v.array if isinstance(v, Near) else v for v in outs]
    both = list(zip((*arrays, *outs), (*in_near, *out_near)))
    count = sum(cuts(v.shape, v.dtype) for v, near in both if not near)
    held = [pltpu.VMEM(v.shape, v.dtype) for v, near in both if not near]

    def kernel(*refs):
        info_ref, refs = refs[0], refs[1:]
        in_refs, refs = refs[: len(arrays)], refs[len(arrays) :]
        raw_refs, refs = refs[: len(raws)], refs[len(raws) :]
        out_refs, refs = refs[: len(outs)], refs[len(outs) :]
        spaces, refs = list(refs[: len(held)]), refs[len(held) :]
        sems, rest = refs[0], refs[1:]
        first = 0
        fetched, sent = [], []
        for v, near, ref in zip(arrays, in_near, in_refs):
            if near:
                fetched.append(Held(ref))
                continue
            fetched.append(In(ref, spaces.pop(0), sems, first, v.shape, v.dtype))
            first += cuts(v.shape, v.dtype)
        for v, near, ref in zip(outs, out_near, out_refs):
            if near:
                sent.append(Held(ref))
                continue
            sent.append(Out(spaces.pop(0), ref, sems, first, v.shape, v.dtype))
            first += cuts(v.shape, v.dtype)
        for one in fetched:
            one.start()
        body(info_ref, fetched, raw_refs, sent, rest)
        for one in fetched:
            one.get()
        moves = [one for one in sent if isinstance(one, Out)]
        for one in moves:
            if not one.started:
                one.start()
        for one in moves:
            one.wait()

    if after:
        info = tied(info, *after)

    def pinned(v, near=False):
        return v if near else pltpu.with_memory_space_constraint(v, pltpu.HBM)

    def spec(near=False):
        return pl.BlockSpec(memory_space=pltpu.VMEM if near else pltpu.HBM)

    return pl.pallas_call(
        kernel,
        name=name,
        out_shape=tuple(
            shape(v.shape, v.dtype) if near else pltpu.HBM(v.shape, v.dtype)
            for v, near in zip(outs, out_near)
        ),
        in_specs=[pl.BlockSpec(memory_space=pltpu.SMEM)]
        + [spec(near) for near in in_near]
        + [spec()] * len(raws),
        out_specs=tuple(spec(near) for near in out_near),
        scratch_shapes=[*held, pltpu.SemaphoreType.DMA((max(count, 1),)), *scratch],
        compiler_params=pltpu.CompilerParams(vmem_limit_bytes=limit * MIB),
        cost_estimate=pl.CostEstimate(
            flops=1000 + cost * 10**9, bytes_accessed=1000, transcendentals=0
        ),
    )(info, *[pinned(v, near) for v, near in zip(arrays, in_near)], *[pinned(v) for v in raws])


def expert_from(values, dz, dx):
    pairs = [
        (z * SIDE + x, ((z - dz) % SIDE) * SIDE + (x - dx) % SIDE)
        for z in range(SIDE)
        for x in range(SIDE)
    ]
    return lax.ppermute(values, "expert", pairs)


def dp_from(values, dy):
    pairs = [(y * 2 + c, ((y - dy) % SIDE) * 2 + c) for y in range(SIDE) for c in range(2)]
    return lax.ppermute(values, "dp", pairs)


def core_swap(values):
    return lax.ppermute(values, "dp", [(d, d ^ 1) for d in range(DP)])


def gather_ring(values, step, *others):
    near = {m: step(values, m) for m in (1, 3)}
    far = step(tied(values, *others) if others else values, 2)
    return [values, near[1], far, near[3]]


def along_z(values, m):
    return expert_from(values, m, 0)


def along_x(values, m):
    return expert_from(values, 0, m)


def gather_y(values):
    far = {m: dp_from(values, m) for m in (1, 3, 2)}
    return [values, far[1], far[2], far[3]]


def gather_dp(values, *others):
    mine = gather_y(values)
    if others:
        mine[2] = tied(mine[2], *others)
    return mine + [core_swap(part) for part in mine]


def send_pairs(pairs):
    return [dp_from(pairs[m], SIDE - m) for m in (1, 3, 2)]


def add_parts(first, others):
    total = first.astype(f32)
    for other in others:
        total = total + other.astype(f32)
    return total


def pair_kernel(info, ins, parts, outs, scratch):
    for m in range(SIDE):
        mine, other = ins[m].get()[...], ins[SIDE + m].get()[...]
        outs[m].ref[...] = (mine.astype(f32) + other.astype(f32)).astype(bf16)
        outs[m].start()


def pair_up(info, mine, other, name):
    swapped = [core_swap(part) for part in other]
    part = shape(mine[0].shape, bf16)
    return run(pair_kernel, name, (info, *mine, *swapped), (), (part,) * SIDE)


def swap_side(values):
    return lax.all_to_all(
        values, "expert", split_axis=0, concat_axis=0, tiled=True, axis_index_groups=SAME_SIDE
    )


def swap_all(values):
    return lax.all_to_all(values, "expert", split_axis=0, concat_axis=0, tiled=True)


def part_place(info, r):
    return ((info[2] + r % SIDE) % SIDE) * 2 + (info[3] ^ (r // SIDE))


def aligned(index, step):
    return pl.ds(pl.multiple_of(index * step, step), step)


def rotated(values, c, s):
    w1, w2 = values[: HD // 2], values[HD // 2 :]
    return jnp.concatenate([w1 * c - w2 * s, w2 * c + w1 * s], axis=0)


def rotated_back(values, c, s):
    w1, w2 = values[: HD // 2], values[HD // 2 :]
    return jnp.concatenate([w1 * c + w2 * s, w2 * c - w1 * s], axis=0)


def allowed(ki, qi, start):
    key = ki * QB + lax.broadcasted_iota(jnp.int32, (QB, QB), 0)
    keep = key >= start
    if ki == qi:
        keep = keep & (key <= qi * QB + lax.broadcasted_iota(jnp.int32, (QB, QB), 1))
    return keep


def place_parts(info, parts, pieces, sems, place=part_place):
    copies = []
    for r in range(8):
        for k, piece in enumerate(pieces):
            source, target = piece(parts[r], place(info, r))
            copies.append(pltpu.make_async_copy(source, target, sems.at[r * len(pieces) + k]))
    for copy in copies:
        copy.start()
    return copies


def wait_all(copies):
    for copy in copies:
        copy.wait()


def dense_kernel(info, ins, parts, outs, scratch):
    router, names = ins
    query, key, value, w_out, cot, states = parts
    dense, outward, cots = [out.ref for out in outs]
    sems = scratch[0]
    mine = info[0] % 2
    halves = []
    for target, first, side in ((dense, 0, mine), (outward, D, 1 - mine)):
        for source, width, column in ((query, 512, 0), (key, 256, 512), (value, 256, 768)):
            halves.append(
                (
                    source.at[:, aligned(side, width)],
                    target.at[pl.ds(0, TOK), pl.ds(first + column, width)],
                )
            )
    copies = [
        pltpu.make_async_copy(source, target, sems.at[k])
        for k, (source, target) in enumerate(
            (
                *halves,
                (w_out, outward.at[:, pl.ds(0, D)]),
                (cot, cots.at[pl.ds(0, TOK), :]),
                (states, cots.at[pl.ds(TOK + EXTRA, TOK), :]),
            )
        )
    ]
    for copy in copies:
        copy.start()
    rows = slice(TOK, TOK + EXTRA)
    dense[rows, 384:D] = jnp.zeros((EXTRA, D - 384), bf16)
    dense[rows, 0:128] = router.get()[0:EXTRA, :]
    dense[rows, 128:256] = router.get()[EXTRA : 2 * EXTRA, :]
    dense[rows, 256:384] = names.get()[EXTRA : 2 * EXTRA, :].astype(bf16)
    cots[rows, TOK:D] = jnp.zeros((EXTRA, D - TOK), bf16)
    cots[rows, 0:TOK] = names.get()[0:EXTRA, :].astype(bf16)
    wait_all(copies)


def pack_kernel(info, ins, parts, outs, scratch):
    gate, up, down = parts
    packed = outs[0].ref
    sems = scratch[0]
    pairs = []
    for i in range(2):
        for k, source in enumerate(
            (
                gate.at[i],
                up.at[i],
                down.at[i, :, pl.ds(0, HALF)],
                down.at[i, :, pl.ds(HALF, HALF)],
            )
        ):
            row, count = i * 384 + (0, 128, 256, 320)[k], (128, 128, 64, 64)[k]
            pairs.append((source, packed.at[pl.ds(row, count), :]))
    copies = [
        pltpu.make_async_copy(source, target, sems.at[k])
        for k, (source, target) in enumerate(pairs)
    ]
    for copy in copies:
        copy.start()
    wait_all(copies)


def qkv_kernel(info, ins, parts, outs, scratch):
    states, partner, cos, sin = ins
    small, send = outs
    wide, rows, sems = scratch
    copies = place_parts(
        info,
        parts,
        [
            lambda part, d: (part.at[pl.ds(0, TOK), :], wide.at[aligned(d, TOK), :]),
            *(
                lambda part, d, k=k: (
                    part.at[pl.ds(TOK, EXTRA), pl.ds(128 * k, 128)],
                    small.ref.at[pl.ds(EXTRA * k, EXTRA), aligned(d, TOK)],
                )
                for k in range(3)
            ),
        ],
        sems,
    )
    mine = info[0] % 2
    rows[mine] = states.get()[...].astype(f32)
    rows[1 - mine] = partner.get()[...].astype(f32)
    x = jnp.concatenate([rows[0], rows[1]], axis=0)
    r = lax.rsqrt(jnp.mean(x * x, axis=-1, keepdims=True) + eps)
    cos, sin = cos.get()[...], sin.get()[...]
    wait_all(copies)
    small.start()
    gain = small.ref[2 * EXTRA : 3 * EXTRA, :].astype(f32)[0:1, :]
    low = (x * r * gain).astype(bf16)
    turned = mm(low, wide[:, 512:1024]).T
    for g in range(4):
        key = rotated(turned[g * HD : (g + 1) * HD], cos, sin)
        value = turned[256 + g * HD : 256 + (g + 1) * HD]
        both = jnp.concatenate([key, value], axis=0).astype(bf16)
        for n in range(2):
            for j in range(2):
                send.ref[2 * g + n, j, HD : 3 * HD, :] = both[:, j * TOK : (j + 1) * TOK]
    turned = mm(low, wide[:, 0:512]).T
    for h in range(8):
        query = rotated(turned[h * HD : (h + 1) * HD], cos, sin).astype(bf16).astype(f32)
        query = (query * (HD**-0.5)).astype(bf16)
        for j in range(2):
            send.ref[h, j, 0:HD, :] = query[:, j * TOK : (j + 1) * TOK]


def spread_heads(arrived, qz, kvt, kvn):
    for i in range(SEQ // QB):
        span = slice(i * QB, (i + 1) * QB)
        got = jnp.concatenate([arrived[i // 2 * 4 + x, i % 2] for x in range(SIDE)], axis=1)
        qz[0:HD, span] = got[0:HD]
        qz[HD:128, span] = jnp.zeros((HD, QB), bf16)
        kvt[:, span] = got[HD : 3 * HD]
        kvn[span, :] = got[HD : 3 * HD].astype(f32).T.astype(bf16)


def attend_kernel(info, ins, parts, outs, scratch):
    start = ins[1].get()
    out_t, lse, send = outs
    qz, kvt, kvn = scratch
    spread_heads(ins[0].get(), qz, kvt, kvn)
    for qi in range(SEQ // QB):
        span = slice(qi * QB, (qi + 1) * QB)
        query = qz[:, span]
        top = jnp.full((1, QB), -jnp.inf, f32)
        total = jnp.zeros((1, QB), f32)
        mixed = jnp.zeros((HD, QB), f32)
        for ki in range(qi, -1, -1):
            keys = slice(ki * QB, (ki + 1) * QB)
            scores = jnp.where(allowed(ki, qi, start[:, span]), mm(kvn[keys, :], query), masked)
            higher = jnp.maximum(top, jnp.max(scores, axis=0, keepdims=True))
            weights = jnp.exp(scores - higher)
            shrink = jnp.exp(top - higher)
            total = total * shrink + jnp.sum(weights, axis=0, keepdims=True)
            mixed = mixed * shrink + mm(kvt[HD:128, keys], weights.astype(bf16))
            top = higher
        mixed = mixed / total
        lse.ref[:, span] = top + jnp.log(total)
        out_t.ref[:, span] = mixed
        for j in range(QB // TOK):
            send.ref[qi * (QB // TOK) + j] = mixed[:, j * TOK : (j + 1) * TOK].astype(bf16)


def shards(gathered):
    return [gathered.at[d] for d in range(DP)]


def shard_place(info, r):
    return r


def w_out_pieces(target):
    return [lambda part, d: (part.at[:, pl.ds(0, D)], target.at[aligned(d, TOK), :])]


def ranks(choose):
    order = lax.broadcasted_iota(jnp.int32, (TOK, TOK), 0)
    before = (order < lax.broadcasted_iota(jnp.int32, (TOK, TOK), 1)).astype(bf16)
    return mm(choose.astype(bf16), before).astype(jnp.int32)


def project_kernel(info, ins, parts, outs, scratch):
    mixed_t, states, small, routes = ins
    hidden, send, table, ordered = outs
    w_out, sems = scratch
    copies = place_parts(info, parts, w_out_pieces(w_out), sems)
    names = lax.broadcasted_iota(jnp.int32, (EXPERTS, TOK), 0)
    choose = jnp.zeros((EXPERTS, TOK), f32)
    routes = routes.get()
    for j in range(8):
        choose = choose + (names == routes[j : j + 1, :]).astype(f32)
    rank = jnp.where(choose > 0.0, ranks(choose), -1)
    slots = lax.broadcasted_iota(jnp.int32, (CAP, TOK), 0)
    for e in range(0, EXPERTS, 2):
        table.ref[e * CAP : (e + 2) * CAP, :] = jnp.concatenate(
            [(rank[e : e + 1] == slots).astype(f32), (rank[e + 1 : e + 2] == slots).astype(f32)],
            axis=0,
        ).astype(bf16)
    mixed_t = mixed_t.get()
    for h in range(HEADS):
        rows = slice(DEV_OF[h] * HD, (DEV_OF[h] + 1) * HD)
        ordered.ref[h * HD : (h + 1) * HD, :] = mixed_t[rows, :]
    ordered.start()
    mixed = ordered.ref[...].astype(f32).T.astype(bf16)
    gain = small.get()[2 * EXTRA : 3 * EXTRA, :].astype(f32)[1:2, :]
    wait_all(copies)
    value = states.get()[...].astype(f32) + mm(mixed, w_out[...])
    hidden.ref[...] = value
    r = lax.rsqrt(jnp.mean(value * value, axis=-1, keepdims=True) + eps)
    ffn = (value * r * gain).astype(bf16)
    step = 2 * ROWS // len(send.copies)
    for k in range(len(send.copies)):
        rows = slice(k * step, (k + 1) * step)
        send.ref[rows, :] = mm(table.ref[rows, :], ffn).astype(bf16)
        send.start_part(k)


def rows_kernel(info, ins, parts, outs, scratch):
    grads, slots = outs
    cots, choose, sems = scratch
    first = (info[0] * SIDE + info[1]) * 2
    copies = [
        pltpu.make_async_copy(
            parts[0].at[pl.ds(t * ROW_STEP, TOK + EXTRA), :], cots.at[t], sems.at[t]
        )
        for t in range(PEERS)
    ]
    for copy in copies:
        copy.start()
    wait_all(copies)
    for t in range(PEERS):
        routes = cots[t, TOK : TOK + EXTRA, 0:TOK].astype(f32)[0:8, :].astype(jnp.int32)
        for i in range(2):
            named = (routes == first + i).astype(f32)
            choose[2 * t + i : 2 * t + i + 1, :] = jnp.sum(named, axis=0, keepdims=True)
    rank = jnp.where(choose[...] > 0.0, ranks(choose[...]), -1)
    order = lax.broadcasted_iota(jnp.int32, (CAP, TOK), 0)
    for t in range(0, PEERS, 2):
        rows = []
        for k in (t, t + 1):
            hot = jnp.concatenate(
                [(rank[2 * k + i : 2 * k + i + 1] == order).astype(f32) for i in range(2)], axis=0
            )
            slots.ref[k] = hot.astype(bf16)
            rows.append(mm(hot.astype(bf16), cots[k, 0:TOK, :]))
        for i in range(2):
            mine = jnp.concatenate([row[i * CAP : (i + 1) * CAP] for row in rows], axis=0)
            grads.ref[i, t * CAP : (t + 2) * CAP, :] = mine.astype(bf16)


def norm_kernel(info, ins, parts, outs, scratch):
    gain = ins[0].get()[2 * EXTRA : 3 * EXTRA, :].astype(f32)[0:1, :]
    normed = outs[0]
    rows, sems = scratch
    copies = [
        pltpu.make_async_copy(
            parts[0].at[pl.ds(t * ROW_STEP + TOK + EXTRA, TOK), :], rows.at[t], sems.at[t]
        )
        for t in range(PEERS)
    ]
    for copy in copies:
        copy.start()
    step = PEERS // len(normed.copies)
    for t in range(PEERS):
        copies[t].wait()
        x = rows[t].astype(f32)
        r = lax.rsqrt(jnp.mean(x * x, axis=-1, keepdims=True) + eps)
        normed.ref[t * TOK : (t + 1) * TOK, :] = (x * r * gain).astype(bf16)
        if t % step == step - 1:
            normed.start_part(t // step)


def unweave(source, target):
    for s in range(0, PEERS, 2):
        held = source.get_part(s // 2)
        rows = [held[(s + k) * 2 * CAP : (s + k + 1) * 2 * CAP, :].astype(f32) for k in range(2)]
        for i in range(2):
            mine = jnp.concatenate([row[i * CAP : (i + 1) * CAP] for row in rows], axis=0)
            target[i, s * CAP : (s + 2) * CAP, :] = mine.astype(bf16)


def weave(spread, sent):
    for s in range(PEERS):
        rows = slice(s * CAP, (s + 1) * CAP)
        sent.ref[s * 2 * CAP : (s + 1) * 2 * CAP, :] = jnp.concatenate(
            [spread[0, rows, :], spread[1, rows, :]], axis=0
        ).astype(bf16)
        if s % 2 == 1:
            sent.start_part(s // 2)


def expert_kernel(info, ins, parts, outs, scratch):
    arrived, grads, small = ins
    sent, xs, acted, dgate, dup, gates, lgs = [out.ref for out in outs]
    spread, wg, wu, wd, sems = scratch

    def piece(i, k):
        first, count, target, column = (
            (0, TOK, wg, 0),
            (128, TOK, wu, 0),
            (256, HD, wd, 0),
            (320, HD, wd, HALF),
        )[k]
        return lambda part, d: (
            part.at[pl.ds(i * 384 + first, count), :],
            target.at[i, aligned(d, count), pl.ds(column, HALF)],
        )

    copies = place_parts(
        info,
        shards(parts[0]),
        [piece(i, k) for i in range(2) for k in range(4)],
        sems,
        shard_place,
    )
    unweave(arrived, xs)
    outs[1].start()
    grads = grads.get()
    small = small.get()
    wait_all(copies)
    first = (info[0] * SIDE + info[1]) * 2
    chunk = ROWS // 2

    for n in range(4):
        i = n // 2
        rows = slice(n % 2 * chunk, (n % 2 + 1) * chunk)
        x = xs[i, rows, :]
        router = small[0 : 2 * EXTRA, :]
        logits = mm(x, router, NT)
        peak = jnp.max(logits, axis=-1, keepdims=True)
        chances = jnp.exp(logits - peak)
        chances = chances / jnp.sum(chances, axis=-1, keepdims=True)
        mine = (lax.broadcasted_iota(jnp.int32, (chunk, EXPERTS), 1) == first + i).astype(f32)
        gate = jnp.sum(chances * mine, axis=-1, keepdims=True)
        gate_pre = mm(x, wg[i])
        up_pre = mm(x, wu[i])
        sigmoid = 1.0 / (1.0 + jnp.exp(-gate_pre))
        silu = gate_pre * sigmoid
        act = (silu * up_pre).astype(bf16)
        acted[i, rows, :] = act
        back = mm(grads[i, rows, :], wd[i], NT)
        dot = jnp.sum(act.astype(f32) * back, axis=-1, keepdims=True)
        back = back * gate
        gate_grad = (back * up_pre * (sigmoid * (1.0 + gate_pre * (1.0 - sigmoid)))).astype(bf16)
        up_grad = (back * silu).astype(bf16)
        dgate[i, rows, :] = gate_grad
        dup[i, rows, :] = up_grad
        lg = (dot * gate * (mine - chances)).astype(bf16)
        lgs[i, rows, :] = jnp.concatenate([lg, jnp.zeros((chunk, 128 - EXPERTS), bf16)], axis=1)
        gates[i, rows, :] = jnp.broadcast_to(gate, (chunk, 128))
        spread[i, rows, :] = (
            mm(gate_grad, wg[i], NT) + mm(up_grad, wu[i], NT) + mm(lg, router)
        )
        if n % 2 == 1:
            for one in outs[2:]:
                one.start_part(i)
    weave(spread, outs[0])


def weights_kernel(info, ins, parts, outs, scratch):
    xs, gs, acted, dgate, dup, gates, lgs, slots = ins
    routed = outs[0].ref
    mine, other = [out.ref for out in outs[1:5]], [out.ref for out in outs[5:9]]
    spread, wd, sums, down_sums, router_grad, sems = scratch
    def piece(i, k):
        return lambda part, d: (
            part.at[pl.ds(i * 384 + 256 + HD * k, HD), :],
            wd.at[i, aligned(d, HD), pl.ds(k * HALF, HALF)],
        )

    copies = place_parts(
        info,
        shards(parts[0]),
        [piece(i, k) for i in range(2) for k in range(2)],
        sems,
        shard_place,
    )
    xs, gs, acted, dgate, dup, gates, lgs, slots = [one.get() for one in ins]
    wait_all(copies)
    router_grad[...] = jnp.zeros_like(router_grad)

    def step(i, carry):
        source = xs[i]
        gate = gates[i][:, 0:1]
        spread[i] = mm(acted[i], wd[i]) * gate
        slot_grad = (gs[i].astype(f32) * gate).astype(bf16)
        router_grad[...] += mm(lgs[i], source, TN)
        sums[0] = mm(source, dgate[i], TN).astype(bf16)
        sums[1] = mm(source, dup[i], TN).astype(bf16)
        down_sums[...] = mm(acted[i], slot_grad, TN).astype(bf16)
        for r in range(8):
            d = part_place(info, r)
            target = (*mine, *other)[r]
            target[i, 0:128, :] = sums[0, aligned(d, TOK), :]
            target[i, 128:256, :] = sums[1, aligned(d, TOK), :]
            target[i, 256:320, :] = down_sums[aligned(d, HD), 0:HALF]
            target[i, 320:384, :] = down_sums[aligned(d, HD), HALF:D]
        return carry

    lax.fori_loop(0, 2, step, 0)
    outs[9].ref[...] = router_grad[0:EXPERTS, :].astype(bf16)
    for one in (*outs[5:9], *outs[1:5]):
        one.start()
    for t in range(PEERS):
        span = slice(t * CAP, (t + 1) * CAP)
        rows = jnp.concatenate([spread[i, span, :] for i in range(2)], axis=0).astype(bf16)
        routed[t * TOK : (t + 1) * TOK, :] = mm(slots[t], rows, TN).astype(bf16)


def hidden_kernel(info, ins, parts, outs, scratch):
    arrived, table, hidden, cot, small = ins
    hidden_grad, low, send = outs
    w_out, sems = scratch
    copies = place_parts(info, parts, w_out_pieces(w_out), sems)
    step = 2 * ROWS // 8
    table = table.get()
    grad = jnp.zeros((TOK, D), f32)
    for k in range(8):
        rows = slice(k * step, (k + 1) * step)
        grad = grad + mm(table[rows, :], arrived.get_part(k)[rows, :], TN)
    hidden = hidden.get()[...]
    gain = small.get()[2 * EXTRA : 3 * EXTRA, :].astype(f32)[1:2, :]
    r = lax.rsqrt(jnp.mean(hidden * hidden, axis=-1, keepdims=True) + eps)
    scaled = grad * gain
    dot = jnp.mean(scaled * hidden, axis=-1, keepdims=True)
    total = cot.get()[...].astype(f32) + r * scaled - hidden * (r * r * r * dot)
    gain_grad = jnp.sum(grad * hidden * r, axis=0, keepdims=True)
    gain_grad = jnp.concatenate([gain_grad, jnp.zeros((EXTRA - 1, D), f32)], axis=0)
    low.ref[TOK : TOK + EXTRA, :] = gain_grad.astype(bf16)
    hidden_grad.ref[...] = total
    low.ref[0:TOK, :] = total.astype(bf16)
    wait_all(copies)
    turned = mm(w_out[...], low.ref[0:TOK, :], NT).astype(bf16)
    for e in range(PEERS):
        send.ref[e] = turned[HEAD_OF[e] * HD : (HEAD_OF[e] + 1) * HD, :]


def out_weights_kernel(info, ins, parts, outs, scratch):
    mixed_a, mixed_b, router_a, router_b, low_a, low_b = [one.get() for one in ins]
    extra = scratch[0]
    router = router_a[...].astype(f32) + router_b[...].astype(f32)
    gains = slice(TOK, TOK + EXTRA)
    gain = low_a[gains, :].astype(f32) + low_b[gains, :].astype(f32)
    rest = jnp.zeros((128 - EXPERTS - EXTRA, D), f32)
    extra[...] = jnp.concatenate([router, gain, rest], axis=0).T
    low = jnp.concatenate([low_a[0:TOK, :], low_b[0:TOK, :]], axis=0)
    for m in range(SIDE):
        rows = aligned(part_place(info, m), TOK)
        mixed = jnp.concatenate([mixed_a[rows, :], mixed_b[rows, :]], axis=1)
        outs[m].ref[:, 0:D] = mm(mixed, low).astype(bf16)
        outs[m].ref[:, D:PACK] = extra[rows, :].astype(bf16)
        outs[m].start()


def attend_back_kernel(info, ins, parts, outs, scratch):
    heads, out_t, lse, arrived, cos, sin, start = [one.get() for one in ins[0:7]]
    send = outs[0].ref
    qz, kvt, kvn, oz, qon, dq, low, delta, sums = scratch
    steps = SEQ // QB
    spread_heads(heads, qz, kvt, kvn)
    for i in range(steps):
        span = slice(i * QB, (i + 1) * QB)
        got = jnp.concatenate([arrived[i * 4 + j] for j in range(4)], axis=1)
        oz[0:HD, span] = jnp.zeros((HD, QB), bf16)
        oz[HD:128, span] = got
        wide = got.astype(f32)
        delta[:, span] = jnp.sum(wide * out_t[:, span], axis=0, keepdims=True)
        qon[span, :] = jnp.concatenate([qz[0:HD, span].astype(f32), wide], axis=0).T.astype(bf16)
        dq[:, span] = jnp.zeros((HD, QB), f32)
    for ki in range(steps):
        keys = slice(ki * QB, (ki + 1) * QB)
        value_sum = jnp.zeros((QB, 128), f32)
        key_sum = jnp.zeros((QB, 128), f32)
        for qi in range(ki, steps):
            span = slice(qi * QB, (qi + 1) * QB)
            scores = mm(kvn[keys, :], qz[:, span])
            expo = jnp.where(
                allowed(ki, qi, start[:, span]), jnp.exp(scores - lse[:, span]), 0.0
            )
            back = mm(kvn[keys, :], oz[:, span])
            score_grad = (expo * (back - delta[:, span])).astype(bf16)
            value_sum = value_sum + mm(expo.astype(bf16), qon[span, :])
            key_sum = key_sum + mm(score_grad, qon[span, :])
            dq[:, span] += mm(kvt[0:HD, keys], score_grad)
        lane = lax.broadcasted_iota(jnp.int32, (QB, 128), 1)
        turned = jnp.where(lane < HD, key_sum, value_sum).T
        low[HD : 2 * HD, keys] = rotated_back(turned[0:HD], cos[:, keys], sin[:, keys]).astype(bf16)
        low[2 * HD : 3 * HD, keys] = turned[HD:128].astype(bf16)
    for i in range(steps):
        span = slice(i * QB, (i + 1) * QB)
        low[0:HD, span] = rotated_back(
            dq[:, span] * (HD**-0.5), cos[:, span], sin[:, span]
        ).astype(bf16)
    for j in range(PEERS):
        send[j] = low[:, j * TOK : (j + 1) * TOK]
    outs[0].start()
    total = mm(low[...], ins[7].get()[...]).astype(bf16)
    for d in range(DP):
        sums[d] = total[:, d * TOK : (d + 1) * TOK]
    for r in (4, 5, 6, 7, 0, 1, 2, 3):
        outs[1 + r].ref[...] = sums[part_place(info, r)]
        outs[1 + r].start()


def input_kernel(info, ins, parts, outs, scratch):
    arrived, hidden_grad, states, small = ins[0:4]
    grad, query, key, value, out, router, rest = [one.ref for one in outs]
    wide, sums, sems = scratch
    mine = info[0] % 2
    copies = []
    for half, first, side in ((parts[0:8], 0, mine), (parts[8:16], D, 1 - mine)):
        copies += place_parts(
            info,
            half,
            [
                lambda part, d, a=a, b=b, w=w, first=first, side=side: (
                    part.at[pl.ds(0, TOK), pl.ds(first + a, w)],
                    wide.at[aligned(d, TOK), pl.ds(pl.multiple_of(b + side * w, 256), w)],
                )
                for a, b, w in ((0, 0, 512), (512, 1024, 256), (768, 1536, 256))
            ],
            sems.at[0 if first == 0 else 1],
        )
    arrived = arrived.get()

    def pair_sum(first, count):
        rows = slice(first, first + count)
        pairs = [
            arrived[DEV_OF[g], rows, :].astype(f32) + arrived[DEV_OF[g + 1], rows, :].astype(f32)
            for g in range(0, HEADS, 2)
        ]
        return jnp.concatenate(pairs, axis=0)

    def by_head(first):
        rows = [arrived[DEV_OF[h], first : first + HD, :].astype(f32) for h in range(HEADS)]
        return jnp.concatenate(rows, axis=0)

    dq = by_head(0).T.astype(bf16)
    dk = pair_sum(HD, HD).T.astype(bf16)
    dv = pair_sum(2 * HD, HD).T.astype(bf16)
    query[...] = by_head(192).T
    key[...] = pair_sum(192 + HD, HD).T
    value[...] = pair_sum(192 + 2 * HD, HD).T
    for j in range(PEERS):
        rows = arrived[j, 384:456, :].astype(f32)
        for g in range(9):
            target = out.at[:, g * 128 : (g + 1) * 128] if g < 8 else sums
            target[j * 8 : (j + 1) * 8, :] = rows[g * 8 : (g + 1) * 8, :]
    for one in outs[1:5]:
        one.start()
    turned = sums[...].T
    router[...] = turned[0:EXPERTS, :]
    rest[1:2, :] = turned[EXPERTS : EXPERTS + 1, :]
    weighted = sum(
        jnp.sum(total[...] * own.get()[...].astype(f32), axis=-1, keepdims=True)
        for total, own in zip((query, key, value), ins[4:7])
    )
    weighted = jnp.concatenate([weighted, jnp.zeros((TOK, 127), f32)], axis=1).T
    rest[0:1, :] = weighted[0:1, :] / ins[7].get()[...].astype(f32)
    wait_all(copies)
    back = (
        mm(dq, wide[:, 0:1024], NT)
        + mm(dk, wide[:, 1024:1536], NT)
        + mm(dv, wide[:, 1536:2048], NT)
    )
    x = states.get()[...].astype(f32)
    gain = small.get()[2 * EXTRA : 3 * EXTRA, :].astype(f32)[0:1, :]
    r = lax.rsqrt(jnp.mean(x * x, axis=-1, keepdims=True) + eps)
    scaled = back * gain
    dot = jnp.mean(scaled * x, axis=-1, keepdims=True)
    grad[...] = hidden_grad.get()[...] + r * scaled - x * (r * r * r * dot)


def per_device(
    inputs,
    segments,
    routes,
    gain_attn,
    w_query,
    w_key,
    w_value,
    w_out,
    gain_ffn,
    w_router,
    expert_gate,
    expert_up,
    expert_down,
    cotangent,
):
    place = lax.axis_index("expert")
    row = lax.axis_index("dp")
    info = jnp.stack([place // SIDE, place % SIDE, row // 2, row % 2]).astype(jnp.int32)
    states = inputs[0]
    cot = cotangent[0]
    my_routes = routes[0].T

    segment_row = segments[0][None, :]
    index = jnp.arange(SEQ, dtype=jnp.int32)[None, :]
    start = jnp.zeros((1, SEQ), jnp.int32)
    for s in range(3):
        count = jnp.sum((segment_row == s).astype(jnp.int32))
        start = start + jnp.where(segment_row > s, count, 0)
    freqs = theta ** (-jnp.arange(0, HD, 2, dtype=f32) / HD)
    angles = freqs[:, None] * (index - start).astype(f32)
    cosine, sine = jnp.cos(angles), jnp.sin(angles)
    blocks = [(place // 8 * 2 + j) * 4 + place % 4 for j in range(2)]
    my_angles = jnp.concatenate(
        [lax.dynamic_slice_in_dim(angles, block * TOK, TOK, 1) for block in blocks], axis=1
    )
    my_cosine, my_sine = jnp.cos(my_angles), jnp.sin(my_angles)

    packed = run(
        pack_kernel,
        "pack",
        (info,),
        (expert_gate, expert_up, expert_down),
        (shape((768, HALF), bf16),),
        (pltpu.SemaphoreType.DMA((8,)),),
    )[0]
    names = jnp.concatenate(
        [
            my_routes.astype(f32),
            jnp.zeros((EXTRA - 8, TOK), f32),
            gain_attn.astype(f32)[None, :],
            gain_ffn.astype(f32)[None, :],
            jnp.zeros((EXTRA - 2, TOK), f32),
        ],
        axis=0,
    )
    dense, outward, cots = run(
        dense_kernel,
        "dense",
        (info, w_router.T, Near(names)),
        (w_query, w_key, w_value, w_out, cot, states),
        (
            shape((TOK + EXTRA, D), bf16),
            shape((TOK, 2 * D), bf16),
            shape((ROW_STEP, D), bf16),
        ),
        (pltpu.SemaphoreType.DMA((9,)),),
    )
    cots = lax.all_gather(cots, "expert", axis=0, tiled=True)
    partner = lax.ppermute(states, "expert", [(e, e ^ 4) for e in range(PEERS)])
    dense = gather_dp(dense, packed, cosine, sine, my_cosine, my_sine, partner)

    small, heads = run(
        qkv_kernel,
        "qkv",
        (info, states, partner, Near(my_cosine), Near(my_sine)),
        dense,
        (
            shape((3 * EXTRA, D), bf16),
            shape((8, 2, 3 * HD, TOK), bf16),
        ),
        (
            pltpu.VMEM((D, D), bf16),
            pltpu.VMEM((2, TOK, D), f32),
            pltpu.SemaphoreType.DMA((32,)),
        ),
        cost=5,
    )
    heads = swap_side(heads)

    packed = lax.all_gather(tied(packed, small), "dp", axis=0)
    outward = gather_y(tied(outward, small))

    out_t, lse, mixed_send = run(
        attend_kernel,
        "attend",
        (info, Near(heads), Near(start)),
        (),
        (
            shape((HD, SEQ), f32),
            shape((1, SEQ), f32),
            shape((HEADS, HD, TOK), bf16),
        ),
        (
            pltpu.VMEM((128, SEQ), bf16),
            pltpu.VMEM((128, SEQ), bf16),
            pltpu.VMEM((SEQ, 128), bf16),
        ),
        cost=6,
    )
    outward = list(lax.optimization_barrier((*outward, mixed_send))[0:SIDE])
    outward += [core_swap(part) for part in outward]
    mixed_t = swap_all(mixed_send).reshape(HEADS * HD, TOK)

    hidden, send, table, ordered = run(
        project_kernel,
        "project",
        (info, Near(mixed_t), states, small, my_routes),
        outward,
        (
            shape((TOK, D), f32),
            shape((2 * ROWS, D), bf16),
            shape((2 * ROWS, TOK), bf16),
            shape((HEADS * HD, TOK), bf16),
        ),
        (pltpu.VMEM((D, D), bf16), pltpu.SemaphoreType.DMA((8,))),
        cost=5,
    )
    arrived = swap_all(send)

    grad_rows, slots = run(
        rows_kernel,
        "grad_rows",
        (info,),
        (cots,),
        (Near(shape((2, ROWS, D), bf16)), shape((PEERS, 2 * CAP, TOK), bf16)),
        (
            pltpu.VMEM((PEERS, TOK + EXTRA, D), bf16),
            pltpu.VMEM((2 * PEERS, TOK), f32),
            pltpu.SemaphoreType.DMA((PEERS,)),
        ),
        limit=32,
    )
    normed = run(
        norm_kernel,
        "normed",
        (info, small),
        (cots,),
        (shape((SEQ, D), bf16),),
        (pltpu.VMEM((PEERS, TOK, D), bf16), pltpu.SemaphoreType.DMA((PEERS,))),
        after=(table,),
    )[0]

    sent_grad, xs, acted, dgate, dup, gates, lgs = run(
        expert_kernel,
        "experts",
        (info, arrived, Near(grad_rows), small),
        (packed,),
        (
            shape((2 * ROWS, D), bf16),
            shape((2, ROWS, D), bf16),
            shape((2, ROWS, EF), bf16),
            shape((2, ROWS, EF), bf16),
            shape((2, ROWS, EF), bf16),
            shape((2, ROWS, 128), f32),
            shape((2, ROWS, 128), bf16),
        ),
        (
            pltpu.VMEM((2, ROWS, D), f32),
            pltpu.VMEM((2, D, EF), bf16),
            pltpu.VMEM((2, D, EF), bf16),
            pltpu.VMEM((2, EF, D), bf16),
            pltpu.SemaphoreType.DMA((64,)),
        ),
        limit=28,
        after=(normed,),
        cost=12,
    )
    back = swap_all(sent_grad)

    routed, *expert_grads, router_grad = run(
        weights_kernel,
        "weights",
        (info, xs, Near(grad_rows), acted, dgate, dup, gates, lgs, slots),
        (packed,),
        (
            shape((SEQ, D), bf16),
            *(shape((2, 384, 512), bf16),) * 8,
            shape((EXPERTS, D), bf16),
        ),
        (
            pltpu.VMEM((2, ROWS, D), f32),
            pltpu.VMEM((2, EF, D), bf16),
            pltpu.VMEM((2, D, EF), bf16),
            pltpu.VMEM((EF, D), bf16),
            pltpu.VMEM((128, D), f32),
            pltpu.SemaphoreType.DMA((32,)),
        ),
        limit=40,
    )
    expert_pairs = pair_up(info, expert_grads[0:4], expert_grads[4:8], "expert_pairs")
    expert_near = [dp_from(expert_pairs[m], SIDE - m) for m in (1, 3)]

    hidden_grad, low, grad_send = run(
        hidden_kernel,
        "hidden_grad",
        (info, back, table, hidden, cot, small),
        outward,
        (
            shape((TOK, D), f32),
            shape((TOK + EXTRA, D), bf16),
            shape((HEADS, HD, TOK), bf16),
        ),
        (pltpu.VMEM((D, D), bf16), pltpu.SemaphoreType.DMA((8,))),
        after=(router_grad, *expert_pairs),
        cost=4,
    )
    mixed_grad = swap_all(grad_send)

    out_pairs = run(
        out_weights_kernel,
        "out_weights",
        (
            info,
            ordered,
            core_swap(ordered),
            router_grad,
            core_swap(router_grad),
            low,
            core_swap(low),
        ),
        (),
        (shape((TOK, PACK), bf16),) * SIDE,
        (pltpu.VMEM((D, 128), f32),),
    )

    routed = lax.psum_scatter(tied(routed, expert_pairs[0]), "expert", scatter_dimension=0, tiled=True)
    output = (hidden + routed.astype(f32)).astype(bf16)

    grads_send, *w_grads = run(
        attend_back_kernel,
        "attend_back",
        (info, heads, out_t, lse, Near(mixed_grad), cosine, sine, start, normed),
        (),
        (
            shape((PEERS, 192, TOK), bf16),
            *(shape((192, TOK), bf16),) * 8,
        ),
        (
            pltpu.VMEM((128, SEQ), bf16),
            pltpu.VMEM((128, SEQ), bf16),
            pltpu.VMEM((SEQ, 128), bf16),
            pltpu.VMEM((128, SEQ), bf16),
            pltpu.VMEM((SEQ, 128), bf16),
            pltpu.VMEM((HD, SEQ), f32),
            pltpu.VMEM((192, SEQ), bf16),
            pltpu.VMEM((1, SEQ), f32),
            pltpu.VMEM((DP, 192, TOK), bf16),
        ),
        limit=32,
        after=(*out_pairs, *expert_near),
        cost=12,
    )
    out_far = send_pairs(out_pairs)
    *w_grads, _, _, _ = lax.optimization_barrier((*w_grads, *out_far))
    w_pairs = [
        (mine.astype(f32) + core_swap(other).astype(f32)).astype(bf16)
        for mine, other in zip(w_grads[0:4], w_grads[4:8])
    ]
    w_sums = add_parts(w_pairs[0], send_pairs(w_pairs)).astype(bf16)
    expert_far = dp_from(tied(expert_pairs[2], w_sums), 2)
    expert_sums = add_parts(expert_pairs[0], (*expert_near, expert_far))
    out_sums = add_parts(out_pairs[0], out_far).astype(bf16)
    out_sums = swap_all(out_sums).reshape(PEERS, 8, PACK)
    out_sums = jnp.sum(out_sums.astype(f32), axis=0).astype(bf16)
    out_sums = jnp.concatenate([out_sums[:, g * 128 : (g + 1) * 128] for g in range(9)], axis=0)

    ends = jnp.concatenate([w_sums, out_sums], axis=0)
    last = jnp.concatenate(
        [grads_send, jnp.broadcast_to(ends[None], (PEERS, 264, TOK))], axis=1
    )
    last = swap_all(last)

    grad_input, sum_query, sum_key, sum_value, sum_out, sum_router, sum_gains = run(
        input_kernel,
        "grad_input",
        (info, Near(last), hidden_grad, states, small, w_query, w_key, w_value, gain_attn[None, :]),
        (*dense, *outward),
        (
            shape((TOK, D), f32),
            shape((TOK, 1024), f32),
            shape((TOK, 512), f32),
            shape((TOK, 512), f32),
            shape((TOK, D), f32),
            Near(shape((EXPERTS, TOK), f32)),
            Near(shape((2, TOK), f32)),
        ),
        (
            pltpu.VMEM((D, 2048), bf16),
            pltpu.VMEM((TOK, 128), f32),
            pltpu.SemaphoreType.DMA((2, 24)),
        ),
        limit=32,
        after=(output,),
        cost=7,
    )
    return (
        output[None],
        grad_input[None],
        sum_gains[0],
        sum_query,
        sum_key,
        sum_value,
        sum_out,
        sum_gains[1],
        sum_router.T,
        expert_sums[:, 0:128],
        expert_sums[:, 128:256],
        jnp.concatenate([expert_sums[:, 256:320], expert_sums[:, 320:384]], axis=2),
    )


def solution(mesh):
    placed = (
        P("dp", "expert", None),
        P("dp", None),
        P("dp", "expert", None),
        P("dp"),
        P("dp", None),
        P("dp", None),
        P("dp", None),
        P("dp", None),
        P("dp"),
        P("dp", None),
        P("expert", "dp", None),
        P("expert", "dp", None),
        P("expert", "dp", None),
        P("dp", "expert", None),
    )
    return jax.shard_map(
        per_device,
        mesh=mesh,
        in_specs=placed,
        out_specs=(
            P("dp", "expert", None),
            P("dp", "expert", None),
            P("dp"),
            P("dp", None),
            P("dp", None),
            P("dp", None),
            P("dp", None),
            P("dp"),
            P("dp", None),
            P("expert", "dp", None),
            P("expert", "dp", None),
            P("expert", "dp", None),
        ),
        check_vma=False,
    )
```

```python
import jax
import jax.numpy as jnp
from jax import lax
from jax.experimental import pallas as pl
from jax.experimental.pallas import tpu as pltpu
from jax.sharding import PartitionSpec as P

D = 1024
HEADS = 16
HD = 64
EF = 512
EXPERTS = 32
CAP = 40
TOK = 128
SEQ = 2048
SIDE = 4
PEERS = 16
DP = 8
QB = 512
HALF = 512
ROWS = PEERS * CAP
EXTRA = 16
PACK = 1152
ROW_STEP = 2 * TOK + EXTRA

HEAD_OF = [(e // 4 % 2) * 8 + e // 8 * 4 + e % 4 for e in range(PEERS)]
DEV_OF = [HEAD_OF.index(h) for h in range(HEADS)]
SAME_SIDE = [[e for e in range(PEERS) if e // 4 % 2 == p] for p in range(2)]

eps = 1e-06
theta = 10000.0
masked = -1000000000.0
bf16 = jnp.bfloat16
f32 = jnp.float32
MIB = 1 << 20

NN = (((1,), (0,)), ((), ()))
NT = (((1,), (1,)), ((), ()))
TN = (((0,), (0,)), ((), ()))


def mm(left, right, dims=NN):
    return lax.dot_general(left, right, dims, preferred_element_type=f32)


def shape(dims, dtype):
    return jax.ShapeDtypeStruct(dims, dtype)


def cuts(dims, dtype):
    if dims[0] == 2 and len(dims) == 3:
        return 2
    size = jnp.dtype(dtype).itemsize
    for dim in dims:
        size *= dim
    step = 16 if len(dims) == 2 else 1
    for count in (8, 4, 2):
        if dims[0] % (count * step) == 0 and size // count >= MIB // 4:
            return count
    return 1


class Moved:
    def __init__(self, source, target, sems, first, dims, dtype):
        count = cuts(dims, dtype)
        rows = dims[0] // count
        self.copies = [
            pltpu.make_async_copy(
                source.at[pl.ds(k * rows, rows)], target.at[pl.ds(k * rows, rows)], sems.at[first + k]
            )
            for k in range(count)
        ]
        self.started = False
        self.waited = False

    def start(self):
        self.started = True
        for copy in self.copies:
            copy.start()

    def wait(self):
        if not self.waited:
            self.waited = True
            for copy in self.copies:
                copy.wait()


class In(Moved):
    def __init__(self, source, target, *rest):
        super().__init__(source, target, *rest)
        self.target = target

    def get(self):
        self.wait()
        return self.target

    def get_part(self, k):
        self.copies[k].wait()
        self.waited = k == len(self.copies) - 1
        return self.target


class Out(Moved):
    def __init__(self, source, target, *rest):
        super().__init__(source, target, *rest)
        self.ref = source

    def start_part(self, k):
        self.started = True
        self.copies[k].start()


class Near:
    def __init__(self, array):
        self.array = array


class Held:
    def __init__(self, ref):
        self.ref = ref

    def get(self):
        return self.ref

    def start(self):
        pass


def tied(value, *others):
    return lax.optimization_barrier((value, *others))[0]


def run(body, name, ins, raws, outs, scratch=(), limit=24, after=(), cost=0):
    info, arrays = ins[0], ins[1:]
    in_near = [isinstance(v, Near) for v in arrays]
    out_near = [isinstance(v, Near) for v in outs]
    arrays = [v.array if isinstance(v, Near) else v for v in arrays]
    outs = [v.array if isinstance(v, Near) else v for v in outs]
    both = list(zip((*arrays, *outs), (*in_near, *out_near)))
    count = sum(cuts(v.shape, v.dtype) for v, near in both if not near)
    held = [pltpu.VMEM(v.shape, v.dtype) for v, near in both if not near]

    def kernel(*refs):
        info_ref, refs = refs[0], refs[1:]
        in_refs, refs = refs[: len(arrays)], refs[len(arrays) :]
        raw_refs, refs = refs[: len(raws)], refs[len(raws) :]
        out_refs, refs = refs[: len(outs)], refs[len(outs) :]
        spaces, refs = list(refs[: len(held)]), refs[len(held) :]
        sems, rest = refs[0], refs[1:]
        first = 0
        fetched, sent = [], []
        for v, near, ref in zip(arrays, in_near, in_refs):
            if near:
                fetched.append(Held(ref))
                continue
            fetched.append(In(ref, spaces.pop(0), sems, first, v.shape, v.dtype))
            first += cuts(v.shape, v.dtype)
        for v, near, ref in zip(outs, out_near, out_refs):
            if near:
                sent.append(Held(ref))
                continue
            sent.append(Out(spaces.pop(0), ref, sems, first, v.shape, v.dtype))
            first += cuts(v.shape, v.dtype)
        for one in fetched:
            one.start()
        body(info_ref, fetched, raw_refs, sent, rest)
        for one in fetched:
            one.get()
        moves = [one for one in sent if isinstance(one, Out)]
        for one in moves:
            if not one.started:
                one.start()
        for one in moves:
            one.wait()

    if after:
        info = tied(info, *after)

    def pinned(v, near=False):
        return v if near else pltpu.with_memory_space_constraint(v, pltpu.HBM)

    def spec(near=False):
        return pl.BlockSpec(memory_space=pltpu.VMEM if near else pltpu.HBM)

    return pl.pallas_call(
        kernel,
        name=name,
        out_shape=tuple(
            shape(v.shape, v.dtype) if near else pltpu.HBM(v.shape, v.dtype)
            for v, near in zip(outs, out_near)
        ),
        in_specs=[pl.BlockSpec(memory_space=pltpu.SMEM)]
        + [spec(near) for near in in_near]
        + [spec()] * len(raws),
        out_specs=tuple(spec(near) for near in out_near),
        scratch_shapes=[*held, pltpu.SemaphoreType.DMA((max(count, 1),)), *scratch],
        compiler_params=pltpu.CompilerParams(vmem_limit_bytes=limit * MIB),
        cost_estimate=pl.CostEstimate(
            flops=1000 + cost * 10**9, bytes_accessed=1000, transcendentals=0
        ),
    )(info, *[pinned(v, near) for v, near in zip(arrays, in_near)], *[pinned(v) for v in raws])


def expert_from(values, dz, dx):
    pairs = [
        (z * SIDE + x, ((z - dz) % SIDE) * SIDE + (x - dx) % SIDE)
        for z in range(SIDE)
        for x in range(SIDE)
    ]
    return lax.ppermute(values, "expert", pairs)


def dp_from(values, dy):
    pairs = [(y * 2 + c, ((y - dy) % SIDE) * 2 + c) for y in range(SIDE) for c in range(2)]
    return lax.ppermute(values, "dp", pairs)


def core_swap(values):
    return lax.ppermute(values, "dp", [(d, d ^ 1) for d in range(DP)])


def gather_ring(values, step, *others):
    near = {m: step(values, m) for m in (1, 3)}
    far = step(tied(values, *others) if others else values, 2)
    return [values, near[1], far, near[3]]


def along_z(values, m):
    return expert_from(values, m, 0)


def along_x(values, m):
    return expert_from(values, 0, m)


def gather_y(values):
    far = {m: dp_from(values, m) for m in (1, 3, 2)}
    return [values, far[1], far[2], far[3]]


def gather_dp(values, *others):
    mine = gather_y(values)
    if others:
        mine[2] = tied(mine[2], *others)
    return mine + [core_swap(part) for part in mine]


def send_pairs(pairs):
    return [dp_from(pairs[m], SIDE - m) for m in (1, 3, 2)]


def add_parts(first, others):
    total = first.astype(f32)
    for other in others:
        total = total + other.astype(f32)
    return total


def pair_kernel(info, ins, parts, outs, scratch):
    for m in range(SIDE):
        mine, other = ins[m].get()[...], ins[SIDE + m].get()[...]
        outs[m].ref[...] = (mine.astype(f32) + other.astype(f32)).astype(bf16)
        outs[m].start()


def pair_up(info, mine, other, name):
    swapped = [core_swap(part) for part in other]
    part = shape(mine[0].shape, bf16)
    return run(pair_kernel, name, (info, *mine, *swapped), (), (part,) * SIDE)


def swap_side(values):
    return lax.all_to_all(
        values, "expert", split_axis=0, concat_axis=0, tiled=True, axis_index_groups=SAME_SIDE
    )


def swap_all(values):
    return lax.all_to_all(values, "expert", split_axis=0, concat_axis=0, tiled=True)


def part_place(info, r):
    return ((info[2] + r % SIDE) % SIDE) * 2 + (info[3] ^ (r // SIDE))


def aligned(index, step):
    return pl.ds(pl.multiple_of(index * step, step), step)


def rotated(values, c, s):
    w1, w2 = values[: HD // 2], values[HD // 2 :]
    return jnp.concatenate([w1 * c - w2 * s, w2 * c + w1 * s], axis=0)


def rotated_back(values, c, s):
    w1, w2 = values[: HD // 2], values[HD // 2 :]
    return jnp.concatenate([w1 * c + w2 * s, w2 * c - w1 * s], axis=0)


def allowed(ki, qi, start):
    key = ki * QB + lax.broadcasted_iota(jnp.int32, (QB, QB), 0)
    keep = key >= start
    if ki == qi:
        keep = keep & (key <= qi * QB + lax.broadcasted_iota(jnp.int32, (QB, QB), 1))
    return keep


def place_parts(info, parts, pieces, sems, place=part_place):
    copies = []
    for r in range(8):
        for k, piece in enumerate(pieces):
            source, target = piece(parts[r], place(info, r))
            copies.append(pltpu.make_async_copy(source, target, sems.at[r * len(pieces) + k]))
    for copy in copies:
        copy.start()
    return copies


def wait_all(copies):
    for copy in copies:
        copy.wait()


def dense_kernel(info, ins, parts, outs, scratch):
    router, names = ins
    query, key, value, w_out, cot, states = parts
    dense, outward, cots = [out.ref for out in outs]
    sems = scratch[0]
    mine = info[0] % 2
    halves = []
    for target, first, side in ((dense, 0, mine), (outward, D, 1 - mine)):
        for source, width, column in ((query, 512, 0), (key, 256, 512), (value, 256, 768)):
            halves.append(
                (
                    source.at[:, aligned(side, width)],
                    target.at[pl.ds(0, TOK), pl.ds(first + column, width)],
                )
            )
    copies = [
        pltpu.make_async_copy(source, target, sems.at[k])
        for k, (source, target) in enumerate(
            (
                *halves,
                (w_out, outward.at[:, pl.ds(0, D)]),
                (cot, cots.at[pl.ds(0, TOK), :]),
                (states, cots.at[pl.ds(TOK + EXTRA, TOK), :]),
            )
        )
    ]
    for copy in copies:
        copy.start()
    rows = slice(TOK, TOK + EXTRA)
    dense[rows, 384:D] = jnp.zeros((EXTRA, D - 384), bf16)
    dense[rows, 0:128] = router.get()[0:EXTRA, :]
    dense[rows, 128:256] = router.get()[EXTRA : 2 * EXTRA, :]
    dense[rows, 256:384] = names.get()[EXTRA : 2 * EXTRA, :].astype(bf16)
    cots[rows, TOK:D] = jnp.zeros((EXTRA, D - TOK), bf16)
    cots[rows, 0:TOK] = names.get()[0:EXTRA, :].astype(bf16)
    wait_all(copies)


def pack_kernel(info, ins, parts, outs, scratch):
    gate, up, down = parts
    packed = outs[0].ref
    sems = scratch[0]
    pairs = []
    for i in range(2):
        for k, source in enumerate(
            (
                gate.at[i],
                up.at[i],
                down.at[i, :, pl.ds(0, HALF)],
                down.at[i, :, pl.ds(HALF, HALF)],
            )
        ):
            row, count = i * 384 + (0, 128, 256, 320)[k], (128, 128, 64, 64)[k]
            pairs.append((source, packed.at[pl.ds(row, count), :]))
    copies = [
        pltpu.make_async_copy(source, target, sems.at[k])
        for k, (source, target) in enumerate(pairs)
    ]
    for copy in copies:
        copy.start()
    wait_all(copies)


def qkv_kernel(info, ins, parts, outs, scratch):
    states, partner, cos, sin = ins
    small, send = outs
    wide, rows, sems = scratch
    copies = place_parts(
        info,
        parts,
        [
            lambda part, d: (part.at[pl.ds(0, TOK), :], wide.at[aligned(d, TOK), :]),
            *(
                lambda part, d, k=k: (
                    part.at[pl.ds(TOK, EXTRA), pl.ds(128 * k, 128)],
                    small.ref.at[pl.ds(EXTRA * k, EXTRA), aligned(d, TOK)],
                )
                for k in range(3)
            ),
        ],
        sems,
    )
    mine = info[0] % 2
    rows[mine] = states.get()[...].astype(f32)
    rows[1 - mine] = partner.get()[...].astype(f32)
    x = jnp.concatenate([rows[0], rows[1]], axis=0)
    r = lax.rsqrt(jnp.mean(x * x, axis=-1, keepdims=True) + eps)
    cos, sin = cos.get()[...], sin.get()[...]
    wait_all(copies)
    small.start()
    gain = small.ref[2 * EXTRA : 3 * EXTRA, :].astype(f32)[0:1, :]
    low = (x * r * gain).astype(bf16)
    turned = mm(low, wide[:, 512:1024]).T
    for g in range(4):
        key = rotated(turned[g * HD : (g + 1) * HD], cos, sin)
        value = turned[256 + g * HD : 256 + (g + 1) * HD]
        both = jnp.concatenate([key, value], axis=0).astype(bf16)
        for n in range(2):
            for j in range(2):
                send.ref[2 * g + n, j, HD : 3 * HD, :] = both[:, j * TOK : (j + 1) * TOK]
    turned = mm(low, wide[:, 0:512]).T
    for h in range(8):
        query = rotated(turned[h * HD : (h + 1) * HD], cos, sin).astype(bf16).astype(f32)
        query = (query * (HD**-0.5)).astype(bf16)
        for j in range(2):
            send.ref[h, j, 0:HD, :] = query[:, j * TOK : (j + 1) * TOK]


def spread_heads(arrived, qz, kvt, kvn):
    for i in range(SEQ // QB):
        span = slice(i * QB, (i + 1) * QB)
        got = jnp.concatenate([arrived[i // 2 * 4 + x, i % 2] for x in range(SIDE)], axis=1)
        qz[0:HD, span] = got[0:HD]
        qz[HD:128, span] = jnp.zeros((HD, QB), bf16)
        kvt[:, span] = got[HD : 3 * HD]
        kvn[span, :] = got[HD : 3 * HD].astype(f32).T.astype(bf16)


def attend_kernel(info, ins, parts, outs, scratch):
    start = ins[1].get()
    out_t, lse, send = outs
    qz, kvt, kvn = scratch
    spread_heads(ins[0].get(), qz, kvt, kvn)
    for qi in range(SEQ // QB):
        span = slice(qi * QB, (qi + 1) * QB)
        query = qz[:, span]
        top = jnp.full((1, QB), -jnp.inf, f32)
        total = jnp.zeros((1, QB), f32)
        mixed = jnp.zeros((HD, QB), f32)
        for ki in range(qi, -1, -1):
            keys = slice(ki * QB, (ki + 1) * QB)
            scores = jnp.where(allowed(ki, qi, start[:, span]), mm(kvn[keys, :], query), masked)
            higher = jnp.maximum(top, jnp.max(scores, axis=0, keepdims=True))
            weights = jnp.exp(scores - higher)
            shrink = jnp.exp(top - higher)
            total = total * shrink + jnp.sum(weights, axis=0, keepdims=True)
            mixed = mixed * shrink + mm(kvt[HD:128, keys], weights.astype(bf16))
            top = higher
        mixed = mixed / total
        lse.ref[:, span] = top + jnp.log(total)
        out_t.ref[:, span] = mixed
        for j in range(QB // TOK):
            send.ref[qi * (QB // TOK) + j] = mixed[:, j * TOK : (j + 1) * TOK].astype(bf16)


def shards(gathered):
    return [gathered.at[d] for d in range(DP)]


def shard_place(info, r):
    return r


def w_out_pieces(target):
    return [lambda part, d: (part.at[:, pl.ds(0, D)], target.at[aligned(d, TOK), :])]


def ranks(choose):
    order = lax.broadcasted_iota(jnp.int32, (TOK, TOK), 0)
    before = (order < lax.broadcasted_iota(jnp.int32, (TOK, TOK), 1)).astype(bf16)
    return mm(choose.astype(bf16), before).astype(jnp.int32)


def project_kernel(info, ins, parts, outs, scratch):
    mixed_t, states, small, routes = ins
    hidden, send, table, ordered = outs
    w_out, sems = scratch
    copies = place_parts(info, parts, w_out_pieces(w_out), sems)
    names = lax.broadcasted_iota(jnp.int32, (EXPERTS, TOK), 0)
    choose = jnp.zeros((EXPERTS, TOK), f32)
    routes = routes.get()
    for j in range(8):
        choose = choose + (names == routes[j : j + 1, :]).astype(f32)
    rank = jnp.where(choose > 0.0, ranks(choose), -1)
    slots = lax.broadcasted_iota(jnp.int32, (CAP, TOK), 0)
    for e in range(0, EXPERTS, 2):
        table.ref[e * CAP : (e + 2) * CAP, :] = jnp.concatenate(
            [(rank[e : e + 1] == slots).astype(f32), (rank[e + 1 : e + 2] == slots).astype(f32)],
            axis=0,
        ).astype(bf16)
    mixed_t = mixed_t.get()
    for h in range(HEADS):
        rows = slice(DEV_OF[h] * HD, (DEV_OF[h] + 1) * HD)
        ordered.ref[h * HD : (h + 1) * HD, :] = mixed_t[rows, :]
    ordered.start()
    mixed = ordered.ref[...].astype(f32).T.astype(bf16)
    gain = small.get()[2 * EXTRA : 3 * EXTRA, :].astype(f32)[1:2, :]
    wait_all(copies)
    value = states.get()[...].astype(f32) + mm(mixed, w_out[...])
    hidden.ref[...] = value
    hidden.start()
    table.start()
    r = lax.rsqrt(jnp.mean(value * value, axis=-1, keepdims=True) + eps)
    ffn = (value * r * gain).astype(bf16)
    step = 2 * ROWS // len(send.copies)
    for k in range(len(send.copies)):
        rows = slice(k * step, (k + 1) * step)
        send.ref[rows, :] = mm(table.ref[rows, :], ffn).astype(bf16)
        send.start_part(k)


def rows_kernel(info, ins, parts, outs, scratch):
    grads, slots = outs
    cots, choose, sems = scratch
    first = (info[0] * SIDE + info[1]) * 2
    copies = [
        pltpu.make_async_copy(
            parts[0].at[pl.ds(t * ROW_STEP, TOK + EXTRA), :], cots.at[t], sems.at[t]
        )
        for t in range(PEERS)
    ]
    for copy in copies:
        copy.start()
    wait_all(copies)
    for t in range(PEERS):
        routes = cots[t, TOK : TOK + EXTRA, 0:TOK].astype(f32)[0:8, :].astype(jnp.int32)
        for i in range(2):
            named = (routes == first + i).astype(f32)
            choose[2 * t + i : 2 * t + i + 1, :] = jnp.sum(named, axis=0, keepdims=True)
    rank = jnp.where(choose[...] > 0.0, ranks(choose[...]), -1)
    order = lax.broadcasted_iota(jnp.int32, (CAP, TOK), 0)
    for t in range(0, PEERS, 2):
        rows = []
        for k in (t, t + 1):
            hot = jnp.concatenate(
                [(rank[2 * k + i : 2 * k + i + 1] == order).astype(f32) for i in range(2)], axis=0
            )
            slots.ref[k] = hot.astype(bf16)
            rows.append(mm(hot.astype(bf16), cots[k, 0:TOK, :]))
        for i in range(2):
            mine = jnp.concatenate([row[i * CAP : (i + 1) * CAP] for row in rows], axis=0)
            grads.ref[i, t * CAP : (t + 2) * CAP, :] = mine.astype(bf16)


def norm_kernel(info, ins, parts, outs, scratch):
    gain = ins[0].get()[2 * EXTRA : 3 * EXTRA, :].astype(f32)[0:1, :]
    normed = outs[0]
    rows, sems = scratch
    copies = [
        pltpu.make_async_copy(
            parts[0].at[pl.ds(t * ROW_STEP + TOK + EXTRA, TOK), :], rows.at[t], sems.at[t]
        )
        for t in range(PEERS)
    ]
    for copy in copies:
        copy.start()
    step = PEERS // len(normed.copies)
    for t in range(PEERS):
        copies[t].wait()
        x = rows[t].astype(f32)
        r = lax.rsqrt(jnp.mean(x * x, axis=-1, keepdims=True) + eps)
        normed.ref[t * TOK : (t + 1) * TOK, :] = (x * r * gain).astype(bf16)
        if t % step == step - 1:
            normed.start_part(t // step)


def unweave(source, target):
    for s in range(0, PEERS, 2):
        held = source.get_part(s // 2)
        rows = [held[(s + k) * 2 * CAP : (s + k + 1) * 2 * CAP, :].astype(f32) for k in range(2)]
        for i in range(2):
            mine = jnp.concatenate([row[i * CAP : (i + 1) * CAP] for row in rows], axis=0)
            target[i, s * CAP : (s + 2) * CAP, :] = mine.astype(bf16)


def weave(spread, sent):
    for s in range(PEERS):
        rows = slice(s * CAP, (s + 1) * CAP)
        sent.ref[s * 2 * CAP : (s + 1) * 2 * CAP, :] = jnp.concatenate(
            [spread[0, rows, :], spread[1, rows, :]], axis=0
        ).astype(bf16)
        if s % 2 == 1:
            sent.start_part(s // 2)


def expert_kernel(info, ins, parts, outs, scratch):
    arrived, grads, small = ins
    sent, xs, acted, dgate, dup, gates, lgs = [out.ref for out in outs]
    spread, wg, wu, wd, sems = scratch

    def piece(i, k):
        first, count, target, column = (
            (0, TOK, wg, 0),
            (128, TOK, wu, 0),
            (256, HD, wd, 0),
            (320, HD, wd, HALF),
        )[k]
        return lambda part, d: (
            part.at[pl.ds(i * 384 + first, count), :],
            target.at[i, aligned(d, count), pl.ds(column, HALF)],
        )

    copies = place_parts(
        info,
        shards(parts[0]),
        [piece(i, k) for i in range(2) for k in range(4)],
        sems,
        shard_place,
    )
    unweave(arrived, xs)
    outs[1].start()
    grads = grads.get()
    small = small.get()
    wait_all(copies)
    first = (info[0] * SIDE + info[1]) * 2
    chunk = ROWS // 2

    for n in range(4):
        i = n // 2
        rows = slice(n % 2 * chunk, (n % 2 + 1) * chunk)
        x = xs[i, rows, :]
        router = small[0 : 2 * EXTRA, :]
        logits = mm(x, router, NT)
        peak = jnp.max(logits, axis=-1, keepdims=True)
        chances = jnp.exp(logits - peak)
        chances = chances / jnp.sum(chances, axis=-1, keepdims=True)
        mine = (lax.broadcasted_iota(jnp.int32, (chunk, EXPERTS), 1) == first + i).astype(f32)
        gate = jnp.sum(chances * mine, axis=-1, keepdims=True)
        gate_pre = mm(x, wg[i])
        up_pre = mm(x, wu[i])
        sigmoid = 1.0 / (1.0 + jnp.exp(-gate_pre))
        silu = gate_pre * sigmoid
        act = (silu * up_pre).astype(bf16)
        acted[i, rows, :] = act
        back = mm(grads[i, rows, :], wd[i], NT)
        dot = jnp.sum(act.astype(f32) * back, axis=-1, keepdims=True)
        back = back * gate
        gate_grad = (back * up_pre * (sigmoid * (1.0 + gate_pre * (1.0 - sigmoid)))).astype(bf16)
        up_grad = (back * silu).astype(bf16)
        dgate[i, rows, :] = gate_grad
        dup[i, rows, :] = up_grad
        lg = (dot * gate * (mine - chances)).astype(bf16)
        lgs[i, rows, :] = jnp.concatenate([lg, jnp.zeros((chunk, 128 - EXPERTS), bf16)], axis=1)
        gates[i, rows, :] = jnp.broadcast_to(gate, (chunk, 128))
        spread[i, rows, :] = (
            mm(gate_grad, wg[i], NT) + mm(up_grad, wu[i], NT) + mm(lg, router)
        )
        if n % 2 == 1:
            for one in outs[2:]:
                one.start_part(i)
    weave(spread, outs[0])


def weights_kernel(info, ins, parts, outs, scratch):
    xs, gs, acted, dgate, dup, gates, lgs, slots = ins
    routed = outs[0].ref
    mine, other = [out.ref for out in outs[1:5]], [out.ref for out in outs[5:9]]
    spread, wd, sums, down_sums, router_grad, sems = scratch
    def piece(i, k):
        return lambda part, d: (
            part.at[pl.ds(i * 384 + 256 + HD * k, HD), :],
            wd.at[i, aligned(d, HD), pl.ds(k * HALF, HALF)],
        )

    copies = place_parts(
        info,
        shards(parts[0]),
        [piece(i, k) for i in range(2) for k in range(2)],
        sems,
        shard_place,
    )
    xs, gs, acted, dgate, dup, gates, lgs, slots = [one.get() for one in ins]
    wait_all(copies)
    router_grad[...] = jnp.zeros_like(router_grad)

    def step(i, carry):
        source = xs[i]
        gate = gates[i][:, 0:1]
        spread[i] = mm(acted[i], wd[i]) * gate
        slot_grad = (gs[i].astype(f32) * gate).astype(bf16)
        router_grad[...] += mm(lgs[i], source, TN)
        sums[0] = mm(source, dgate[i], TN).astype(bf16)
        sums[1] = mm(source, dup[i], TN).astype(bf16)
        down_sums[...] = mm(acted[i], slot_grad, TN).astype(bf16)
        for r in range(8):
            d = part_place(info, r)
            target = (*mine, *other)[r]
            target[i, 0:128, :] = sums[0, aligned(d, TOK), :]
            target[i, 128:256, :] = sums[1, aligned(d, TOK), :]
            target[i, 256:320, :] = down_sums[aligned(d, HD), 0:HALF]
            target[i, 320:384, :] = down_sums[aligned(d, HD), HALF:D]
        return carry

    lax.fori_loop(0, 2, step, 0)
    outs[9].ref[...] = router_grad[0:EXPERTS, :].astype(bf16)
    for one in (*outs[5:9], *outs[1:5]):
        one.start()
    for t in range(PEERS):
        span = slice(t * CAP, (t + 1) * CAP)
        rows = jnp.concatenate([spread[i, span, :] for i in range(2)], axis=0).astype(bf16)
        routed[t * TOK : (t + 1) * TOK, :] = mm(slots[t], rows, TN).astype(bf16)


def hidden_kernel(info, ins, parts, outs, scratch):
    arrived, table, hidden, cot, small = ins
    hidden_grad, low, send = outs
    w_out, sems = scratch
    copies = place_parts(info, parts, w_out_pieces(w_out), sems)
    turned_table = table.get()[...].astype(f32).T.astype(bf16)
    grad = mm(turned_table, arrived.get()[...])
    hidden = hidden.get()[...]
    gain = small.get()[2 * EXTRA : 3 * EXTRA, :].astype(f32)[1:2, :]
    r = lax.rsqrt(jnp.mean(hidden * hidden, axis=-1, keepdims=True) + eps)
    scaled = grad * gain
    dot = jnp.mean(scaled * hidden, axis=-1, keepdims=True)
    total = cot.get()[...].astype(f32) + r * scaled - hidden * (r * r * r * dot)
    gain_grad = jnp.sum(grad * hidden * r, axis=0, keepdims=True)
    gain_grad = jnp.concatenate([gain_grad, jnp.zeros((EXTRA - 1, D), f32)], axis=0)
    low.ref[TOK : TOK + EXTRA, :] = gain_grad.astype(bf16)
    hidden_grad.ref[...] = total
    low.ref[0:TOK, :] = total.astype(bf16)
    hidden_grad.start()
    low.start()
    wait_all(copies)
    turned = mm(w_out[...], low.ref[0:TOK, :], NT).astype(bf16)
    for e in range(PEERS):
        send.ref[e] = turned[HEAD_OF[e] * HD : (HEAD_OF[e] + 1) * HD, :]


def out_weights_kernel(info, ins, parts, outs, scratch):
    mixed_a, mixed_b, router_a, router_b, low_a, low_b = [one.get() for one in ins]
    extra = scratch[0]
    router = router_a[...].astype(f32) + router_b[...].astype(f32)
    gains = slice(TOK, TOK + EXTRA)
    gain = low_a[gains, :].astype(f32) + low_b[gains, :].astype(f32)
    rest = jnp.zeros((128 - EXPERTS - EXTRA, D), f32)
    extra[...] = jnp.concatenate([router, gain, rest], axis=0).T
    low = jnp.concatenate([low_a[0:TOK, :], low_b[0:TOK, :]], axis=0)
    for m in range(SIDE):
        rows = aligned(part_place(info, m), TOK)
        mixed = jnp.concatenate([mixed_a[rows, :], mixed_b[rows, :]], axis=1)
        outs[m].ref[:, 0:D] = mm(mixed, low).astype(bf16)
        outs[m].ref[:, D:PACK] = extra[rows, :].astype(bf16)
        outs[m].start()


def attend_back_kernel(info, ins, parts, outs, scratch):
    heads, out_t, lse, arrived, cos, sin, start = [one.get() for one in ins[0:7]]
    send = outs[0].ref
    qz, kvt, kvn, oz, qon, dq, low, delta, sums = scratch
    steps = SEQ // QB
    spread_heads(heads, qz, kvt, kvn)
    for i in range(steps):
        span = slice(i * QB, (i + 1) * QB)
        got = jnp.concatenate([arrived[i * 4 + j] for j in range(4)], axis=1)
        oz[0:HD, span] = jnp.zeros((HD, QB), bf16)
        oz[HD:128, span] = got
        wide = got.astype(f32)
        delta[:, span] = jnp.sum(wide * out_t[:, span], axis=0, keepdims=True)
        qon[span, :] = jnp.concatenate([qz[0:HD, span].astype(f32), wide], axis=0).T.astype(bf16)
        dq[:, span] = jnp.zeros((HD, QB), f32)
    for ki in range(steps):
        keys = slice(ki * QB, (ki + 1) * QB)
        value_sum = jnp.zeros((QB, 128), f32)
        key_sum = jnp.zeros((QB, 128), f32)
        for qi in range(ki, steps):
            span = slice(qi * QB, (qi + 1) * QB)
            scores = mm(kvn[keys, :], qz[:, span])
            expo = jnp.where(
                allowed(ki, qi, start[:, span]), jnp.exp(scores - lse[:, span]), 0.0
            )
            back = mm(kvn[keys, :], oz[:, span])
            score_grad = (expo * (back - delta[:, span])).astype(bf16)
            value_sum = value_sum + mm(expo.astype(bf16), qon[span, :])
            key_sum = key_sum + mm(score_grad, qon[span, :])
            dq[:, span] += mm(kvt[0:HD, keys], score_grad)
        lane = lax.broadcasted_iota(jnp.int32, (QB, 128), 1)
        turned = jnp.where(lane < HD, key_sum, value_sum).T
        low[HD : 2 * HD, keys] = rotated_back(turned[0:HD], cos[:, keys], sin[:, keys]).astype(bf16)
        low[2 * HD : 3 * HD, keys] = turned[HD:128].astype(bf16)
    for i in range(steps):
        span = slice(i * QB, (i + 1) * QB)
        low[0:HD, span] = rotated_back(
            dq[:, span] * (HD**-0.5), cos[:, span], sin[:, span]
        ).astype(bf16)
    for j in range(PEERS):
        send[j] = low[:, j * TOK : (j + 1) * TOK]
    outs[0].start()
    total = mm(low[...], ins[7].get()[...]).astype(bf16)
    for d in range(DP):
        sums[d] = total[:, d * TOK : (d + 1) * TOK]
    for r in (4, 5, 6, 7, 0, 1, 2, 3):
        outs[1 + r].ref[...] = sums[part_place(info, r)]
        outs[1 + r].start()


def input_kernel(info, ins, parts, outs, scratch):
    arrived, hidden_grad, states, small = ins[0:4]
    grad, query, key, value, out, router, rest_attn, rest_ffn = [one.ref for one in outs]
    wide, sums, sems = scratch
    mine = info[0] % 2
    copies = []
    for half, first, side in ((parts[0:8], 0, mine), (parts[8:16], D, 1 - mine)):
        copies += place_parts(
            info,
            half,
            [
                lambda part, d, a=a, b=b, w=w, first=first, side=side: (
                    part.at[pl.ds(0, TOK), pl.ds(first + a, w)],
                    wide.at[aligned(d, TOK), pl.ds(pl.multiple_of(b + side * w, 256), w)],
                )
                for a, b, w in ((0, 0, 512), (512, 1024, 256), (768, 1536, 256))
            ],
            sems.at[0 if first == 0 else 1],
        )
    arrived = arrived.get()

    def pair_sum(first, count):
        rows = slice(first, first + count)
        pairs = [
            arrived[DEV_OF[g], rows, :].astype(f32) + arrived[DEV_OF[g + 1], rows, :].astype(f32)
            for g in range(0, HEADS, 2)
        ]
        return jnp.concatenate(pairs, axis=0)

    def by_head(first):
        rows = [arrived[DEV_OF[h], first : first + HD, :].astype(f32) for h in range(HEADS)]
        return jnp.concatenate(rows, axis=0)

    dq = by_head(0).T.astype(bf16)
    dk = pair_sum(HD, HD).T.astype(bf16)
    dv = pair_sum(2 * HD, HD).T.astype(bf16)
    query[...] = by_head(192).T
    key[...] = pair_sum(192 + HD, HD).T
    value[...] = pair_sum(192 + 2 * HD, HD).T
    for j in range(PEERS):
        rows = arrived[j, 384:456, :].astype(f32)
        for g in range(9):
            target = out.at[:, g * 128 : (g + 1) * 128] if g < 8 else sums
            target[j * 8 : (j + 1) * 8, :] = rows[g * 8 : (g + 1) * 8, :]
    for one in outs[1:5]:
        one.start()
    turned = sums[...].T
    router[...] = turned[0:EXPERTS, :]
    rest_ffn[...] = turned[EXPERTS : EXPERTS + 1, :]
    weighted = sum(
        jnp.sum(total[...] * own.get()[...].astype(f32), axis=-1, keepdims=True)
        for total, own in zip((query, key, value), ins[4:7])
    )
    weighted = jnp.concatenate([weighted, jnp.zeros((TOK, 127), f32)], axis=1).T
    rest_attn[...] = weighted[0:1, :] / ins[7].get()[...].astype(f32)
    wait_all(copies)
    back = (
        mm(dq, wide[:, 0:1024], NT)
        + mm(dk, wide[:, 1024:1536], NT)
        + mm(dv, wide[:, 1536:2048], NT)
    )
    x = states.get()[...].astype(f32)
    gain = small.get()[2 * EXTRA : 3 * EXTRA, :].astype(f32)[0:1, :]
    r = lax.rsqrt(jnp.mean(x * x, axis=-1, keepdims=True) + eps)
    scaled = back * gain
    dot = jnp.mean(scaled * x, axis=-1, keepdims=True)
    grad[...] = hidden_grad.get()[...] + r * scaled - x * (r * r * r * dot)


def per_device(
    inputs,
    segments,
    routes,
    gain_attn,
    w_query,
    w_key,
    w_value,
    w_out,
    gain_ffn,
    w_router,
    expert_gate,
    expert_up,
    expert_down,
    cotangent,
):
    place = lax.axis_index("expert")
    row = lax.axis_index("dp")
    info = jnp.stack([place // SIDE, place % SIDE, row // 2, row % 2]).astype(jnp.int32)
    states = inputs[0]
    cot = cotangent[0]
    my_routes = routes[0].T

    segment_row = segments[0][None, :]
    index = jnp.arange(SEQ, dtype=jnp.int32)[None, :]
    start = jnp.zeros((1, SEQ), jnp.int32)
    for s in range(3):
        count = jnp.sum((segment_row == s).astype(jnp.int32))
        start = start + jnp.where(segment_row > s, count, 0)
    freqs = theta ** (-jnp.arange(0, HD, 2, dtype=f32) / HD)
    angles = freqs[:, None] * (index - start).astype(f32)
    cosine, sine = jnp.cos(angles), jnp.sin(angles)
    blocks = [(place // 8 * 2 + j) * 4 + place % 4 for j in range(2)]
    my_angles = jnp.concatenate(
        [lax.dynamic_slice_in_dim(angles, block * TOK, TOK, 1) for block in blocks], axis=1
    )
    my_cosine, my_sine = jnp.cos(my_angles), jnp.sin(my_angles)

    packed = run(
        pack_kernel,
        "pack",
        (info,),
        (expert_gate, expert_up, expert_down),
        (shape((768, HALF), bf16),),
        (pltpu.SemaphoreType.DMA((8,)),),
    )[0]
    names = jnp.concatenate(
        [
            my_routes.astype(f32),
            jnp.zeros((EXTRA - 8, TOK), f32),
            gain_attn.astype(f32)[None, :],
            gain_ffn.astype(f32)[None, :],
            jnp.zeros((EXTRA - 2, TOK), f32),
        ],
        axis=0,
    )
    dense, outward, cots = run(
        dense_kernel,
        "dense",
        (info, w_router.T, Near(names)),
        (w_query, w_key, w_value, w_out, cot, states),
        (
            shape((TOK + EXTRA, D), bf16),
            shape((TOK, 2 * D), bf16),
            shape((ROW_STEP, D), bf16),
        ),
        (pltpu.SemaphoreType.DMA((9,)),),
    )
    cots = lax.all_gather(cots, "expert", axis=0, tiled=True)
    partner = lax.ppermute(states, "expert", [(e, e ^ 4) for e in range(PEERS)])
    dense = gather_dp(dense, packed, cosine, sine, my_cosine, my_sine, partner)

    small, heads = run(
        qkv_kernel,
        "qkv",
        (info, states, partner, Near(my_cosine), Near(my_sine)),
        dense,
        (
            shape((3 * EXTRA, D), bf16),
            shape((8, 2, 3 * HD, TOK), bf16),
        ),
        (
            pltpu.VMEM((D, D), bf16),
            pltpu.VMEM((2, TOK, D), f32),
            pltpu.SemaphoreType.DMA((32,)),
        ),
        cost=5,
    )
    heads = swap_side(heads)

    packed = lax.all_gather(tied(packed, small), "dp", axis=0)
    outward = gather_y(tied(outward, small))

    out_t, lse, mixed_send = run(
        attend_kernel,
        "attend",
        (info, Near(heads), Near(start)),
        (),
        (
            shape((HD, SEQ), f32),
            shape((1, SEQ), f32),
            shape((HEADS, HD, TOK), bf16),
        ),
        (
            pltpu.VMEM((128, SEQ), bf16),
            pltpu.VMEM((128, SEQ), bf16),
            pltpu.VMEM((SEQ, 128), bf16),
        ),
        cost=6,
    )
    outward = list(lax.optimization_barrier((*outward, mixed_send))[0:SIDE])
    outward += [core_swap(part) for part in outward]
    mixed_t = swap_all(mixed_send).reshape(HEADS * HD, TOK)

    hidden, send, table, ordered = run(
        project_kernel,
        "project",
        (info, Near(mixed_t), states, small, my_routes),
        outward,
        (
            shape((TOK, D), f32),
            shape((2 * ROWS, D), bf16),
            shape((2 * ROWS, TOK), bf16),
            shape((HEADS * HD, TOK), bf16),
        ),
        (pltpu.VMEM((D, D), bf16), pltpu.SemaphoreType.DMA((8,))),
        cost=5,
    )
    arrived = swap_all(send)

    grad_rows, slots = run(
        rows_kernel,
        "grad_rows",
        (info,),
        (cots,),
        (Near(shape((2, ROWS, D), bf16)), shape((PEERS, 2 * CAP, TOK), bf16)),
        (
            pltpu.VMEM((PEERS, TOK + EXTRA, D), bf16),
            pltpu.VMEM((2 * PEERS, TOK), f32),
            pltpu.SemaphoreType.DMA((PEERS,)),
        ),
        limit=32,
    )
    normed = run(
        norm_kernel,
        "normed",
        (info, small),
        (cots,),
        (shape((SEQ, D), bf16),),
        (pltpu.VMEM((PEERS, TOK, D), bf16), pltpu.SemaphoreType.DMA((PEERS,))),
        after=(table,),
    )[0]

    sent_grad, xs, acted, dgate, dup, gates, lgs = run(
        expert_kernel,
        "experts",
        (info, arrived, Near(grad_rows), small),
        (packed,),
        (
            shape((2 * ROWS, D), bf16),
            shape((2, ROWS, D), bf16),
            shape((2, ROWS, EF), bf16),
            shape((2, ROWS, EF), bf16),
            shape((2, ROWS, EF), bf16),
            shape((2, ROWS, 128), f32),
            shape((2, ROWS, 128), bf16),
        ),
        (
            pltpu.VMEM((2, ROWS, D), f32),
            pltpu.VMEM((2, D, EF), bf16),
            pltpu.VMEM((2, D, EF), bf16),
            pltpu.VMEM((2, EF, D), bf16),
            pltpu.SemaphoreType.DMA((64,)),
        ),
        limit=28,
        after=(normed,),
        cost=12,
    )
    back = swap_all(sent_grad)

    routed, *expert_grads, router_grad = run(
        weights_kernel,
        "weights",
        (info, xs, Near(grad_rows), acted, dgate, dup, gates, lgs, slots),
        (packed,),
        (
            shape((SEQ, D), bf16),
            *(shape((2, 384, 512), bf16),) * 8,
            shape((EXPERTS, D), bf16),
        ),
        (
            pltpu.VMEM((2, ROWS, D), f32),
            pltpu.VMEM((2, EF, D), bf16),
            pltpu.VMEM((2, D, EF), bf16),
            pltpu.VMEM((EF, D), bf16),
            pltpu.VMEM((128, D), f32),
            pltpu.SemaphoreType.DMA((32,)),
        ),
        limit=40,
    )
    expert_pairs = pair_up(info, expert_grads[0:4], expert_grads[4:8], "expert_pairs")
    expert_near = [dp_from(expert_pairs[m], SIDE - m) for m in (1, 3)]

    hidden_grad, low, grad_send = run(
        hidden_kernel,
        "hidden_grad",
        (info, back, table, hidden, cot, small),
        outward,
        (
            shape((TOK, D), f32),
            shape((TOK + EXTRA, D), bf16),
            shape((HEADS, HD, TOK), bf16),
        ),
        (pltpu.VMEM((D, D), bf16), pltpu.SemaphoreType.DMA((8,))),
        after=(router_grad, *expert_pairs),
        cost=4,
    )
    mixed_grad = swap_all(grad_send)

    out_pairs = run(
        out_weights_kernel,
        "out_weights",
        (
            info,
            ordered,
            core_swap(ordered),
            router_grad,
            core_swap(router_grad),
            low,
            core_swap(low),
        ),
        (),
        (shape((TOK, PACK), bf16),) * SIDE,
        (pltpu.VMEM((D, 128), f32),),
    )

    routed = lax.psum_scatter(tied(routed, expert_pairs[0]), "expert", scatter_dimension=0, tiled=True)
    output = (hidden + routed.astype(f32)).astype(bf16)

    grads_send, *w_grads = run(
        attend_back_kernel,
        "attend_back",
        (info, heads, out_t, lse, Near(mixed_grad), cosine, sine, start, normed),
        (),
        (
            shape((PEERS, 192, TOK), bf16),
            *(shape((192, TOK), bf16),) * 8,
        ),
        (
            pltpu.VMEM((128, SEQ), bf16),
            pltpu.VMEM((128, SEQ), bf16),
            pltpu.VMEM((SEQ, 128), bf16),
            pltpu.VMEM((128, SEQ), bf16),
            pltpu.VMEM((SEQ, 128), bf16),
            pltpu.VMEM((HD, SEQ), f32),
            pltpu.VMEM((192, SEQ), bf16),
            pltpu.VMEM((1, SEQ), f32),
            pltpu.VMEM((DP, 192, TOK), bf16),
        ),
        limit=32,
        after=(*out_pairs, *expert_near),
        cost=12,
    )
    out_far = send_pairs(out_pairs)
    *w_grads, _, _, _ = lax.optimization_barrier((*w_grads, *out_far))
    w_pairs = [
        (mine.astype(f32) + core_swap(other).astype(f32)).astype(bf16)
        for mine, other in zip(w_grads[0:4], w_grads[4:8])
    ]
    w_sums = add_parts(w_pairs[0], send_pairs(w_pairs)).astype(bf16)
    expert_far = dp_from(tied(expert_pairs[2], w_sums), 2)
    expert_sums = add_parts(expert_pairs[0], (*expert_near, expert_far))
    out_sums = add_parts(out_pairs[0], out_far).astype(bf16)
    out_sums = swap_all(out_sums).reshape(PEERS, 8, PACK)
    out_sums = jnp.sum(out_sums.astype(f32), axis=0).astype(bf16)
    out_sums = jnp.concatenate([out_sums[:, g * 128 : (g + 1) * 128] for g in range(9)], axis=0)

    ends = jnp.concatenate([w_sums, out_sums], axis=0)
    last = jnp.concatenate(
        [grads_send, jnp.broadcast_to(ends[None], (PEERS, 264, TOK))], axis=1
    )
    last = swap_all(last)

    grad_input, sum_query, sum_key, sum_value, sum_out, sum_router, sum_attn, sum_ffn = run(
        input_kernel,
        "grad_input",
        (info, Near(last), hidden_grad, states, small, w_query, w_key, w_value, gain_attn[None, :]),
        (*dense, *outward),
        (
            shape((TOK, D), f32),
            shape((TOK, 1024), f32),
            shape((TOK, 512), f32),
            shape((TOK, 512), f32),
            shape((TOK, D), f32),
            Near(shape((EXPERTS, TOK), f32)),
            Near(shape((1, TOK), f32)),
            Near(shape((1, TOK), f32)),
        ),
        (
            pltpu.VMEM((D, 2048), bf16),
            pltpu.VMEM((TOK, 128), f32),
            pltpu.SemaphoreType.DMA((2, 24)),
        ),
        limit=32,
        after=(output,),
        cost=7,
    )
    return (
        output[None],
        grad_input[None],
        sum_attn.reshape(TOK),
        sum_query,
        sum_key,
        sum_value,
        sum_out,
        sum_ffn.reshape(TOK),
        sum_router.T,
        expert_sums[:, 0:128],
        expert_sums[:, 128:256],
        jnp.concatenate([expert_sums[:, 256:320], expert_sums[:, 320:384]], axis=2),
    )


def solution(mesh):
    placed = (
        P("dp", "expert", None),
        P("dp", None),
        P("dp", "expert", None),
        P("dp"),
        P("dp", None),
        P("dp", None),
        P("dp", None),
        P("dp", None),
        P("dp"),
        P("dp", None),
        P("expert", "dp", None),
        P("expert", "dp", None),
        P("expert", "dp", None),
        P("dp", "expert", None),
    )
    return jax.shard_map(
        per_device,
        mesh=mesh,
        in_specs=placed,
        out_specs=(
            P("dp", "expert", None),
            P("dp", "expert", None),
            P("dp"),
            P("dp", None),
            P("dp", None),
            P("dp", None),
            P("dp", None),
            P("dp"),
            P("dp", None),
            P("expert", "dp", None),
            P("expert", "dp", None),
            P("expert", "dp", None),
        ),
        check_vma=False,
    )
```
